32 devices in a mesh: dp: 8 (over z, core), fsdp: 4 (over y, x).
Axes of the slice: x: 2, y: 2, z: 4, core: 2. Of those that a mesh axis runs over, the one named last changes fastest.
Arguments:
- layer_input: bfloat16 [32768, 1024], P(('dp', 'fsdp')), may hold values from -6 to 6
- segment_ids: int32 [32768], P(('dp', 'fsdp')), may hold values from 0 to 4, as said below
- relative_buckets: int32 [2047], replicated, may hold values from 0 to 31, as said below
- first_gain: bfloat16 [1024], P(('dp', 'fsdp')), may hold values from 0.5 to 1.5
- query_weight: bfloat16 [1024, 1024], P(('dp', 'fsdp')), may hold values from -0.0625 to 0.0625
- key_weight: bfloat16 [1024, 1024], P(('dp', 'fsdp')), may hold values from -0.0625 to 0.0625
- value_weight: bfloat16 [1024, 1024], P(('dp', 'fsdp')), may hold values from -0.1875 to 0.1875
- output_projection: bfloat16 [1024, 1024], P(('dp', 'fsdp')), may hold values from -0.75 to 0.75
- relative_table: bfloat16 [32, 16], replicated, may hold values from -5 to 5
- second_gain: bfloat16 [1024], P(('dp', 'fsdp')), may hold values from 0.5 to 1.5
- gate_weight: bfloat16 [1024, 2816], P(('dp', 'fsdp')), may hold values from -0.1875 to 0.1875
- up_weight: bfloat16 [1024, 2816], P(('dp', 'fsdp')), may hold values from -0.1875 to 0.1875
- down_projection: bfloat16 [1024, 2816], P(('dp', 'fsdp')), may hold values from -0.15625 to 0.15625
- output_cotangent: bfloat16 [32768, 1024], P(('dp', 'fsdp')), may hold values from -6 to 6
Outputs:
- block_output: bfloat16 [32768, 1024], P(('dp', 'fsdp'))
- input_gradient: float32 [32768, 1024], P(('dp', 'fsdp'))
- query_gradient: float32 [1024, 1024], P(('dp', 'fsdp'))
- key_gradient: float32 [1024, 1024], P(('dp', 'fsdp'))
- value_gradient: float32 [1024, 1024], P(('dp', 'fsdp'))
- output_gradient: float32 [1024, 1024], P(('dp', 'fsdp'))
- gate_gradient: float32 [1024, 2816], P(('dp', 'fsdp'))
- up_gradient: float32 [1024, 2816], P(('dp', 'fsdp'))
- down_gradient: float32 [1024, 2816], P(('dp', 'fsdp'))
- first_gain_gradient: float32 [1024], P(('dp', 'fsdp'))
- second_gain_gradient: float32 [1024], P(('dp', 'fsdp'))
- table_gradient: float32 [32, 16], replicated
The draws below stay inside these ranges and needn't reach their ends.
Inputs may be any that keep to these rules, and one draw needn't show every extreme that they name: `segment_ids`: each packed row of 1024 tokens holds 4 image-text pairs numbered 1 to 4 in order, each a run of consecutive positions, then padding with id 0 to the row's end; a row holds 512 to 1024 live tokens, and some row has no padding. `relative_buckets`: entry 1023 + r is the bucket of the offset r = key position minus query position; it is 0 at r = 0, never falls as the size of r grows on either side, lies in 1 to 15 for r < 0 and in 16 to 31 for r > 0, and the largest offsets of both sides take the largest buckets of their side.
All inputs are finite; a program needn't handle non-finite values.
Results may differ from the reference program's by a relative error of at most 0.015.
Values may be sent and summed in bfloat16 or wider, within the bound.
No kernel may reach another device: no remote copies, remote signals or barrier semaphores. Data moves between devices by JAX's collectives and lax.ppermute only.
A program may use at most 192 MiB of HBM per device.

```python
import jax
import jax.numpy as jnp
from jax import lax

D = 1024
HEADS = 16
HEAD_DIM = 64
FF = 2816
BUCKETS = 32
SEQ = 1024
PAIRS = 4
INNER = 1024
TOKENS = 32768


def draw_segment_ids(key, part):
    key = jax.random.fold_in(key, 7)
    key_length, key_full, key_cut = jax.random.split(key, 3)
    row_count = TOKENS // SEQ
    live_length = jax.random.randint(key_length, (row_count, 1), SEQ // 2, SEQ + 1)
    full_row = jax.random.randint(key_full, (), 0, row_count)
    live_length = jnp.where(jnp.arange(row_count)[:, None] == full_row, SEQ, live_length)
    cut_spread = live_length // (4 * PAIRS)
    jitter = jax.random.randint(key_cut, (row_count, PAIRS - 1), 0, 1 << 20) % (2 * cut_spread + 1) - cut_spread
    cut_points = jnp.arange(1, PAIRS)[None, :] * live_length // PAIRS + jitter
    positions = jnp.arange(SEQ)
    segment_id = 1 + jnp.sum((positions[None, :, None] >= cut_points[:, None, :]).astype(jnp.int32), axis=-1)
    segment_id = jnp.where(positions[None, :] < live_length, segment_id, 0)
    return segment_id.reshape(TOKENS).astype(jnp.int32)


def bucket_side(key):
    offset = jnp.arange(1, SEQ)
    draws = jax.random.randint(key, (SEQ - 1,), 0, 1 << 20) % (offset + 1)
    step = jnp.where(offset < 8, 1, (draws < 2).astype(jnp.int32))
    level = jnp.minimum(BUCKETS // 2 - 1, jnp.cumsum(step))
    return level.at[SEQ - 2].set(BUCKETS // 2 - 1).astype(jnp.int32)


def draw_relative_buckets(key, part):
    key = jax.random.fold_in(key, 11)
    key_ahead, key_behind = jax.random.split(key)
    ahead = bucket_side(key_ahead) + BUCKETS // 2
    behind = bucket_side(key_behind)
    return jnp.concatenate([behind[::-1], jnp.zeros((1,), jnp.int32), ahead]).astype(jnp.int32)


def block_scale(key, shape, pieces, least, largest):
    def one(axis_at, parts):
        heights = jax.random.uniform(jax.random.fold_in(jax.random.fold_in(key, 6), axis_at), (parts,), jnp.float32, least / len(pieces), largest / len(pieces))
        return jnp.repeat(jnp.exp(heights), shape[axis_at] // parts).reshape((-1,) + (1,) * (len(shape) - axis_at - 1))

    level = one(*pieces[0])
    for cut in pieces[1:]:
        level = level * one(*cut)
    return level


def centred(stream_key, dims, scale, limit, cuts=(), dtype=jnp.bfloat16):
    level = block_scale(stream_key, dims, cuts, -0.22, 0.18) if cuts else 1.0
    array = jax.random.normal(stream_key, dims, jnp.float32) * scale * level
    return jnp.minimum(jnp.maximum(array, -limit), limit).astype(dtype)


def setup_inputs(seed: int = 0) -> dict:
    streams_of = jax.random.split(jax.random.key(seed), 15)
    layer_input = centred(streams_of[0], (TOKENS, D), 1.0, 6.0, ((0, 32),))
    segment_ids = draw_segment_ids(jax.random.fold_in(streams_of[14], 71), 0)
    relative_buckets = draw_relative_buckets(jax.random.fold_in(streams_of[14], 71), 0)
    first_gain = jnp.clip(1.0 + 0.1 * jax.random.normal(streams_of[3], (D,), jnp.float32), 0.5, 1.5).astype(jnp.bfloat16)
    query_weight = centred(streams_of[4], (D, INNER), (8 * D) ** -0.5, 0.0625, ((0, 32),))
    key_weight = centred(streams_of[5], (D, INNER), (8 * D) ** -0.5, 0.0625, ((0, 32),))
    value_weight = centred(streams_of[6], (D, INNER), D ** -0.5, 0.1875, ((0, 32),))
    output_projection = centred(streams_of[7], (D, INNER), (INNER // 16) ** -0.5, 0.75, ((0, 32),))
    relative_table = centred(streams_of[8], (BUCKETS, HEADS), 1.0, 5.0)
    second_gain = jnp.clip(1.0 + 0.1 * jax.random.normal(streams_of[9], (D,), jnp.float32), 0.5, 1.5).astype(jnp.bfloat16)
    gate_weight = centred(streams_of[10], (D, FF), D ** -0.5, 0.1875, ((0, 32),))
    up_weight = centred(streams_of[11], (D, FF), D ** -0.5, 0.1875, ((0, 32),))
    down_projection = centred(streams_of[12], (D, FF), (FF // 2) ** -0.5, 0.15625, ((0, 32),))
    output_cotangent = centred(streams_of[13], (TOKENS, D), 1.0, 6.0, ((0, 32),))
    return {"layer_input": layer_input, "segment_ids": segment_ids, "relative_buckets": relative_buckets, "first_gain": first_gain, "query_weight": query_weight, "key_weight": key_weight, "value_weight": value_weight, "output_projection": output_projection, "relative_table": relative_table, "second_gain": second_gain, "gate_weight": gate_weight, "up_weight": up_weight, "down_projection": down_projection, "output_cotangent": output_cotangent}


@jax.custom_vjp
def low(v):
    return lax.optimization_barrier(v.astype(jnp.bfloat16)).astype(jnp.float32)

@jax.custom_vjp
def low_back(v):
    return v

def low_keep(v):
    return (low(v), None)

def low_pass(kept, grad):
    return (grad,)

def back_keep(v):
    return (v, None)

def back_low(kept, grad):
    return (low(grad),)
low.defvjp(low_keep, low_pass)
low_back.defvjp(back_keep, back_low)
EPS = 1e-06
NEGATIVE = -1e+30
HIGHEST_ACCURACY = lax.Precision.HIGHEST

def norm_rows(values, gain):
    return values * lax.rsqrt(lax.optimization_barrier(jnp.mean(values * values, axis=-1, keepdims=True)) + EPS) * gain

def project(input_rows, weight_matrix):
    return jnp.einsum('zhj,jg->zhg', input_rows, weight_matrix, precision=HIGHEST_ACCURACY)

def attend(query, keys, values, offsets, segments):
    seq_count, length, width = query.shape
    half_count = HEADS // 2
    index = (jnp.arange(length)[None, :] - jnp.arange(length)[:, None] + length - 1).astype(jnp.int32)
    allowed = (segments[:, :, None] == segments[:, None, :]) & (segments[:, None, :] > 0)

    def split(matrix):
        return jnp.moveaxis(matrix.reshape(seq_count, length, half_count, 2, HEAD_DIM), 2, 0)
    offset_pairs = jnp.moveaxis(offsets.reshape(2 * length - 1, half_count, 2), 1, 0)

    def pair(items):
        query_pair, key_pair, value_pair, offset_pair = items
        bias = jnp.moveaxis(jnp.take(offset_pair, index, axis=0), 2, 0)
        scores = jnp.einsum('sqhd,skhd->shqk', query_pair, key_pair, precision=HIGHEST_ACCURACY) + bias[None]
        scores = jnp.where(allowed[:, None], low_back(scores), NEGATIVE)
        peak = lax.optimization_barrier(jnp.max(scores, axis=-1, keepdims=True))
        raised = jnp.exp(scores - peak)
        prob = raised / lax.optimization_barrier(jnp.sum(raised, axis=-1, keepdims=True))
        return jnp.einsum('shqk,skhd->sqhd', low(prob), value_pair, precision=HIGHEST_ACCURACY)
    mixed_heads = lax.map(jax.checkpoint(pair), (split(query), split(keys), split(values), offset_pairs))
    return jnp.moveaxis(mixed_heads, 0, 2).reshape(seq_count, length, width)

def layer(layer_input, first_gain, query_weight, key_weight, value_weight, output_projection, relative_table, second_gain, gate_weight, up_weight, down_projection, segments, relative_buckets):
    normed = low(norm_rows(layer_input, first_gain))
    query = low_back(low(project(normed, query_weight)))
    keys = low_back(low(project(normed, key_weight)))
    values = low_back(low(project(normed, value_weight)))
    offsets = relative_table[relative_buckets]
    attended_values = low_back(low(attend(query, keys, values, offsets, segments)))
    hidden_units = layer_input + low_back(jnp.einsum('fjr,tr->fjt', attended_values, output_projection, precision=HIGHEST_ACCURACY))
    normed_two = low(norm_rows(hidden_units, second_gain))
    gate = low_back(project(normed_two, gate_weight))
    upward = low_back(project(normed_two, up_weight))
    mixed_heads = low(jax.nn.gelu(gate, approximate=True) * upward)
    residual_branch = low_back(jnp.einsum('mrt,yt->mry', mixed_heads, down_projection, precision=HIGHEST_ACCURACY))
    live = (segments > 0).astype(jnp.float32)[:, :, None]
    return (hidden_units + residual_branch) * live

def reference(layer_input, segment_ids, relative_buckets, first_gain, query_weight, key_weight, value_weight, output_projection, relative_table, second_gain, gate_weight, up_weight, down_projection, output_cotangent):
    row_count = layer_input.shape[0] // SEQ
    group = max((count_each for count_each in range(1, row_count + 1) if row_count % count_each == 0 and count_each * SEQ <= max(4096, SEQ)))
    turns = row_count // group
    params = tuple((item.astype(jnp.float32) for item in (first_gain, query_weight, key_weight, value_weight, output_projection, relative_table, second_gain, gate_weight, up_weight, down_projection)))
    input_rows = layer_input.astype(jnp.float32).reshape(turns, group, SEQ, D)
    segments = segment_ids.reshape(turns, group, SEQ)
    cotangents = output_cotangent.astype(jnp.float32).reshape(turns, group, SEQ, D)

    def one_group(totals, items):
        inputs_now, segments_now, cotangent_now = items

        def forward(values, *weights):
            return layer(values, *weights, segments_now, relative_buckets)
        result, pull = jax.vjp(forward, inputs_now, *params)
        grads = pull(cotangent_now)
        summed = tuple((total + grad for total, grad in zip(totals, grads[1:])))
        return (summed, (result.astype(jnp.bfloat16), grads[0]))
    starts = tuple((jnp.zeros_like(item) for item in params))
    totals, (outputs, input_grads) = lax.scan(one_group, starts, (input_rows, segments, cotangents))
    return (outputs.reshape(-1, D), input_grads.reshape(-1, D), totals[1], totals[2], totals[3], totals[4], totals[7], totals[8], totals[9], totals[0], totals[6], totals[5])
```

```python
import functools

import jax
import jax.numpy as jnp
import numpy as np
from jax import lax
from jax.experimental import pallas as pl
from jax.experimental.pallas import tpu as pltpu
from jax.sharding import PartitionSpec as P

F32 = jnp.float32
BF = jnp.bfloat16
HEADS = 16
BUCKETS = 32
SEQ = 1024
D = 1024
FF = 2816
BLK = 128
NB = SEQ // BLK
STRIP = (2 * NB - 1) * BLK
UNIT = 4
EPS = 1e-06
NEG = -1e30
VLIM = 60 * 1024 * 1024
AXES = ("dp", "fsdp")
GROUP = 512
PIECES = (768, 1024, 1024)
TILE = 256
FT = 256
ANY = pl.BlockSpec(memory_space=pl.ANY)
SMEM = pl.BlockSpec(memory_space=pltpu.SMEM)
HIGHEST = lax.Precision.HIGHEST
GELU_A = 0.7978845608028654
GELU_B = 0.044715


def params(grid=1):
    return pltpu.CompilerParams(vmem_limit_bytes=VLIM, dimension_semantics=("arbitrary",) * grid)


def cost(flops, moved, trans=0):
    return pl.CostEstimate(flops=int(flops), bytes_accessed=int(moved), transcendentals=int(trans))


def nt(a,b): return lax.dot_general(a,b,(((1,),(1,)),((),())),preferred_element_type=F32)
def nn(a,b): return lax.dot_general(a,b,(((1,),(0,)),((),())),preferred_element_type=F32)

def build_strip(rev_ref, strip):
    for h in range(2):
        row=jnp.broadcast_to(rev_ref[h:h+1,:],(8,2*SEQ))
        base=pltpu.roll(row,0,1,stride=1,stride_axis=0)
        for m in range(BLK//8):
            turned=pltpu.roll(base,(8*m-(BLK-1))%(2*SEQ),1)
            for d in range(2*NB-1):
                e=2*NB-2-d
                strip[d*BLK+8*m:d*BLK+8*m+8,h*BLK:(h+1)*BLK]=turned[:,e*BLK:(e+1)*BLK]

def fold_strip(strip, out_ref):
    for h in range(2):
        total=jnp.zeros((8,2*SEQ),F32)
        for m in range(BLK//8):
            parts=[strip[(2*NB-2-e)*BLK+8*m:(2*NB-2-e)*BLK+8*m+8,h*BLK:(h+1)*BLK] for e in range(2*NB-1)]
            parts.append(jnp.zeros((8,BLK),F32))
            total=total+pltpu.roll(jnp.concatenate(parts,axis=1),(BLK-1-8*m)%(2*SEQ),1)
        row=total[0:1]
        for s in range(1,8):
            row=row+pltpu.roll(total[s:s+1],2*SEQ-s,1)
        out_ref[h:h+1,:]=row

def lanes_mask():
    lane=lax.broadcasted_iota(jnp.int32,(1,BLK),1)
    return lane<64

def stack_heads(x, first):
    zero=jnp.zeros_like(x)
    return jnp.concatenate([jnp.where(first,x,zero),jnp.where(first,zero,x)],axis=0)


def strip_kernel(rev_ref, strip):
    build_strip(rev_ref, strip)

def make_strips(rev):
    return pl.pallas_call(strip_kernel,grid=(8,),
        in_specs=[pl.BlockSpec((None,2,2*SEQ),lambda p:(p,0,0))],
        out_specs=pl.BlockSpec((None,STRIP,2*BLK),lambda p:(p,0,0)),
        out_shape=jax.ShapeDtypeStruct((8,STRIP,2*BLK),F32),
        compiler_params=pltpu.CompilerParams(vmem_limit_bytes=VLIM),
        name="bias_strips")(rev)

def attn_fwd_kernel(rng_ref, segk_ref, segq_ref, strip, q_ref, k_ref, v_ref, o_ref, lse_ref, vt):
    first=lanes_mask()
    for u in range(UNIT):
        vt[u]=v_ref[:,u*BLK:(u+1)*BLK].T
    mean=jnp.sum(v_ref[...].astype(F32),axis=0,keepdims=True)*(1.0/SEQ)

    def block(qi, carry):
        q0=pl.multiple_of(qi*BLK,BLK)
        lo=rng_ref[qi]; width=rng_ref[NB+qi]
        k0=pl.multiple_of(lo*BLK,BLK)
        b0=pl.multiple_of((lo-qi+NB-1)*BLK,BLK)
        segq=segq_ref[pl.ds(qi,1),:]
        @pl.when(width==0)
        def _():
            o_ref[pl.ds(q0,BLK),:]=jnp.broadcast_to(mean,(BLK,UNIT*BLK)).astype(BF)
            for u in range(UNIT):
                lse_ref[u,pl.ds(qi,1),:]=jnp.zeros((1,2*BLK),F32)
        for w in range(1,NB+1):
            @pl.when(width==w)
            def _():
                rows=w*BLK
                allowed=segk_ref[pl.ds(k0,rows),:]==segq
                live_row=segq>0
                live_row=jnp.concatenate([live_row,live_row],axis=1)
                live_col=segk_ref[pl.ds(q0,BLK),:]>0
                units=[slice(u*BLK,(u+1)*BLK) for u in range(UNIT)]
                qcats=[stack_heads(q_ref[pl.ds(q0,BLK),lanes],first) for lanes in units]
                scores=[nt(k_ref[pl.ds(k0,rows),lanes],qcat) for lanes,qcat in zip(units,qcats)]
                probs=[]; stats=[]; totals=[]
                for u in range(UNIT):
                    both=[]; stat=[]; tot=[]
                    s=scores[u]+strip[u,pl.ds(b0,rows),:]
                    for h in range(2):
                        sh=jnp.where(allowed,s[:,h*BLK:(h+1)*BLK],NEG)
                        peak=jnp.max(sh,axis=0,keepdims=True)
                        e=jnp.exp(sh-peak)
                        t=jnp.sum(e,axis=0,keepdims=True)
                        both.append(e.astype(BF)); stat.append(peak+jnp.log(t)); tot.append(t)
                    probs.append(jnp.concatenate(both,axis=1)); stats.append(jnp.concatenate(stat,axis=1)); totals.append(jnp.concatenate(tot,axis=1))
                ots=[nn(vt[u,:,pl.ds(k0,rows)],probs[u]) for u in range(UNIT)]
                for u,lanes in enumerate(units):
                    ot=ots[u]*(1.0/totals[u])
                    o=jnp.concatenate([ot[:64,:BLK],ot[64:,BLK:]],axis=0).T
                    o_ref[pl.ds(q0,BLK),lanes]=jnp.where(live_col,o,mean[:,lanes]).astype(BF)
                    lse_ref[u,pl.ds(qi,1),:]=jnp.where(live_row,stats[u],0.0)
        return carry
    lax.fori_loop(0,NB,block,0)

def attn_bwd_kernel(rng_ref, segk_ref, segq_ref, strip, q_ref, k_ref, v_ref, g_ref, lse_ref,
                    dq_ref, dk_ref, dv_ref, off_ref, dstrip, kt, dk, dv):
    first=lanes_mask()
    dstrip[...]=jnp.zeros_like(dstrip)
    dk[...]=jnp.zeros_like(dk)
    for u in range(UNIT):
        lanes=slice(u*BLK,(u+1)*BLK)
        kt[u]=k_ref[:,lanes].T
        padded=jnp.where(segk_ref[...]>0,0.0,g_ref[:,lanes].astype(F32))
        dv[:,lanes]=jnp.broadcast_to(jnp.sum(padded,axis=0,keepdims=True)*(1.0/SEQ),(SEQ,BLK))

    def block(qi, carry):
        q0=pl.multiple_of(qi*BLK,BLK)
        lo=rng_ref[qi]; width=rng_ref[NB+qi]
        k0=pl.multiple_of(lo*BLK,BLK)
        b0=pl.multiple_of((lo-qi+NB-1)*BLK,BLK)
        segq=segq_ref[pl.ds(qi,1),:]
        @pl.when(width==0)
        def _():
            dq_ref[pl.ds(q0,BLK),:]=jnp.zeros((BLK,UNIT*BLK),BF)
        for w in range(1,NB+1):
            @pl.when(width==w)
            def _():
                rows=w*BLK
                allowed=segk_ref[pl.ds(k0,rows),:]==segq
                units=[slice(u*BLK,(u+1)*BLK) for u in range(UNIT)]
                qcats=[stack_heads(q_ref[pl.ds(q0,BLK),lanes],first) for lanes in units]
                gcats=[stack_heads(g_ref[pl.ds(q0,BLK),lanes],first) for lanes in units]
                scores=[nt(k_ref[pl.ds(k0,rows),lanes],qcat) for lanes,qcat in zip(units,qcats)]
                dps=[nt(v_ref[pl.ds(k0,rows),lanes],gcat) for lanes,gcat in zip(units,gcats)]
                probs=[]; grads=[]
                for u in range(UNIT):
                    lse=lse_ref[u,pl.ds(qi,1),:]
                    s=scores[u]+strip[u,pl.ds(b0,rows),:]
                    ps=[]; ds=[]
                    for h in range(2):
                        cols=slice(h*BLK,(h+1)*BLK)
                        prob=jnp.exp(jnp.where(allowed,s[:,cols],NEG)-lse[:,cols])
                        t=prob*dps[u][:,cols]
                        inner=jnp.sum(t,axis=0,keepdims=True)
                        d=t-prob*inner
                        dstrip[u,pl.ds(b0,rows),cols]+=d
                        ps.append(prob.astype(BF)); ds.append(d.astype(BF))
                    probs.append(jnp.concatenate(ps,axis=1)); grads.append(jnp.concatenate(ds,axis=1))
                for u,lanes in enumerate(units):
                    dv[pl.ds(k0,rows),lanes]+=nn(probs[u],gcats[u])
                dqts=[nn(kt[u,:,pl.ds(k0,rows)],grads[u]) for u in range(UNIT)]
                for u,lanes in enumerate(units):
                    dk[pl.ds(k0,rows),lanes]+=nn(grads[u],qcats[u])
                for u,lanes in enumerate(units):
                    dq_ref[pl.ds(q0,BLK),lanes]=jnp.concatenate([dqts[u][:64,:BLK],dqts[u][64:,BLK:]],axis=0).T.astype(BF)
        return carry
    lax.fori_loop(0,NB,block,0)
    dk_ref[...]=dk[...].astype(BF)
    dv_ref[...]=dv[...].astype(BF)
    for u in range(UNIT):
        fold_strip(dstrip.at[u], off_ref.at[u])

def attn_fwd(rng,segk,segq,strips,qkv,pairs,first_pair):
    n=pairs//UNIT; f=first_pair//UNIT; wide=UNIT*BLK
    c=lambda o:pl.BlockSpec((SEQ,wide),lambda p,r:(0,o+p))
    gs=pltpu.PrefetchScalarGridSpec(num_scalar_prefetch=1,grid=(n,),
        in_specs=[pl.BlockSpec((SEQ,BLK),lambda p,r:(0,0)),pl.BlockSpec((NB,BLK),lambda p,r:(0,0)),
                  pl.BlockSpec((UNIT,STRIP,2*BLK),lambda p,r:(f+p,0,0)),
                  c(0),c(n),c(2*n)],
        out_specs=[c(0),pl.BlockSpec((UNIT,NB,2*BLK),lambda p,r:(p,0,0))],
        scratch_shapes=[pltpu.VMEM((UNIT,BLK,SEQ),BF)])
    return pl.pallas_call(attn_fwd_kernel,grid_spec=gs,
        out_shape=[jax.ShapeDtypeStruct((SEQ,pairs*BLK),BF),jax.ShapeDtypeStruct((pairs,NB,2*BLK),F32)],
        compiler_params=pltpu.CompilerParams(vmem_limit_bytes=VLIM,dimension_semantics=("arbitrary",)),
        cost_estimate=pl.CostEstimate(flops=pairs*2*2*SEQ*SEQ*64*4,bytes_accessed=pairs*4*SEQ*BLK*2,transcendentals=pairs*SEQ*SEQ),
        name="attention_forward")(rng,segk,segq,strips,qkv,qkv,qkv)

def attn_bwd(rng,segk,segq,strips,qkv,g,lse,pairs,first_pair):
    n=pairs//UNIT; f=first_pair//UNIT; wide=UNIT*BLK
    c=lambda o:pl.BlockSpec((SEQ,wide),lambda p,r:(0,o+p))
    gs=pltpu.PrefetchScalarGridSpec(num_scalar_prefetch=1,grid=(n,),
        in_specs=[pl.BlockSpec((SEQ,BLK),lambda p,r:(0,0)),pl.BlockSpec((NB,BLK),lambda p,r:(0,0)),
                  pl.BlockSpec((UNIT,STRIP,2*BLK),lambda p,r:(f+p,0,0)),
                  c(0),c(n),c(2*n),c(f),
                  pl.BlockSpec((UNIT,NB,2*BLK),lambda p,r:(p,0,0))],
        out_specs=[c(0),c(0),c(0),pl.BlockSpec((UNIT,2,2*SEQ),lambda p,r:(p,0,0))],
        scratch_shapes=[pltpu.VMEM((UNIT,STRIP,2*BLK),F32),pltpu.VMEM((UNIT,BLK,SEQ),BF),
                        pltpu.VMEM((SEQ,wide),F32),pltpu.VMEM((SEQ,wide),F32)])
    sh=jax.ShapeDtypeStruct((SEQ,pairs*BLK),BF)
    return pl.pallas_call(attn_bwd_kernel,grid_spec=gs,
        out_shape=[sh,sh,sh,jax.ShapeDtypeStruct((pairs,2,2*SEQ),F32)],
        compiler_params=pltpu.CompilerParams(vmem_limit_bytes=VLIM,dimension_semantics=("arbitrary",)),
        cost_estimate=pl.CostEstimate(flops=pairs*5*2*SEQ*SEQ*64*4,bytes_accessed=pairs*8*SEQ*BLK*2,transcendentals=pairs*SEQ*SEQ),
        name="attention_backward")(rng,segk,segq,strips,qkv,qkv,qkv,g,lse)

def ranges(seg):
    s=seg.reshape(NB,BLK)
    least=s[:,0]; most=jnp.max(s,axis=1)
    lo=jnp.sum((most[None,:]<least[:,None])&(least[None,:]>0),axis=1)
    hi=jnp.sum((least[None,:]<=most[:,None])&(least[None,:]>0),axis=1)
    w=jnp.where(least>0,hi-lo,0)
    return jnp.concatenate([jnp.where(least>0,lo,0),w]).astype(jnp.int32)


def shift_blocks(load, src_ref, size):
    per = BLK // size
    lane = lax.broadcasted_iota(jnp.int32, (1, BLK), 1) // size
    for q in range(D // BLK):
        chunk = None
        for t in range(per):
            a = src_ref[q * per + t]
            piece = load(pl.multiple_of((a // per) * BLK, BLK))
            piece = pltpu.roll(piece, lax.rem((t - lax.rem(a, per)) * size + BLK, BLK), 1)
            chunk = piece if chunk is None else jnp.where(lane == t, piece, chunk)
        yield q, chunk


def prep_kernel(size, src_ref, x_ref, c_ref, seg_ref, xo_ref, co_ref, ct_ref):
    live = seg_ref[...] > 0
    for q, chunk in shift_blocks(lambda at: x_ref[:, pl.ds(at, BLK)].astype(F32), src_ref, size):
        xo_ref[:, q * BLK : (q + 1) * BLK] = chunk.astype(BF)
    for q, chunk in shift_blocks(lambda at: c_ref[:, pl.ds(at, BLK)].astype(F32), src_ref, size):
        low = jnp.where(live, chunk, 0.0).astype(BF)
        co_ref[:, q * BLK : (q + 1) * BLK] = low
        ct_ref[q * BLK : (q + 1) * BLK, :] = low.T


def prepare(src, x, c, segk, size):
    rows = TILE
    blk = lambda: pl.BlockSpec((rows, D), lambda i: (i, 0))
    sh = jax.ShapeDtypeStruct((SEQ, D), BF)
    return pl.pallas_call(
        functools.partial(prep_kernel, size),
        grid=(SEQ // rows,),
        in_specs=[SMEM, blk(), blk(), pl.BlockSpec((rows, BLK), lambda i: (i, 0))],
        out_specs=[blk(), blk(), pl.BlockSpec((D, rows), lambda i: (0, i))],
        out_shape=[sh, sh, jax.ShapeDtypeStruct((D, SEQ), BF)],
        compiler_params=params(),
        cost_estimate=cost(0, 10 * SEQ * D),
        name="prepare",
    )(src, x, c, segk)


def block_copies(refs, layout, dst, sems):
    copies = []
    for n, (ref, (row, rows, col, cols, start)) in enumerate(zip(refs, layout)):
        copies.append(
            pltpu.make_async_copy(
                ref.at[:, pl.ds(start, cols)], dst.at[pl.ds(row, rows), pl.ds(col, cols)], sems.at[n]
            )
        )
    return copies


def scaled_rows(x):
    return lax.rsqrt(jnp.mean(x * x, axis=-1, keepdims=True) + EPS)


def qkv_kernel(lead, layout, *refs):
    n = len(layout)
    x_ref, blocks, refs = refs[0], refs[1 : 1 + n], refs[1 + n :]
    if lead:
        out_ref, normed_ref, turned_ref, gains_ref, w, sems = refs
    else:
        out_ref, w, sems = refs

    @pl.when(pl.program_id(0) == 0)
    def _():
        copies = block_copies(blocks, layout, w, sems)
        for c in copies:
            c.start()
        for c in copies:
            c.wait()
        if lead:
            gains_ref[...] = w[:, 3 * GROUP :].astype(F32).T[:8]

    if lead:
        x = x_ref[...].astype(F32)
        normed = (x * scaled_rows(x) * gains_ref[0:1, :]).astype(BF)
        normed_ref[...] = normed
        turned_ref[...] = normed.T
    else:
        normed = x_ref[...]
    for j in range(3):
        cols = slice(j * GROUP, (j + 1) * GROUP)
        out_ref[:, cols] = nn(normed, w[:, cols]).astype(BF)


def project(x, blocks, layout, lead):
    width = 3 * GROUP + (BLK if lead else 0)
    rows = TILE
    tok = lambda c: pl.BlockSpec((rows, c), lambda i: (i, 0))
    out_specs = [tok(3 * GROUP)]
    out_shape = [jax.ShapeDtypeStruct((SEQ, 3 * GROUP), BF)]
    if lead:
        out_specs += [tok(D), pl.BlockSpec((D, rows), lambda i: (0, i)), pl.BlockSpec((8, D), lambda i: (0, 0))]
        out_shape += [
            jax.ShapeDtypeStruct((SEQ, D), BF),
            jax.ShapeDtypeStruct((D, SEQ), BF),
            jax.ShapeDtypeStruct((8, D), F32),
        ]
    return pl.pallas_call(
        functools.partial(qkv_kernel, lead, layout),
        grid=(SEQ // rows,),
        in_specs=[tok(D)] + [ANY] * len(blocks),
        out_specs=out_specs,
        out_shape=out_shape,
        scratch_shapes=[pltpu.VMEM((D, width), BF), pltpu.SemaphoreType.DMA((len(blocks),))],
        compiler_params=params(),
        cost_estimate=cost(2 * SEQ * D * 3 * GROUP, 2 * D * width + 4 * SEQ * D),
        name="query_key_value",
    )(x, *blocks)


def hidden_kernel(layout, *refs):
    n = len(layout)
    a0, a1, x_ref, gains_ref = refs[:4]
    blocks = refs[4 : 4 + n]
    h_ref, n2_ref, n2t_ref, w, sems = refs[4 + n :]

    @pl.when(pl.program_id(0) == 0)
    def _():
        copies = block_copies(blocks, layout, w, sems)
        for c in copies:
            c.start()
        for c in copies:
            c.wait()

    hidden = x_ref[...].astype(F32) + (nt(a0[...], w[:, :GROUP]) + nt(a1[...], w[:, GROUP:]))
    h_ref[...] = hidden
    normed = (hidden * scaled_rows(hidden) * gains_ref[1:2, :]).astype(BF)
    n2_ref[...] = normed
    n2t_ref[...] = normed.T


def hidden_units(a0, a1, x, gains, blocks, layout):
    rows = TILE
    tok = lambda c: pl.BlockSpec((rows, c), lambda i: (i, 0))
    return pl.pallas_call(
        functools.partial(hidden_kernel, layout),
        grid=(SEQ // rows,),
        in_specs=[tok(GROUP), tok(GROUP), tok(D), pl.BlockSpec((8, D), lambda i: (0, 0))] + [ANY] * len(blocks),
        out_specs=[tok(D), tok(D), pl.BlockSpec((D, rows), lambda i: (0, i))],
        out_shape=[
            jax.ShapeDtypeStruct((SEQ, D), F32),
            jax.ShapeDtypeStruct((SEQ, D), BF),
            jax.ShapeDtypeStruct((D, SEQ), BF),
        ],
        scratch_shapes=[pltpu.VMEM((D, 2 * GROUP), BF), pltpu.SemaphoreType.DMA((len(blocks),))],
        compiler_params=params(),
        cost_estimate=cost(2 * SEQ * D * D, 16 * SEQ * D),
        name="hidden_units",
    )(a0, a1, x, gains, *blocks)


def feed_kernel(lead, width, start, *refs):
    n2, n2t, cot, cott, wlo, whi = refs[:6]
    refs = refs[6:]
    if not lead:
        bo_in, ng_in = refs[:2]
        refs = refs[2:]
    keep, send, bo_out, ng_out = refs[:4]
    n2_v, n2t_v, cot_v, cott_v, w, stage, bo, ng, mix_v, gg_v, ug_v, sem_w, sem_o, sem_i = refs[4:]
    half = D // 2
    tiles = width // FT

    def weight_copies(f):
        out = []
        for j in range(3):
            col = pl.multiple_of(j * width + f * FT, FT)
            for s, src in enumerate((wlo, whi)):
                out.append(
                    pltpu.make_async_copy(
                        src.at[:, pl.ds(start + col, FT)],
                        w.at[pl.ds(s * half, half), pl.ds(col, FT)],
                        sem_w.at[f, 2 * j + s],
                    )
                )
        return out

    def term_copies(f):
        out = []
        for j in range(3):
            col = pl.multiple_of(j * width + f * FT, FT)
            for s, dst in enumerate((keep, send)):
                out.append(
                    pltpu.make_async_copy(
                        stage.at[pl.ds(s * half, half), pl.ds(col, FT)],
                        dst.at[:, pl.ds(col, FT)],
                        sem_o.at[f, 2 * j + s],
                    )
                )
        return out

    first = [
        pltpu.make_async_copy(n2, n2_v, sem_i.at[0]),
        pltpu.make_async_copy(cot, cot_v, sem_i.at[1]),
    ]
    second = [
        pltpu.make_async_copy(n2t, n2t_v, sem_i.at[2]),
        pltpu.make_async_copy(cott, cott_v, sem_i.at[3]),
    ]
    if not lead:
        sums_in = [
            pltpu.make_async_copy(bo_in, bo, sem_i.at[4]),
            pltpu.make_async_copy(ng_in, ng, sem_i.at[5]),
        ]
    sums_out = [
        pltpu.make_async_copy(bo, bo_out, sem_i.at[6]),
        pltpu.make_async_copy(ng, ng_out, sem_i.at[7]),
    ]
    for c in weight_copies(0) + first:
        c.start()
    if not lead:
        for c in sums_in:
            c.start()
    for c in second:
        c.start()
    for f in range(1, tiles):
        for c in weight_copies(f):
            c.start()
    if lead:
        bo[...] = jnp.zeros_like(bo)
        ng[...] = jnp.zeros_like(ng)
    for c in first:
        c.wait()

    def step(f, carry):
        for c in weight_copies(f):
            c.wait()
        at = [pl.ds(pl.multiple_of(j * width + f * FT, FT), FT) for j in range(3)]

        def tokens(i, inner):
            rows = pl.ds(pl.multiple_of(i * TILE, TILE), TILE)
            n = n2_v[rows, :]
            gate = nn(n, w[:, at[0]])
            upward = nn(n, w[:, at[1]])
            mixed_grad = nn(cot_v[rows, :], w[:, at[2]])
            square = gate * gate
            bend = jnp.tanh(GELU_A * (gate + GELU_B * (gate * square)))
            curve = 0.5 * (1.0 + bend)
            active = gate * curve
            slope = curve + (0.5 * gate) * (1.0 - bend * bend) * (GELU_A * (1.0 + (3.0 * GELU_B) * square))
            mixed = (active * upward).astype(BF)
            gate_grad = (mixed_grad * upward * slope).astype(BF)
            up_grad = (mixed_grad * active).astype(BF)
            mix_v[rows, :] = mixed
            gg_v[rows, :] = gate_grad
            ug_v[rows, :] = up_grad
            if not lead:

                @pl.when((f == 0) & (i == 0))
                def _():
                    for c in sums_in:
                        c.wait()

            bo[rows, :] += nt(mixed, w[:, at[2]])
            ng[rows, :] += nt(gate_grad, w[:, at[0]]) + nt(up_grad, w[:, at[1]])
            return inner

        lax.fori_loop(0, SEQ // TILE, tokens, 0)

        @pl.when(f == 0)
        def _():
            for c in second:
                c.wait()

        @pl.when(f == tiles - 1)
        def _():
            for c in sums_out:
                c.start()

        def features(i, inner):
            rows = pl.ds(pl.multiple_of(i * TILE, TILE), TILE)
            n = n2t_v[rows, :]
            stage[rows, at[0]] = nn(n, gg_v[...]).astype(BF)
            stage[rows, at[1]] = nn(n, ug_v[...]).astype(BF)
            stage[rows, at[2]] = nn(cott_v[rows, :], mix_v[...]).astype(BF)
            return inner

        lax.fori_loop(0, D // TILE, features, 0)
        for c in term_copies(f):
            c.start()
        return carry

    lax.fori_loop(0, tiles, step, 0)
    for c in sums_out:
        c.wait()

    def drain(f, carry):
        for c in term_copies(f):
            c.wait()
        return carry

    lax.fori_loop(0, tiles, drain, 0)


def feed(n2, n2t, cot, cott, blocks, start, width, sums):
    lead = sums is None
    tiles = width // FT
    acts = [n2, n2t, cot, cott, *blocks] + ([] if lead else list(sums))
    half = jax.ShapeDtypeStruct((D // 2, 3 * width), BF)
    total = jax.ShapeDtypeStruct((SEQ, D), F32)
    bf = lambda *s: pltpu.VMEM(s, BF)
    return pl.pallas_call(
        functools.partial(feed_kernel, lead, width, start),
        in_specs=[ANY] * len(acts),
        out_specs=[ANY] * 4,
        out_shape=[half, half, total, total],
        scratch_shapes=[
            bf(SEQ, D), bf(D, SEQ), bf(SEQ, D), bf(D, SEQ), bf(D, 3 * width), bf(D, 3 * width),
            pltpu.VMEM((SEQ, D), F32), pltpu.VMEM((SEQ, D), F32),
            bf(SEQ, FT), bf(SEQ, FT), bf(SEQ, FT),
            pltpu.SemaphoreType.DMA((tiles, 6)), pltpu.SemaphoreType.DMA((tiles, 6)), pltpu.SemaphoreType.DMA((8,)),
        ],
        compiler_params=pltpu.CompilerParams(vmem_limit_bytes=VLIM),
        cost_estimate=cost(9 * 2 * SEQ * D * width, 12 * D * width + 24 * SEQ * D, SEQ * width),
        name="feed_forward",
    )(*acts)


def middle_kernel(layout, *refs):
    n = len(layout)
    h_ref, ng_ref, c_ref, gains_ref = refs[:4]
    blocks = refs[4 : 4 + n]
    hg_ref, bt_ref, ag_ref, gain_ref, w, sems = refs[4 + n :]

    @pl.when(pl.program_id(0) == 0)
    def _():
        copies = block_copies(blocks, layout, w, sems)
        for c in copies:
            c.start()
        for c in copies:
            c.wait()
        gain_ref[...] = jnp.zeros_like(gain_ref)

    hidden = h_ref[...]
    grad = ng_ref[...]
    scale = scaled_rows(hidden)
    gain_ref[0:1, :] += jnp.sum(grad * hidden * scale, axis=0, keepdims=True)
    grad = grad * gains_ref[1:2, :]
    mean = jnp.mean(grad * hidden, axis=-1, keepdims=True)
    out = c_ref[...].astype(F32) + (scale * grad - hidden * (scale * scale * scale * mean))
    hg_ref[...] = out
    low = out.astype(BF)
    bt_ref[...] = low.T
    ag_ref[...] = nn(low, w[...]).astype(BF)


def middle(hidden, ng, cot, gains, blocks, layout):
    rows = TILE
    tok = lambda c: pl.BlockSpec((rows, c), lambda i: (i, 0))
    return pl.pallas_call(
        functools.partial(middle_kernel, layout),
        grid=(SEQ // rows,),
        in_specs=[tok(D), tok(D), tok(D), pl.BlockSpec((8, D), lambda i: (0, 0))] + [ANY] * len(blocks),
        out_specs=[tok(D), pl.BlockSpec((D, rows), lambda i: (0, i)), tok(D), pl.BlockSpec((8, D), lambda i: (0, 0))],
        out_shape=[
            jax.ShapeDtypeStruct((SEQ, D), F32),
            jax.ShapeDtypeStruct((D, SEQ), BF),
            jax.ShapeDtypeStruct((SEQ, D), BF),
            jax.ShapeDtypeStruct((8, D), F32),
        ],
        scratch_shapes=[pltpu.VMEM((D, D), BF), pltpu.SemaphoreType.DMA((len(blocks),))],
        compiler_params=params(),
        cost_estimate=cost(2 * SEQ * D * D, 20 * SEQ * D),
        name="hidden_gradient",
    )(hidden, ng, cot, gains, *blocks)


def terms_kernel(*refs):
    left, rights, (keep, send) = refs[0], refs[1:-2], refs[-2:]
    i = pl.program_id(0)

    def work(out):
        at = 0
        for r in rights:
            wide = r.shape[1]
            out[:, at : at + wide] = nn(left[...], r[...]).astype(BF)
            at += wide

    @pl.when(i < D // TILE // 2)
    def _():
        work(keep)

    @pl.when(i >= D // TILE // 2)
    def _():
        work(send)


def weight_terms(turned, rights):
    width = sum(r.shape[1] for r in rights)
    half = D // TILE // 2
    sh = jax.ShapeDtypeStruct((D // 2, width), BF)
    return pl.pallas_call(
        terms_kernel,
        grid=(D // TILE,),
        in_specs=[pl.BlockSpec((TILE, SEQ), lambda i: (i, 0))]
        + [pl.BlockSpec(r.shape, lambda i: (0, 0)) for r in rights],
        out_specs=[
            pl.BlockSpec((TILE, width), lambda i: (jnp.minimum(i, half - 1), 0)),
            pl.BlockSpec((TILE, width), lambda i: (jnp.maximum(i - half, 0), 0)),
        ],
        out_shape=[sh, sh],
        compiler_params=params(),
        cost_estimate=cost(2 * SEQ * D * width, 4 * SEQ * D + 4 * D * width),
        name="weight_terms",
    )(turned, *rights)


def last_kernel(size, layouts, *refs):
    n = [len(l) for l in layouts]
    back_ref, x_ref, hg_ref, gains_ref = refs[:4]
    grads = refs[4:10]
    blocks = [refs[10 : 10 + n[0]], refs[10 + n[0] : 10 + n[0] + n[1]]]
    out_ref, gain_ref, w0, w1, scratch, sem0, sem1 = refs[10 + n[0] + n[1] :]

    @pl.when(pl.program_id(0) == 0)
    def _():
        copies = block_copies(blocks[0], layouts[0], w0, sem0) + block_copies(blocks[1], layouts[1], w1, sem1)
        for c in copies:
            c.start()
        for c in copies:
            c.wait()
        gain_ref[...] = jnp.zeros_like(gain_ref)

    grad = None
    for g, w in ((0, w0), (1, w1)):
        for j in range(3):
            part = nt(grads[3 * g + j][...], w[:, j * GROUP : (j + 1) * GROUP])
            grad = part if grad is None else grad + part
    x = x_ref[...].astype(F32)
    scale = scaled_rows(x)
    gain_ref[0:1, :] += jnp.sum(grad * x * scale, axis=0, keepdims=True)
    grad = grad * gains_ref[0:1, :]
    mean = jnp.mean(grad * x, axis=-1, keepdims=True)
    scratch[...] = hg_ref[...] + (scale * grad - x * (scale * scale * scale * mean))
    for q, chunk in shift_blocks(lambda at: scratch[:, pl.ds(at, BLK)], back_ref, size):
        out_ref[:, q * BLK : (q + 1) * BLK] = chunk


def last(back, x, hg, gains, grads, blocks, layouts, size):
    rows = TILE
    tok = lambda c: pl.BlockSpec((rows, c), lambda i: (i, 0))
    return pl.pallas_call(
        functools.partial(last_kernel, size, layouts),
        grid=(SEQ // rows,),
        in_specs=[SMEM, tok(D), tok(D), pl.BlockSpec((8, D), lambda i: (0, 0))]
        + [tok(GROUP)] * 6
        + [ANY] * (len(blocks[0]) + len(blocks[1])),
        out_specs=[tok(D), pl.BlockSpec((8, D), lambda i: (0, 0))],
        out_shape=[jax.ShapeDtypeStruct((SEQ, D), F32), jax.ShapeDtypeStruct((8, D), F32)],
        scratch_shapes=[
            pltpu.VMEM((D, 3 * GROUP), BF), pltpu.VMEM((D, 3 * GROUP), BF), pltpu.VMEM((rows, D), F32),
            pltpu.SemaphoreType.DMA((len(blocks[0]),)), pltpu.SemaphoreType.DMA((len(blocks[1]),)),
        ],
        compiler_params=params(),
        cost_estimate=cost(2 * SEQ * D * 6 * GROUP, 20 * SEQ * D),
        name="input_gradient",
    )(back, x, hg, gains, *grads, *blocks[0], *blocks[1])


def output_plain(size, back_ref, seg_ref, h_ref, bo_ref, out_ref, scratch):
    live = seg_ref[...] > 0
    scratch[...] = h_ref[...] + bo_ref[...]
    for q, chunk in shift_blocks(lambda at: scratch[:, pl.ds(at, BLK)], back_ref, size):
        out_ref[:, q * BLK : (q + 1) * BLK] = jnp.where(live, chunk, 0.0).astype(BF)


def block_output_of(back, segk, hidden, bo, size):
    rows = TILE
    tok = lambda c: pl.BlockSpec((rows, c), lambda i: (i, 0))
    return pl.pallas_call(
        functools.partial(output_plain, size),
        grid=(SEQ // rows,),
        in_specs=[SMEM, tok(BLK), tok(D), tok(D)],
        out_specs=tok(D),
        out_shape=jax.ShapeDtypeStruct((SEQ, D), BF),
        scratch_shapes=[pltpu.VMEM((rows, D), F32)],
        compiler_params=params(),
        cost_estimate=cost(0, 10 * SEQ * D),
        name="block_output",
    )(back, segk, hidden, bo)


def gains_kernel(size, back_ref, one_ref, two_ref, out_ref):
    for j, ref in enumerate((one_ref, two_ref)):
        for q, chunk in shift_blocks(lambda at: ref[:, pl.ds(at, BLK)], back_ref, size):
            out_ref[8 * j + q : 8 * j + q + 1, :] = chunk[0:1]


def natural_gains(back, one, two, size):
    return pl.pallas_call(
        functools.partial(gains_kernel, size),
        in_specs=[SMEM, pl.BlockSpec(memory_space=pltpu.VMEM), pl.BlockSpec(memory_space=pltpu.VMEM)],
        out_specs=pl.BlockSpec(memory_space=pltpu.VMEM),
        out_shape=jax.ShapeDtypeStruct((16, BLK), F32),
        name="gain_terms",
    )(back, one, two)


class Slice:
    def __init__(self, mesh):
        self.count = mesh.shape["dp"] * mesh.shape["fsdp"]
        self.inner = mesh.shape["fsdp"]
        self.core = self.inner
        bits = [1 << b for b in range(self.count.bit_length() - 1)]
        self.rest = [b for b in reversed(bits) if b not in (1, 2, self.core)]
        self.order = [self.core, 2, 1] + self.rest[::-1]
        self.size = D // self.count

    def place(self, index):
        p = index * 0
        for b in self.order:
            p = 2 * p + (index // b) % 2
        return p

    def swap(self, x, bit):
        return lax.ppermute(x, AXES, [(i, i ^ bit) for i in range(self.count)])

    def gather(self, shard, cut):
        line = shard
        for b in self.rest:
            line = jnp.concatenate([line, self.swap(line, b)], axis=0)
        across, along = self.swap(line, 1), self.swap(line, 2)
        low = self.swap(across[:, :cut], 2)
        high = self.swap(along[:, cut:], 1)
        return line, across, along, low, high

    def gather_split(self, shard, cut):
        own = self.gather(shard, cut)
        return own + tuple(self.swap(x, self.core) for x in own)

    def gather_whole(self, shard, cut):
        line, across, along, low, high = self.gather(shard, cut)
        own = jnp.concatenate([line, across, along, jnp.concatenate([low, high], axis=1)], axis=0)
        return own, self.swap(own, self.core)

    def scatter(self, keep, send, cut):
        got = self.swap(send, self.core)
        quarter = D // 8

        def total(r, c):
            rows = slice(r * quarter, (r + 1) * quarter)
            return keep[rows, c].astype(F32) + got[rows, c].astype(F32)

        a, b, both = slice(0, cut), slice(cut, None), slice(None)
        low = self.swap(total(3, a).astype(BF), 2)
        high = self.swap(total(3, b).astype(BF), 1)
        across = jnp.concatenate([total(1, a) + low.astype(F32), total(1, b)], axis=1).astype(BF)
        along = jnp.concatenate([total(2, a), total(2, b) + high.astype(F32)], axis=1).astype(BF)
        line = total(0, both) + self.swap(across, 1).astype(F32) + self.swap(along, 2).astype(F32)
        for bit in self.rest[::-1]:
            half = line.shape[0] // 2
            line = line[:half] + self.swap(line[half:].astype(BF), bit).astype(F32)
        return line

    def sum_all(self, x):
        for bit in self.rest + [1, 2, self.core]:
            x = x + self.swap(x, bit)
        return x


def split_layout(width, cut, used=None):
    used = width if used is None else used
    q = D // 8
    out = []
    for half in range(2):
        at = half * 4 * q
        out += [(at + j * q, q, 0, used, 0) for j in range(3)]
        out += [(at + 3 * q, q, 0, cut, 0), (at + 3 * q, q, cut, used - cut, 0)]
    return tuple(out)


def on_device(
    links,
    layer_input,
    segment_ids,
    relative_buckets,
    first_gain,
    query_weight,
    key_weight,
    value_weight,
    output_projection,
    relative_table,
    second_gain,
    gate_weight,
    up_weight,
    down_projection,
    output_cotangent,
):
    size = links.size
    me = lax.axis_index("dp") * links.inner + lax.axis_index("fsdp")
    place = np.array([links.place(i) for i in range(links.count)], np.int32)
    index = np.argsort(place).astype(np.int32)
    source = jnp.asarray(index) ^ me
    back = jnp.asarray(place) ^ links.place(me)

    gains_shard = jnp.pad(jnp.stack([first_gain, second_gain], axis=1), ((0, 0), (0, BLK - 2)))
    shards = []
    for g in range(2):
        cols = slice(g * GROUP, (g + 1) * GROUP)
        parts = [query_weight[:, cols], key_weight[:, cols], value_weight[:, cols]]
        shards.append(jnp.concatenate(parts + ([gains_shard] if g == 0 else []), axis=1))
    at = 0
    for n, width in enumerate(PIECES):
        cols = slice(at, at + width)
        parts = [gate_weight[:, cols], up_weight[:, cols], down_projection[:, cols]]
        shards.append(jnp.concatenate(([output_projection] if n == 0 else []) + parts, axis=1))
        at += width

    cuts = (7 * BLK, 6 * BLK)
    lead_blocks = links.gather_split(shards[0], cuts[0])
    next_blocks = links.gather_split(shards[1], cuts[1])
    feed_blocks = [links.gather_whole(s, s.shape[1] // 2) for s in shards[2:]]
    layout0 = split_layout(3 * GROUP + BLK, cuts[0])
    layout0_used = split_layout(3 * GROUP + BLK, cuts[0], 3 * GROUP)
    layout1 = split_layout(3 * GROUP, cuts[1])
    layout_o = tuple((s * D // 2, D // 2, 0, D, 0) for s in range(2))

    segk = jnp.broadcast_to(segment_ids[:, None], (SEQ, BLK))
    segq = jnp.where(segment_ids > 0, segment_ids, -1).reshape(NB, BLK)
    spans = ranges(segment_ids)
    one_hot = (relative_buckets[::-1][:, None] == jnp.arange(BUCKETS)[None, :]).astype(BF)
    one_hot = jnp.pad(one_hot, ((0, 1), (0, 0)))
    offsets = lax.dot_general(relative_table, one_hot, (((0,), (1,)), ((), ())), preferred_element_type=F32)
    strips = make_strips(offsets.reshape(HEADS // 2, 2, 2 * SEQ))
    x, cot, cott = prepare(source, layer_input, output_cotangent, segk, size)

    qkv0, normed, turned, gains = project(x, lead_blocks, layout0, True)
    att0, lse0 = attn_fwd(spans, segk, segq, strips, qkv0, 4, 0)
    (qkv1,) = project(normed, next_blocks, layout1, False)
    att1, lse1 = attn_fwd(spans, segk, segq, strips, qkv1, 4, 4)
    hidden, n2, n2t = hidden_units(att0, att1, x, gains, feed_blocks[0], layout_o)

    sums = None
    feed_terms = []
    for n, width in enumerate(PIECES):
        keep, send, bo, ng = feed(n2, n2t, cot, cott, feed_blocks[n], D if n == 0 else 0, width, sums)
        sums = (bo, ng)
        feed_terms.append(links.scatter(keep, send, keep.shape[1] // 2))
    block_output = block_output_of(back, segk, hidden, bo, size)
    hidden_grad, branch_t, attended_grad, second_term = middle(hidden, ng, cot, gains, feed_blocks[0], layout_o)

    grads0 = attn_bwd(spans, segk, segq, strips, qkv0, attended_grad, lse0, 4, 0)
    keep_o, send_o = weight_terms(branch_t, [att0, att1])
    keep0, send0 = weight_terms(turned, grads0[:3])
    term_o = links.scatter(keep_o, send_o, D // 2)
    term0 = links.scatter(keep0, send0, 6 * BLK)
    grads1 = attn_bwd(spans, segk, segq, strips, qkv1, attended_grad, lse1, 4, 4)
    keep1, send1 = weight_terms(turned, grads1[:3])
    term1 = links.scatter(keep1, send1, 6 * BLK)
    input_gradient, first_term = last(
        back, x, hidden_grad, gains, [*grads0[:3], *grads1[:3]], [lead_blocks, next_blocks], [layout0_used, layout1], size
    )
    offset_grads = jnp.concatenate([grads0[3], grads1[3]], axis=0).reshape(HEADS, 2 * SEQ)
    table_term = lax.dot_general(
        one_hot.astype(F32), offset_grads, (((0,), (1,)), ((), ())), precision=HIGHEST, preferred_element_type=F32
    )
    small = jnp.concatenate(
        [natural_gains(back, first_term, second_term, size), table_term.reshape(-1, BLK), jnp.zeros((4, BLK), F32)], axis=0
    )
    small = links.sum_all(small)
    gain_sums = small[:16].reshape(2, D)
    mine = lax.dynamic_slice_in_dim(gain_sums, me * size, size, 1)
    table_gradient = small[16:20].reshape(BUCKETS, HEADS)

    qkv_grads = [
        jnp.concatenate([term0[:, j * GROUP : (j + 1) * GROUP], term1[:, j * GROUP : (j + 1) * GROUP]], axis=1)
        for j in range(3)
    ]
    feed_grads = [
        jnp.concatenate([t[:, j * w : (j + 1) * w] for t, w in zip(feed_terms, PIECES)], axis=1) for j in range(3)
    ]
    return (
        block_output,
        input_gradient,
        *qkv_grads,
        term_o,
        *feed_grads,
        mine[0],
        mine[1],
        table_gradient,
    )


def solution(mesh):
    rows, flat, full = P(AXES, None), P(AXES), P()
    return jax.shard_map(
        functools.partial(on_device, Slice(mesh)),
        mesh=mesh,
        in_specs=(rows, flat, full, flat, rows, rows, rows, rows, full, flat, rows, rows, rows, rows),
        out_specs=(rows,) * 9 + (flat, flat, full),
        check_vma=False,
    )
```

```python
import functools

import jax
import jax.numpy as jnp
import numpy as np
from jax import lax
from jax.experimental import pallas as pl
from jax.experimental.pallas import tpu as pltpu
from jax.sharding import PartitionSpec as P

F32 = jnp.float32
BF = jnp.bfloat16
HEADS = 16
BUCKETS = 32
SEQ = 1024
D = 1024
FF = 2816
BLK = 128
NB = SEQ // BLK
STRIP = (2 * NB - 1) * BLK
EPS = 1e-06
NEG = -1e30
VLIM = 60 * 1024 * 1024
AXES = ("dp", "fsdp")
GROUP = 512
PIECES = (768, 1024, 1024)
TILE = 512
FT = 256
ANY = pl.BlockSpec(memory_space=pl.ANY)
SMEM = pl.BlockSpec(memory_space=pltpu.SMEM)
HIGHEST = lax.Precision.HIGHEST
RATE = 1e9
GELU_A = 0.7978845608028654
GELU_B = 0.044715


def params(grid=1):
    return pltpu.CompilerParams(vmem_limit_bytes=VLIM, dimension_semantics=("arbitrary",) * grid)


def cost(flops, moved, trans=0):
    return pl.CostEstimate(flops=int(flops), bytes_accessed=int(moved), transcendentals=int(trans))


def after(kernel, used, deps):
    if not deps:
        return kernel
    return lambda *refs: kernel(*refs[:used], *refs[used + len(deps) :])


def nt(a,b): return lax.dot_general(a,b,(((1,),(1,)),((),())),preferred_element_type=F32)
def nn(a,b): return lax.dot_general(a,b,(((1,),(0,)),((),())),preferred_element_type=F32)

def build_strip(rev_ref, strip):
    for h in range(2):
        row=jnp.broadcast_to(rev_ref[h:h+1,:],(8,2*SEQ))
        base=pltpu.roll(row,0,1,stride=1,stride_axis=0)
        for m in range(BLK//8):
            turned=pltpu.roll(base,(8*m-(BLK-1))%(2*SEQ),1)
            for d in range(2*NB-1):
                e=2*NB-2-d
                strip[d*BLK+8*m:d*BLK+8*m+8,h*BLK:(h+1)*BLK]=turned[:,e*BLK:(e+1)*BLK]

def fold_strip(strip, out_ref):
    for h in range(2):
        total=jnp.zeros((8,2*SEQ),F32)
        for m in range(BLK//8):
            parts=[strip[(2*NB-2-e)*BLK+8*m:(2*NB-2-e)*BLK+8*m+8,h*BLK:(h+1)*BLK] for e in range(2*NB-1)]
            parts.append(jnp.zeros((8,BLK),F32))
            total=total+pltpu.roll(jnp.concatenate(parts,axis=1),(BLK-1-8*m)%(2*SEQ),1)
        row=total[0:1]
        for s in range(1,8):
            row=row+pltpu.roll(total[s:s+1],2*SEQ-s,1)
        out_ref[h:h+1,:]=row

def lanes_mask():
    lane=lax.broadcasted_iota(jnp.int32,(1,BLK),1)
    return lane<64

def stack_heads(x, first):
    zero=jnp.zeros_like(x)
    return jnp.concatenate([jnp.where(first,x,zero),jnp.where(first,zero,x)],axis=0)


def strip_kernel(rev_ref, strip):
    build_strip(rev_ref, strip)

def make_strips(rev, deps=()):
    return pl.pallas_call(after(strip_kernel, 1, deps),grid=(8,),
        in_specs=[pl.BlockSpec((None,2,2*SEQ),lambda p:(p,0,0))]+[ANY]*len(deps),
        out_specs=pl.BlockSpec((None,STRIP,2*BLK),lambda p:(p,0,0)),
        out_shape=jax.ShapeDtypeStruct((8,STRIP,2*BLK),F32),
        compiler_params=pltpu.CompilerParams(vmem_limit_bytes=VLIM),
        name="bias_strips")(rev, *deps)

def attn_fwd_kernel(UNIT, rng_ref, segk_ref, segq_ref, strip, q_ref, k_ref, v_ref, o_ref, lse_ref, vt):
    first=lanes_mask()
    for u in range(UNIT):
        vt[u]=v_ref[:,u*BLK:(u+1)*BLK].T
    mean=jnp.sum(v_ref[...].astype(F32),axis=0,keepdims=True)*(1.0/SEQ)

    def block(qi, carry):
        q0=pl.multiple_of(qi*BLK,BLK)
        lo=rng_ref[qi]; width=rng_ref[NB+qi]
        k0=pl.multiple_of(lo*BLK,BLK)
        b0=pl.multiple_of((lo-qi+NB-1)*BLK,BLK)
        segq=segq_ref[pl.ds(qi,1),:]
        @pl.when(width==0)
        def _():
            o_ref[pl.ds(q0,BLK),:]=jnp.broadcast_to(mean,(BLK,UNIT*BLK)).astype(BF)
            for u in range(UNIT):
                lse_ref[u,pl.ds(qi,1),:]=jnp.zeros((1,2*BLK),F32)
        for w in range(1,NB+1):
            @pl.when(width==w)
            def _():
                rows=w*BLK
                allowed=segk_ref[pl.ds(k0,rows),:]==segq
                live_row=segq>0
                live_row=jnp.concatenate([live_row,live_row],axis=1)
                live_col=segk_ref[pl.ds(q0,BLK),:]>0
                units=[slice(u*BLK,(u+1)*BLK) for u in range(UNIT)]
                qcats=[stack_heads(q_ref[pl.ds(q0,BLK),lanes],first) for lanes in units]
                scores=[nt(k_ref[pl.ds(k0,rows),lanes],qcat) for lanes,qcat in zip(units,qcats)]
                probs=[]; stats=[]; totals=[]
                for u in range(UNIT):
                    both=[]; stat=[]; tot=[]
                    s=scores[u]+strip[u,pl.ds(b0,rows),:]
                    for h in range(2):
                        sh=jnp.where(allowed,s[:,h*BLK:(h+1)*BLK],NEG)
                        peak=jnp.max(sh,axis=0,keepdims=True)
                        e=jnp.exp(sh-peak)
                        t=jnp.sum(e,axis=0,keepdims=True)
                        both.append(e.astype(BF)); stat.append(peak+jnp.log(t)); tot.append(t)
                    probs.append(jnp.concatenate(both,axis=1)); stats.append(jnp.concatenate(stat,axis=1)); totals.append(jnp.concatenate(tot,axis=1))
                ots=[nn(vt[u,:,pl.ds(k0,rows)],probs[u]) for u in range(UNIT)]
                for u,lanes in enumerate(units):
                    ot=ots[u]*(1.0/totals[u])
                    o=jnp.concatenate([ot[:64,:BLK],ot[64:,BLK:]],axis=0).T
                    o_ref[pl.ds(q0,BLK),lanes]=jnp.where(live_col,o,mean[:,lanes]).astype(BF)
                    lse_ref[u,pl.ds(qi,1),:]=jnp.where(live_row,stats[u],0.0)
        return carry
    lax.fori_loop(0,NB,block,0)

def attn_bwd_kernel(UNIT, rng_ref, segk_ref, segq_ref, strip, q_ref, k_ref, v_ref, g_ref, lse_ref,
                    dq_ref, dk_ref, dv_ref, off_ref, dstrip, kt, dk, dv):
    first=lanes_mask()
    dstrip[...]=jnp.zeros_like(dstrip)
    dk[...]=jnp.zeros_like(dk)
    for u in range(UNIT):
        lanes=slice(u*BLK,(u+1)*BLK)
        kt[u]=k_ref[:,lanes].T
        padded=jnp.where(segk_ref[...]>0,0.0,g_ref[:,lanes].astype(F32))
        dv[:,lanes]=jnp.broadcast_to(jnp.sum(padded,axis=0,keepdims=True)*(1.0/SEQ),(SEQ,BLK))

    def block(qi, carry):
        q0=pl.multiple_of(qi*BLK,BLK)
        lo=rng_ref[qi]; width=rng_ref[NB+qi]
        k0=pl.multiple_of(lo*BLK,BLK)
        b0=pl.multiple_of((lo-qi+NB-1)*BLK,BLK)
        segq=segq_ref[pl.ds(qi,1),:]
        @pl.when(width==0)
        def _():
            dq_ref[pl.ds(q0,BLK),:]=jnp.zeros((BLK,UNIT*BLK),BF)
        for w in range(1,NB+1):
            @pl.when(width==w)
            def _():
                rows=w*BLK
                allowed=segk_ref[pl.ds(k0,rows),:]==segq
                units=[slice(u*BLK,(u+1)*BLK) for u in range(UNIT)]
                qcats=[stack_heads(q_ref[pl.ds(q0,BLK),lanes],first) for lanes in units]
                gcats=[stack_heads(g_ref[pl.ds(q0,BLK),lanes],first) for lanes in units]
                scores=[nt(k_ref[pl.ds(k0,rows),lanes],qcat) for lanes,qcat in zip(units,qcats)]
                dps=[nt(v_ref[pl.ds(k0,rows),lanes],gcat) for lanes,gcat in zip(units,gcats)]
                probs=[]; grads=[]
                for u in range(UNIT):
                    lse=lse_ref[u,pl.ds(qi,1),:]
                    s=scores[u]+strip[u,pl.ds(b0,rows),:]
                    ps=[]; ds=[]
                    for h in range(2):
                        cols=slice(h*BLK,(h+1)*BLK)
                        prob=jnp.exp(jnp.where(allowed,s[:,cols],NEG)-lse[:,cols])
                        t=prob*dps[u][:,cols]
                        inner=jnp.sum(t,axis=0,keepdims=True)
                        d=t-prob*inner
                        dstrip[u,pl.ds(b0,rows),cols]+=d
                        ps.append(prob.astype(BF)); ds.append(d.astype(BF))
                    probs.append(jnp.concatenate(ps,axis=1)); grads.append(jnp.concatenate(ds,axis=1))
                for u,lanes in enumerate(units):
                    dv[pl.ds(k0,rows),lanes]+=nn(probs[u],gcats[u])
                dqts=[nn(kt[u,:,pl.ds(k0,rows)],grads[u]) for u in range(UNIT)]
                for u,lanes in enumerate(units):
                    dk[pl.ds(k0,rows),lanes]+=nn(grads[u],qcats[u])
                for u,lanes in enumerate(units):
                    dq_ref[pl.ds(q0,BLK),lanes]=jnp.concatenate([dqts[u][:64,:BLK],dqts[u][64:,BLK:]],axis=0).T.astype(BF)
        return carry
    lax.fori_loop(0,NB,block,0)
    dk_ref[...]=dk[...].astype(BF)
    dv_ref[...]=dv[...].astype(BF)
    for u in range(UNIT):
        fold_strip(dstrip.at[u], off_ref.at[u])

def attn_fwd(rng, segk, segq, strips, qkv, first_pair, deps=()):
    unit = 4
    wide = unit * BLK
    c = lambda o: pl.BlockSpec((SEQ, wide), lambda p, r: (0, o))
    gs = pltpu.PrefetchScalarGridSpec(
        num_scalar_prefetch=1,
        grid=(1,),
        in_specs=[
            pl.BlockSpec((SEQ, BLK), lambda p, r: (0, 0)),
            pl.BlockSpec((NB, BLK), lambda p, r: (0, 0)),
            pl.BlockSpec((unit, STRIP, 2 * BLK), lambda p, r: (first_pair // unit, 0, 0)),
            c(0), c(1), c(2),
        ] + [ANY] * len(deps),
        out_specs=[c(0), pl.BlockSpec((unit, NB, 2 * BLK), lambda p, r: (0, 0, 0))],
        scratch_shapes=[pltpu.VMEM((unit, BLK, SEQ), BF)],
    )
    return pl.pallas_call(
        after(functools.partial(attn_fwd_kernel, unit), 7, deps),
        grid_spec=gs,
        out_shape=[jax.ShapeDtypeStruct((SEQ, wide), BF), jax.ShapeDtypeStruct((unit, NB, 2 * BLK), F32)],
        compiler_params=params(),
        cost_estimate=cost(13 * RATE, 4 * SEQ * wide * 2),
        name="attention_forward",
    )(rng, segk, segq, strips, qkv, qkv, qkv, *deps)


def attn_bwd(rng, segk, segq, strips, qkv, g, lse, first_pair, deps=()):
    unit = 2
    wide = unit * BLK
    f, l = first_pair // unit, first_pair % 4 // unit
    c = lambda o: pl.BlockSpec((SEQ, wide), lambda p, r: (0, o))
    gs = pltpu.PrefetchScalarGridSpec(
        num_scalar_prefetch=1,
        grid=(1,),
        in_specs=[
            pl.BlockSpec((SEQ, BLK), lambda p, r: (0, 0)),
            pl.BlockSpec((NB, BLK), lambda p, r: (0, 0)),
            pl.BlockSpec((unit, STRIP, 2 * BLK), lambda p, r: (f, 0, 0)),
            c(l), c(2 + l), c(4 + l), c(f),
            pl.BlockSpec((unit, NB, 2 * BLK), lambda p, r: (l, 0, 0)),
        ] + [ANY] * len(deps),
        out_specs=[c(0), c(0), c(0), pl.BlockSpec((unit, 2, 2 * SEQ), lambda p, r: (0, 0, 0))],
        scratch_shapes=[
            pltpu.VMEM((unit, STRIP, 2 * BLK), F32), pltpu.VMEM((unit, BLK, SEQ), BF),
            pltpu.VMEM((SEQ, wide), F32), pltpu.VMEM((SEQ, wide), F32),
        ],
    )
    sh = jax.ShapeDtypeStruct((SEQ, wide), BF)
    return pl.pallas_call(
        after(functools.partial(attn_bwd_kernel, unit), 9, deps),
        grid_spec=gs,
        out_shape=[sh, sh, sh, jax.ShapeDtypeStruct((unit, 2, 2 * SEQ), F32)],
        compiler_params=params(),
        cost_estimate=cost(12 * RATE, 8 * SEQ * wide * 2),
        name="attention_backward",
    )(rng, segk, segq, strips, qkv, qkv, qkv, g, lse, *deps)


def ranges(seg):
    s=seg.reshape(NB,BLK)
    least=s[:,0]; most=jnp.max(s,axis=1)
    lo=jnp.sum((most[None,:]<least[:,None])&(least[None,:]>0),axis=1)
    hi=jnp.sum((least[None,:]<=most[:,None])&(least[None,:]>0),axis=1)
    w=jnp.where(least>0,hi-lo,0)
    return jnp.concatenate([jnp.where(least>0,lo,0),w]).astype(jnp.int32)


def shift_blocks(load, src_ref, size):
    per = BLK // size
    lane = lax.broadcasted_iota(jnp.int32, (1, BLK), 1) // size
    for q in range(D // BLK):
        chunk = None
        for t in range(per):
            a = src_ref[q * per + t]
            piece = load(pl.multiple_of((a // per) * BLK, BLK))
            piece = pltpu.roll(piece, lax.rem((t - lax.rem(a, per)) * size + BLK, BLK), 1)
            chunk = piece if chunk is None else jnp.where(lane == t, piece, chunk)
        yield q, chunk


def prep_kernel(size, src_ref, x_ref, c_ref, seg_ref, xo_ref, co_ref, ct_ref):
    live = seg_ref[...] > 0
    for q, chunk in shift_blocks(lambda at: x_ref[:, pl.ds(at, BLK)].astype(F32), src_ref, size):
        xo_ref[:, q * BLK : (q + 1) * BLK] = chunk.astype(BF)
    for q, chunk in shift_blocks(lambda at: c_ref[:, pl.ds(at, BLK)].astype(F32), src_ref, size):
        low = jnp.where(live, chunk, 0.0).astype(BF)
        co_ref[:, q * BLK : (q + 1) * BLK] = low
        ct_ref[q * BLK : (q + 1) * BLK, :] = low.T


def prepare(src, x, c, segk, size):
    rows = TILE
    blk = lambda: pl.BlockSpec((rows, D), lambda i: (i, 0))
    sh = jax.ShapeDtypeStruct((SEQ, D), BF)
    return pl.pallas_call(
        functools.partial(prep_kernel, size),
        grid=(SEQ // rows,),
        in_specs=[SMEM, blk(), blk(), pl.BlockSpec((rows, BLK), lambda i: (i, 0))],
        out_specs=[blk(), blk(), pl.BlockSpec((D, rows), lambda i: (0, i))],
        out_shape=[sh, sh, jax.ShapeDtypeStruct((D, SEQ), BF)],
        compiler_params=params(),
        cost_estimate=cost(0, 10 * SEQ * D),
        name="prepare",
    )(src, x, c, segk)


def prep_kernel(size, src_ref, x_ref, seg_ref, xo_ref, *turned):
    live = seg_ref[...] > 0
    for q, chunk in shift_blocks(lambda at: x_ref[:, pl.ds(at, BLK)].astype(F32), src_ref, size):
        if turned:
            chunk = jnp.where(live, chunk, 0.0)
        low = chunk.astype(BF)
        xo_ref[:, q * BLK : (q + 1) * BLK] = low
        if turned:
            turned[0][q * BLK : (q + 1) * BLK, :] = low.T


def prepare(src, x, segk, size, masked, deps=()):
    rows = 256
    blk = pl.BlockSpec((rows, D), lambda i: (i, 0))
    out_specs, out_shape = [blk], [jax.ShapeDtypeStruct((SEQ, D), BF)]
    if masked:
        out_specs.append(pl.BlockSpec((D, rows), lambda i: (0, i)))
        out_shape.append(jax.ShapeDtypeStruct((D, SEQ), BF))
    return pl.pallas_call(
        after(functools.partial(prep_kernel, size), 3, deps),
        grid=(SEQ // rows,),
        in_specs=[SMEM, blk, pl.BlockSpec((rows, BLK), lambda i: (i, 0))] + [ANY] * len(deps),
        out_specs=out_specs,
        out_shape=out_shape,
        compiler_params=params(),
        cost_estimate=cost(5 * RATE, 5 * SEQ * D),
        name="prepare",
    )(src, x, segk, *deps)


def pack_kernel(spans, count, *refs):
    ins, outs = refs[:count], refs[count:]
    for out, cols in zip(outs, spans):
        at = 0
        for n, lo, hi in cols:
            out[:, at : at + hi - lo] = ins[n][:, lo:hi]
            at += hi - lo


def pack(shards, spans, deps=()):
    rows = shards[0].shape[0]
    widths = [sum(hi - lo for _, lo, hi in cols) for cols in spans]
    whole = pl.BlockSpec(memory_space=pltpu.VMEM)
    return pl.pallas_call(
        after(functools.partial(pack_kernel, spans, len(shards)), len(shards), deps),
        in_specs=[whole] * len(shards) + [ANY] * len(deps),
        out_specs=[whole] * len(widths),
        out_shape=[jax.ShapeDtypeStruct((rows, w), BF) for w in widths],
        name="pack_shards",
    )(*shards, *deps)


def join(*parts):
    return jnp.concatenate(parts, axis=0)


def add_terms(terms, rows):
    return sum(t[off : off + rows].astype(F32) for t, off in terms).astype(BF)


def finish_kernel(counts, *refs):
    sums, at = [], 0
    for n in counts:
        total = refs[at][...].astype(F32)
        for ref in refs[at + 1 : at + n]:
            total = total + ref[...].astype(F32)
        sums.append(total)
        at += n
    outs = refs[at:]
    for j in range(3):
        outs[j][:, :GROUP] = sums[0][:, D + j * GROUP : D + (j + 1) * GROUP]
        outs[j][:, GROUP:] = sums[1][:, j * GROUP : (j + 1) * GROUP]
    outs[3][...] = sums[0][:, :D]
    at = 0
    for s, width in zip(sums[2:], PIECES):
        for j in range(3):
            outs[4 + j][:, at : at + width] = s[:, j * width : (j + 1) * width]
        at += width


def finish(sets, rows, deps=()):
    flat = [x for terms in sets for x in terms]
    widths = (D,) * 4 + (FF,) * 3
    return pl.pallas_call(
        after(functools.partial(finish_kernel, tuple(len(t) for t in sets)), len(flat), deps),
        grid=(1,),
        in_specs=[pl.BlockSpec((rows, x.shape[1]), lambda i: (0, 0)) for x in flat] + [ANY] * len(deps),
        out_specs=[pl.BlockSpec((rows, w), lambda i: (0, 0)) for w in widths],
        out_shape=[jax.ShapeDtypeStruct((rows, w), F32) for w in widths],
        compiler_params=params(),
        name="weight_gradients",
    )(*flat, *deps)


def layout_of(blocks, order, cols, start=0, at=0):
    q = D // 8
    out = []
    for n, b in enumerate(blocks):
        if b.shape[0] == q:
            out.append((n, n * q, q, at, cols, 0, start))
        else:
            out += [(n, n * 4 * q + p * q, q, at, cols, j * q, start) for j, p in enumerate(order)]
    return tuple(out)


def block_copies(refs, layout, dst, sems, base=0):
    return [
        pltpu.make_async_copy(
            refs[n].at[pl.ds(frm, rows), pl.ds(start, cols)],
            dst.at[pl.ds(row, rows), pl.ds(col, cols)],
            sems.at[base + i],
        )
        for i, (n, row, rows, col, cols, frm, start) in enumerate(layout)
    ]


def fetch(refs, layout, dst, sems):
    copies = block_copies(refs, layout, dst, sems)
    for c in copies:
        c.start()
    for c in copies:
        c.wait()


def scaled_rows(x):
    return lax.rsqrt(jnp.mean(x * x, axis=-1, keepdims=True) + EPS)


def qkv_kernel(lead, layout, count, *refs):
    x_ref, blocks, refs = refs[0], refs[1 : 1 + count], refs[1 + count :]
    if lead:
        out_ref, normed_ref, turned_ref, gains_ref, w, sems = refs
    else:
        out_ref, w, sems = refs
        normed_ref = x_ref
    j = pl.program_id(0)

    @pl.when(j == 0)
    def _():
        fetch(blocks, layout, w, sems)
        if lead:
            gains_ref[...] = w[:, 3 * GROUP :].astype(F32).T[:8]

            def rows_of(i, carry):
                at = pl.multiple_of(i * 256, 256)
                x = x_ref[pl.ds(at, 256), :].astype(F32)
                low = (x * scaled_rows(x) * gains_ref[0:1, :]).astype(BF)
                normed_ref[pl.ds(at, 256), :] = low
                turned_ref[:, pl.ds(at, 256)] = low.T
                return carry

            lax.fori_loop(0, SEQ // 256, rows_of, 0)

    out_ref[...] = nn(normed_ref[...], w[:, pl.ds(pl.multiple_of(j * GROUP, GROUP), GROUP)]).astype(BF)


def project(x, blocks, layout, lead, deps=()):
    width = 3 * GROUP + (BLK if lead else 0)
    whole = lambda r, c: pl.BlockSpec((r, c), lambda j: (0, 0))
    out_specs = [pl.BlockSpec((SEQ, GROUP), lambda j: (0, j))]
    out_shape = [jax.ShapeDtypeStruct((SEQ, 3 * GROUP), BF)]
    if lead:
        out_specs += [whole(SEQ, D), whole(D, SEQ), whole(8, D)]
        out_shape += [
            jax.ShapeDtypeStruct((SEQ, D), BF),
            jax.ShapeDtypeStruct((D, SEQ), BF),
            jax.ShapeDtypeStruct((8, D), F32),
        ]
    n = len(blocks)
    return pl.pallas_call(
        after(functools.partial(qkv_kernel, lead, layout, n), 1 + n, deps),
        grid=(3,),
        in_specs=[whole(SEQ, D)] + [ANY] * (n + len(deps)),
        out_specs=out_specs,
        out_shape=out_shape,
        scratch_shapes=[pltpu.VMEM((D, width), BF), pltpu.SemaphoreType.DMA((len(layout),))],
        compiler_params=params(),
        cost_estimate=cost(6 * RATE, 2 * D * width + 4 * SEQ * D),
        name="query_key_value",
    )(x, *blocks, *deps)


def hidden_kernel(layout, count, *refs):
    a0, a1, x_ref, gains_ref = refs[:4]
    blocks = refs[4 : 4 + count]
    h_ref, n2_ref, n2t_ref, w, sems = refs[4 + count :]

    @pl.when(pl.program_id(0) == 0)
    def _():
        fetch(blocks, layout, w, sems)

    hidden = x_ref[...].astype(F32) + nt(jnp.concatenate([a0[...], a1[...]], axis=1), w[...])
    h_ref[...] = hidden
    normed = (hidden * scaled_rows(hidden) * gains_ref[1:2, :]).astype(BF)
    n2_ref[...] = normed
    n2t_ref[...] = normed.T


def hidden_units(a0, a1, x, gains, blocks, layout, deps=()):
    rows = TILE
    tok = lambda c: pl.BlockSpec((rows, c), lambda i: (i, 0))
    n = len(blocks)
    return pl.pallas_call(
        after(functools.partial(hidden_kernel, layout, n), 4 + n, deps),
        grid=(SEQ // rows,),
        in_specs=[tok(GROUP), tok(GROUP), tok(D), pl.BlockSpec((8, D), lambda i: (0, 0))] + [ANY] * (n + len(deps)),
        out_specs=[tok(D), tok(D), pl.BlockSpec((D, rows), lambda i: (0, i))],
        out_shape=[
            jax.ShapeDtypeStruct((SEQ, D), F32),
            jax.ShapeDtypeStruct((SEQ, D), BF),
            jax.ShapeDtypeStruct((D, SEQ), BF),
        ],
        scratch_shapes=[pltpu.VMEM((D, D), BF), pltpu.SemaphoreType.DMA((len(layout),))],
        compiler_params=params(),
        cost_estimate=cost(6 * RATE, 16 * SEQ * D),
        name="hidden_units",
    )(a0, a1, x, gains, *blocks, *deps)


def feed_kernel(lead, width, size, base, order_in, order_out, *refs):
    gathered = order_in is None
    n2, n2t, cot, cott = refs[:4]
    blocks, refs = refs[4 : 6 if gathered else 12], refs[6 if gathered else 12 :]
    if not lead:
        bo_in, ng_in = refs[:2]
        refs = refs[2:]
    keep, send, bo_out, ng_out = refs[:4]
    n2_v, n2t_v, cot_v, cott_v, w, stage, bo, ng, mix_v, gu_v, sem_w, sem_o, sem_i = refs[4:]
    half, q = D // 2, D // 8
    tiles = width // FT

    def ordered_copies(lo, count):
        source, whole = blocks
        for j in range(3):

            def one(p, carry):
                a = pl.multiple_of(source[p] * size, size)
                col = j * width + lo * FT
                pltpu.make_async_copy(
                    whole.at[pl.ds(a, size), pl.ds(base + col, count * FT)],
                    w.at[pl.ds(pl.multiple_of(p * size, size), size), pl.ds(col, count * FT)],
                    sem_w.at[min(lo, 1), j],
                ).start()
                return carry

            lax.fori_loop(0, D // size, one, 0)

    def ordered_wait(lo, count):
        for j in range(3):
            cols = pl.ds(j * width + lo * FT, count * FT)
            pltpu.make_async_copy(
                blocks[1].at[:, pl.ds(base + j * width + lo * FT, count * FT)], w.at[:, cols], sem_w.at[min(lo, 1), j]
            ).wait()

    def weight_copies(f):
        out = []
        for j in range(3):
            col = pl.multiple_of(j * width + f * FT, FT)
            for r, src in enumerate(blocks):
                out.append(
                    pltpu.make_async_copy(
                        src.at[:, pl.ds(col, FT)], w.at[pl.ds(r * q, q), pl.ds(col, FT)], sem_w.at[f, 8 * j + r]
                    )
                )
        return out

    def term_copies(g):
        col = pl.multiple_of(g * FT, FT)
        return [
            pltpu.make_async_copy(
                stage.at[pl.ds(s * half + p * q, q), pl.ds(col, FT)],
                dst.at[pl.ds(r * q, q), pl.ds(col, FT)],
                sem_o.at[g, 4 * s + r],
            )
            for s, dst in enumerate((keep, send))
            for r, p in enumerate(order_out)
        ]

    first = [pltpu.make_async_copy(n2, n2_v, sem_i.at[0]), pltpu.make_async_copy(cot, cot_v, sem_i.at[1])]
    second = [pltpu.make_async_copy(n2t, n2t_v, sem_i.at[2]), pltpu.make_async_copy(cott, cott_v, sem_i.at[3])]
    sums_in = []
    if not lead:
        sums_in = [pltpu.make_async_copy(bo_in, bo, sem_i.at[4]), pltpu.make_async_copy(ng_in, ng, sem_i.at[5])]
    sums_out = [pltpu.make_async_copy(bo, bo_out, sem_i.at[6]), pltpu.make_async_copy(ng, ng_out, sem_i.at[7])]
    if gathered:
        ordered_copies(0, 1)
        for c in first:
            c.start()
        ordered_copies(1, tiles - 1)
    else:
        for c in weight_copies(0) + first:
            c.start()
        for f in range(1, tiles):
            for c in weight_copies(f):
                c.start()
    for c in sums_in + second:
        c.start()
    for c in first:
        c.wait()

    def units(f, carry):
        if gathered:
            pl.when(f == 0)(lambda: ordered_wait(0, 1))
            pl.when(f == 1)(lambda: ordered_wait(1, tiles - 1))
        else:
            for c in weight_copies(f):
                c.wait()
        at = [pl.ds(pl.multiple_of(j * width + f * FT, FT), FT) for j in range(3)]

        def tokens(i, inner):
            rows = pl.ds(pl.multiple_of(i * TILE, TILE), TILE)
            n = n2_v[rows, :]
            gate = nn(n, w[:, at[0]])
            upward = nn(n, w[:, at[1]])
            mixed_grad = nn(cot_v[rows, :], w[:, at[2]])
            square = gate * gate
            bend = jnp.tanh(gate * (GELU_A + (GELU_A * GELU_B) * square))
            curve = 0.5 * (1.0 + bend)
            active = gate * curve
            slope = curve + (0.5 * gate) * (1.0 - bend * bend) * (GELU_A + (3.0 * GELU_A * GELU_B) * square)
            mix_v[rows, at[0]] = (active * upward).astype(BF)
            gu_v[rows, at[0]] = (mixed_grad * upward * slope).astype(BF)
            gu_v[rows, at[1]] = (mixed_grad * active).astype(BF)
            return inner

        lax.fori_loop(0, SEQ // TILE, tokens, 0)
        return carry

    lax.fori_loop(0, tiles, units, 0)
    for c in sums_in:
        c.wait()

    def sums(i, carry):
        rows = pl.ds(pl.multiple_of(i * TILE, TILE), TILE)
        for j in range(2):
            cols = slice(j * TILE, (j + 1) * TILE)
            one = nt(mix_v[rows, :], w[cols, 2 * width :])
            two = nt(gu_v[rows, :], w[cols, : 2 * width])
            bo[rows, cols] = one if lead else bo[rows, cols] + one
            ng[rows, cols] = two if lead else ng[rows, cols] + two
        return carry

    lax.fori_loop(0, SEQ // TILE, sums, 0)
    for c in sums_out:
        c.start()
    for c in second:
        c.wait()

    def terms(left, right, start):
        def one(f, carry):
            cols = pl.ds(pl.multiple_of(f * FT, FT), FT)
            out = pl.ds(pl.multiple_of(start * FT + f * FT, FT), FT)
            stage[:, out] = nn(left[...], right[:, cols]).astype(BF)
            for c in term_copies(start + f):
                c.start()
            return carry

        return one

    lax.fori_loop(0, 2 * tiles, terms(n2t_v, gu_v, 0), 0)
    lax.fori_loop(0, tiles, terms(cott_v, mix_v, 2 * tiles), 0)
    for c in sums_out:
        c.wait()

    def drain(g, carry):
        for c in term_copies(g):
            c.wait()
        return carry

    lax.fori_loop(0, 3 * tiles, drain, 0)


def feed(n2, n2t, cot, cott, blocks, width, sums, size, base, order_in, order_out, deps=()):
    lead = sums is None
    tiles = width // FT
    acts = [n2, n2t, cot, cott, *blocks] + ([] if lead else list(sums))
    half = jax.ShapeDtypeStruct((D // 2, 3 * width), BF)
    total = jax.ShapeDtypeStruct((SEQ, D), F32)
    bf = lambda *s: pltpu.VMEM(s, BF)
    return pl.pallas_call(
        after(functools.partial(feed_kernel, lead, width, size, base, order_in, order_out), len(acts), deps),
        in_specs=[ANY] * 4 + [ANY if order_in else SMEM] + [ANY] * (len(acts) - 5 + len(deps)),
        out_specs=[ANY] * 4,
        out_shape=[half, half, total, total],
        scratch_shapes=[
            bf(SEQ, D), bf(D, SEQ), bf(SEQ, D), bf(D, SEQ), bf(D, 3 * width), bf(D, 3 * width),
            pltpu.VMEM((SEQ, D), F32), pltpu.VMEM((SEQ, D), F32),
            bf(SEQ, width), bf(SEQ, 2 * width),
            pltpu.SemaphoreType.DMA((tiles, 24)), pltpu.SemaphoreType.DMA((3 * tiles, 8)), pltpu.SemaphoreType.DMA((8,)),
        ],
        compiler_params=pltpu.CompilerParams(vmem_limit_bytes=VLIM),
        cost_estimate=cost(27 * RATE, 12 * D * width + 24 * SEQ * D, SEQ * width),
        name="feed_forward",
    )(*acts, *deps)


def middle_kernel(layout, count, *refs):
    h_ref, ng_ref, c_ref, gains_ref = refs[:4]
    blocks = refs[4 : 4 + count]
    hg_ref, bt_ref, ag_ref, gain_ref, w, sems = refs[4 + count :]

    @pl.when(pl.program_id(0) == 0)
    def _():
        fetch(blocks, layout, w, sems)
        gain_ref[...] = jnp.zeros_like(gain_ref)

    hidden = h_ref[...]
    grad = ng_ref[...]
    scale = scaled_rows(hidden)
    gain_ref[0:1, :] += jnp.sum(grad * hidden * scale, axis=0, keepdims=True)
    grad = grad * gains_ref[1:2, :]
    mean = jnp.mean(grad * hidden, axis=-1, keepdims=True)
    out = c_ref[...].astype(F32) + (scale * grad - hidden * (scale * scale * scale * mean))
    hg_ref[...] = out
    low = out.astype(BF)
    bt_ref[...] = low.T
    ag_ref[...] = nn(low, w[...]).astype(BF)


def middle(hidden, ng, cot, gains, blocks, layout, deps=()):
    rows = TILE
    tok = lambda c: pl.BlockSpec((rows, c), lambda i: (i, 0))
    n = len(blocks)
    return pl.pallas_call(
        after(functools.partial(middle_kernel, layout, n), 4 + n, deps),
        grid=(SEQ // rows,),
        in_specs=[tok(D), tok(D), tok(D), pl.BlockSpec((8, D), lambda i: (0, 0))] + [ANY] * (n + len(deps)),
        out_specs=[tok(D), pl.BlockSpec((D, rows), lambda i: (0, i)), tok(D), pl.BlockSpec((8, D), lambda i: (0, 0))],
        out_shape=[
            jax.ShapeDtypeStruct((SEQ, D), F32),
            jax.ShapeDtypeStruct((D, SEQ), BF),
            jax.ShapeDtypeStruct((SEQ, D), BF),
            jax.ShapeDtypeStruct((8, D), F32),
        ],
        scratch_shapes=[pltpu.VMEM((D, D), BF), pltpu.SemaphoreType.DMA((len(layout),))],
        compiler_params=params(),
        cost_estimate=cost(7 * RATE, 20 * SEQ * D),
        name="hidden_gradient",
    )(hidden, ng, cot, gains, *blocks, *deps)


def terms_kernel(lefts, order, *refs):
    count = sum(n for n in lefts)
    left_refs, rights = refs[: len(lefts)], refs[len(lefts) : len(lefts) + count]
    keep, send = refs[len(lefts) + count :]
    q = D // 8

    def work(out):
        at, r = 0, 0
        for left, n in zip(left_refs, lefts):
            for right in rights[r : r + n]:
                wide = right.shape[1]
                part = nn(left[...], right[...]).astype(BF)
                for j, p in enumerate(order):
                    out[j * q : (j + 1) * q, at : at + wide] = part[p * q : (p + 1) * q]
                at += wide
            r += n

    @pl.when(pl.program_id(0) == 0)
    def _():
        work(keep)

    @pl.when(pl.program_id(0) == 1)
    def _():
        work(send)


def weight_terms(sets, order, deps=()):
    lefts = [s[0] for s in sets]
    rights = [r for s in sets for r in s[1]]
    counts = tuple(len(s[1]) for s in sets)
    width = sum(r.shape[1] for r in rights)
    half = D // 2
    sh = jax.ShapeDtypeStruct((half, width), BF)
    n = len(lefts) + len(rights)
    out = pl.BlockSpec((half, width), lambda i: (0, 0))
    return pl.pallas_call(
        after(functools.partial(terms_kernel, counts, order), n, deps),
        grid=(2,),
        in_specs=[pl.BlockSpec((half, SEQ), lambda i: (i, 0)) for _ in lefts]
        + [pl.BlockSpec(r.shape, lambda i: (0, 0)) for r in rights]
        + [ANY] * len(deps),
        out_specs=[out, out],
        out_shape=[sh, sh],
        compiler_params=params(),
        cost_estimate=cost(4 * RATE * width / 1536, 4 * SEQ * D + 4 * D * width),
        name="weight_terms",
    )(*lefts, *rights, *deps)


def last_kernel(size, layout, count, blocks_n, *refs):
    back_ref, x_ref, hg_ref, gains_ref = refs[:4]
    grads = refs[4 : 4 + count]
    blocks = refs[4 + count : 4 + count + blocks_n]
    out_ref, gain_ref, w, scratch, sems = refs[4 + count + blocks_n :]

    @pl.when(pl.program_id(0) == 0)
    def _():
        fetch(blocks, layout, w, sems)
        gain_ref[...] = jnp.zeros_like(gain_ref)

    grad = nt(jnp.concatenate([g[...] for g in grads], axis=1), w[...])
    x = x_ref[...].astype(F32)
    scale = scaled_rows(x)
    gain_ref[0:1, :] += jnp.sum(grad * x * scale, axis=0, keepdims=True)
    grad = grad * gains_ref[0:1, :]
    mean = jnp.mean(grad * x, axis=-1, keepdims=True)
    scratch[...] = hg_ref[...] + (scale * grad - x * (scale * scale * scale * mean))
    for q, chunk in shift_blocks(lambda at: scratch[:, pl.ds(at, BLK)], back_ref, size):
        out_ref[:, q * BLK : (q + 1) * BLK] = chunk


def last(back, x, hg, gains, grads, blocks, layout, size, deps=()):
    rows = TILE
    tok = lambda c: pl.BlockSpec((rows, c), lambda i: (i, 0))
    n = 4 + len(grads) + len(blocks)
    return pl.pallas_call(
        after(functools.partial(last_kernel, size, layout, len(grads), len(blocks)), n, deps),
        grid=(SEQ // rows,),
        in_specs=[SMEM, tok(D), tok(D), pl.BlockSpec((8, D), lambda i: (0, 0))]
        + [tok(g.shape[1]) for g in grads]
        + [ANY] * (len(blocks) + len(deps)),
        out_specs=[tok(D), pl.BlockSpec((8, D), lambda i: (0, 0))],
        out_shape=[jax.ShapeDtypeStruct((SEQ, D), F32), jax.ShapeDtypeStruct((8, D), F32)],
        scratch_shapes=[
            pltpu.VMEM((D, 6 * GROUP), BF), pltpu.VMEM((rows, D), F32), pltpu.SemaphoreType.DMA((len(layout),)),
        ],
        compiler_params=params(),
        cost_estimate=cost(14 * RATE, 20 * SEQ * D),
        name="input_gradient",
    )(back, x, hg, gains, *grads, *blocks, *deps)


def output_kernel(size, back_ref, seg_ref, h_ref, bo_ref, out_ref, scratch):
    live = seg_ref[...] > 0
    scratch[...] = h_ref[...] + bo_ref[...]
    for q, chunk in shift_blocks(lambda at: scratch[:, pl.ds(at, BLK)], back_ref, size):
        out_ref[:, q * BLK : (q + 1) * BLK] = jnp.where(live, chunk, 0.0).astype(BF)


def block_output_of(back, segk, hidden, bo, size, deps=()):
    rows = 256
    tok = lambda c: pl.BlockSpec((rows, c), lambda i: (i, 0))
    return pl.pallas_call(
        after(functools.partial(output_kernel, size), 4, deps),
        grid=(SEQ // rows,),
        in_specs=[SMEM, tok(BLK), tok(D), tok(D)] + [ANY] * len(deps),
        out_specs=tok(D),
        out_shape=jax.ShapeDtypeStruct((SEQ, D), BF),
        scratch_shapes=[pltpu.VMEM((rows, D), F32)],
        compiler_params=params(),
        cost_estimate=cost(7 * RATE, 10 * SEQ * D),
        name="block_output",
    )(back, segk, hidden, bo, *deps)


def gains_kernel(size, back_ref, one_ref, two_ref, out_ref):
    for j, ref in enumerate((one_ref, two_ref)):
        for q, chunk in shift_blocks(lambda at: ref[:, pl.ds(at, BLK)], back_ref, size):
            out_ref[8 * j + q : 8 * j + q + 1, :] = chunk[0:1]


def natural_gains(back, one, two, size, deps=()):
    return pl.pallas_call(
        after(functools.partial(gains_kernel, size), 3, deps),
        in_specs=[SMEM, pl.BlockSpec(memory_space=pltpu.VMEM), pl.BlockSpec(memory_space=pltpu.VMEM)] + [ANY] * len(deps),
        out_specs=pl.BlockSpec(memory_space=pltpu.VMEM),
        out_shape=jax.ShapeDtypeStruct((16, BLK), F32),
        name="gain_terms",
    )(back, one, two, *deps)


NATURAL = (0, 1, 2, 3)
CROSSED = (0, 2, 1, 3)


class Slice:
    def __init__(self, mesh):
        self.count = mesh.shape["dp"] * mesh.shape["fsdp"]
        self.inner = mesh.shape["fsdp"]
        self.core = self.inner
        bits = [1 << b for b in range(self.count.bit_length() - 1)]
        self.rest = [b for b in reversed(bits) if b not in (1, 2, self.core)]
        self.order = [self.core, 2, 1] + self.rest[::-1]
        self.size = D // self.count

    def place(self, index):
        p = index * 0
        for b in self.order:
            p = 2 * p + (index // b) % 2
        return p

    def swap(self, x, bit):
        return lax.ppermute(x, AXES, [(i, i ^ bit) for i in range(self.count)])

    def sum_all(self, x):
        for bit in self.rest + [1, 2, self.core]:
            x = x + self.swap(x, bit)
        return x


class Order:
    def __init__(self):
        self.token = None

    def hold(self, args):
        leaves, tree = jax.tree.flatten(args)
        at = [i for i, x in enumerate(leaves) if hasattr(x, "aval")]
        if self.token is not None:
            held = lax.optimization_barrier([leaves[i] for i in at] + [self.token])
            for i, x in zip(at, held):
                leaves[i] = x
        return jax.tree.unflatten(tree, leaves)

    def __call__(self, f, *args):
        out = f(*self.hold(args))
        self.token = jax.tree.leaves(out)[0]
        return out


class Chain:
    def __init__(self, links, run):
        self.links, self.run, self.pending = links, run, []


def meet(run, *chains):
    arrays = run.hold([c.pending for c in chains] + [run.token])
    run.token = arrays.pop()
    for c, got in zip(chains, arrays):
        c.met(got)
        c.pending = []


class Gather(Chain):
    def __init__(self, links, run, shard, bit):
        super().__init__(links, run)
        self.line, self.bit, self.bits = run.hold(shard), bit, list(links.rest)
        self.pending = [links.swap(self.line, self.bits.pop(0))]

    def met(self, got):
        self.got = got

    def step(self):
        swap = self.links.swap
        self.line = self.run(join, self.line, self.got[0])
        if self.bits:
            self.pending = [swap(self.line, self.bits.pop(0))]
        else:
            self.pending = [swap(self.line, 1), swap(self.line, 2)]

    def corner(self):
        swap, core = self.links.swap, self.links.core
        across, along = self.got
        self.blocks = [self.line, across, along]
        self.others = [swap(b, core) for b in self.blocks]
        self.pending = [swap(across, 2) if self.bit == 2 else swap(along, 1)]

    def end(self):
        self.blocks.append(self.got[0])
        self.others.append(self.links.swap(self.got[0], self.links.core))
        return tuple(self.blocks + self.others)


class Scatter(Chain):
    def __init__(self, links, run, keep, send):
        super().__init__(links, run)
        self.terms, self.rows, self.bits = [keep], D // 8, links.rest[::-1]
        self.pending = [links.swap(run.hold(send), links.core)]

    def met(self, got):
        self.got = got

    def corner(self):
        self.terms += self.got
        send = self.run(add_terms, [(t, 3 * self.rows) for t in self.terms], self.rows)
        self.pending = [self.links.swap(send, 2)]

    def sides(self):
        along = self.run(add_terms, [(t, 2 * self.rows) for t in self.terms], self.rows)
        along = self.links.swap(along, 2)
        across = self.run(add_terms, [(t, self.rows) for t in self.terms] + [(self.got[0], 0)], self.rows)
        self.pending = [along, self.links.swap(across, 1)]

    def step(self):
        self.terms += self.got
        half = self.rows // 2
        send = self.run(add_terms, [(t, half) for t in self.terms], half)
        self.rows = half
        self.pending = [self.links.swap(send, self.bits.pop(0))]

    def ends(self):
        if self.pending:
            meet(self.run, self)
        while self.bits:
            self.step()
            meet(self.run, self)
        return self.terms + self.got


def on_device(
    links,
    layer_input,
    segment_ids,
    relative_buckets,
    first_gain,
    query_weight,
    key_weight,
    value_weight,
    output_projection,
    relative_table,
    second_gain,
    gate_weight,
    up_weight,
    down_projection,
    output_cotangent,
):
    size = links.size
    me = lax.axis_index("dp") * links.inner + lax.axis_index("fsdp")
    place = np.array([links.place(i) for i in range(links.count)], np.int32)
    index = np.argsort(place).astype(np.int32)
    source = jnp.asarray(index) ^ me
    back = jnp.asarray(place) ^ links.place(me)

    gains_shard = jnp.pad(jnp.stack([first_gain, second_gain], axis=1), ((0, 0), (0, BLK - 2)))
    w1, w2, w3 = PIECES
    feed_shards = (gate_weight, up_weight, down_projection)
    qkv_shards = (query_weight, key_weight, value_weight)
    triple = lambda lo, hi: tuple((n, lo, hi) for n in range(3))
    run = Order()
    segk = jnp.broadcast_to(segment_ids[:, None], (SEQ, BLK))
    segq = jnp.where(segment_ids > 0, segment_ids, -1).reshape(NB, BLK)
    spans = ranges(segment_ids)
    one_hot = (relative_buckets[::-1][:, None] == jnp.arange(BUCKETS)[None, :]).astype(BF)
    one_hot = jnp.pad(one_hot, ((0, 1), (0, 0)))
    offsets = lax.dot_general(relative_table, one_hot, (((0,), (1,)), ((), ())), preferred_element_type=F32)

    (first_shard,) = run(pack, qkv_shards + (gains_shard,), (triple(0, GROUP) + ((3, 0, BLK),),))
    first = Gather(links, run, first_shard, 2)
    (x,) = run(prepare, source, layer_input, segk, size, False)
    meet(run, first)
    first.step()
    (second_shard,) = run(pack, qkv_shards + (output_projection,), (triple(GROUP, 2 * GROUP) + ((3, 0, D),),))
    second = Gather(links, run, second_shard, 1)
    cot, cott = run(prepare, source, output_cotangent, segk, size, True)
    meet(run, first)
    first.step()
    while len(first.pending) < 2:
        meet(run, first)
        first.step()
    f1_shard, late_shard = run(
        pack,
        feed_shards,
        (triple(0, w1), tuple((n, lo, lo + w) for lo, w in ((w1, w2), (w1 + w2, w3)) for n in range(3))),
    )
    late = lax.all_gather(late_shard, AXES, axis=0, tiled=True)
    meet(run, second)
    second.step()
    strips = run(make_strips, offsets.reshape(HEADS // 2, 2, 2 * SEQ))
    meet(run, first)
    first.corner()
    while len(second.pending) < 2:
        meet(run, second)
        second.step()
    f1 = Gather(links, run, f1_shard, 2)
    meet(run, first)
    lead_blocks = first.end()
    layout0 = layout_of(lead_blocks, NATURAL, 3 * GROUP + BLK)
    qkv0, normed, turned, gains = run(project, x, lead_blocks, layout0, True)
    meet(run, second, f1)
    second.corner()
    f1.step()
    att0, lse0 = run(attn_fwd, spans, segk, segq, strips, qkv0, 0)
    meet(run, second, f1)
    next_blocks = second.end()
    f1.step()
    while len(f1.pending) < 2:
        meet(run, f1)
        f1.step()
    layout1 = layout_of(next_blocks, NATURAL, 3 * GROUP)
    layout_o = layout_of(next_blocks, NATURAL, D, 3 * GROUP)
    (qkv1,) = run(project, normed, next_blocks, layout1, False)
    meet(run, f1)
    f1.corner()
    att1, lse1 = run(attn_fwd, spans, segk, segq, strips, qkv1, 4)
    meet(run, f1)
    f1_blocks = f1.end()
    hidden, n2, n2t = run(hidden_units, att0, att1, x, gains, next_blocks, layout_o)
    acts = (n2, n2t, cot, cott)
    keep, send, bo, ng = run(feed, *acts, f1_blocks, w1, None, size, 0, NATURAL, NATURAL)
    s1 = Scatter(links, run, keep, send)
    meet(run, s1)
    s1.corner()
    keep, send, bo, ng = run(feed, *acts, (source, late), w2, (bo, ng), size, 0, None, NATURAL)
    meet(run, s1)
    s2 = Scatter(links, run, keep, send)
    s1.sides()
    meet(run, s2)
    s2.corner()
    keep, send, bo, ng = run(feed, *acts, (source, late), w3, (bo, ng), size, 3 * w2, None, NATURAL)
    meet(run, s1, s2)
    s3 = Scatter(links, run, keep, send)
    s2.sides()
    s1.step()
    meet(run, s3)
    s3.corner()
    hidden_grad, branch_t, attended_grad, second_term = run(middle, hidden, ng, cot, gains, next_blocks, layout_o)
    meet(run, s1)
    s1.step()

    def back_pairs(qkv, lse, first_pair):
        return run(attn_bwd, spans, segk, segq, strips, qkv, attended_grad, lse, first_pair)

    side = lambda a, b: [z for j in range(3) for z in (a[j], b[j])]
    g0 = back_pairs(qkv0, lse0, 0)
    meet(run, s1, s2)
    s2.step()
    g1 = back_pairs(qkv0, lse0, 2)
    meet(run, s2, s3)
    s3.sides()
    s2.step()
    keep, send = run(weight_terms, [(branch_t, [att0, att1]), (turned, side(g0, g1))], NATURAL)
    meet(run, s2)
    s4 = Scatter(links, run, keep, send)
    meet(run, s4)
    s4.corner()
    g2 = back_pairs(qkv1, lse1, 4)
    meet(run, s3)
    s3.step()
    g3 = back_pairs(qkv1, lse1, 6)
    meet(run, s3, s4)
    s4.sides()
    s3.step()
    keep, send = run(weight_terms, [(turned, side(g2, g3))], NATURAL)
    meet(run, s3)
    s5 = Scatter(links, run, keep, send)
    meet(run, s5)
    s5.corner()
    block_output = run(block_output_of, back, segk, hidden, bo, size)
    meet(run, s4, s5)
    s5.sides()
    s4.step()
    input_gradient, first_term = run(
        last, back, x, hidden_grad, gains, side(g0, g1) + side(g2, g3), lead_blocks + next_blocks,
        layout_of(lead_blocks, NATURAL, 3 * GROUP)
        + tuple((n + len(lead_blocks), *l) for n, *l in layout_of(next_blocks, NATURAL, 3 * GROUP, 0, 3 * GROUP)),
        size,
    )
    meet(run, s4, s5)
    s5.step()
    s4.step()
    gain_rows = run(natural_gains, back, first_term, second_term, size)
    offset_grads = jnp.concatenate([g[3] for g in (g0, g1, g2, g3)], axis=0).reshape(HEADS, 2 * SEQ)
    table_term = lax.dot_general(
        one_hot.astype(F32), offset_grads, (((0,), (1,)), ((), ())), precision=HIGHEST, preferred_element_type=F32
    )
    small = jnp.concatenate(
        [gain_rows, table_term.reshape(-1, BLK), jnp.zeros((4, BLK), F32)], axis=0
    )
    small = links.sum_all(small)
    gain_sums = small[:16].reshape(2, D)
    mine = lax.dynamic_slice_in_dim(gain_sums, me * size, size, 1)
    table_gradient = small[16:20].reshape(BUCKETS, HEADS)
    grads = finish([s.ends() for s in (s4, s5, s1, s2, s3)], size)
    return (block_output, input_gradient, *grads, mine[0], mine[1], table_gradient)


def solution(mesh):
    rows, flat, full = P(AXES, None), P(AXES), P()
    return jax.shard_map(
        functools.partial(on_device, Slice(mesh)),
        mesh=mesh,
        in_specs=(rows, flat, full, flat, rows, rows, rows, rows, full, flat, rows, rows, rows, rows),
        out_specs=(rows,) * 9 + (flat, flat, full),
        check_vma=False,
    )
```

```python
import functools

import jax
import jax.numpy as jnp
import numpy as np
from jax import lax
from jax.experimental import pallas as pl
from jax.experimental.pallas import tpu as pltpu
from jax.sharding import PartitionSpec as P

F32 = jnp.float32
BF = jnp.bfloat16
HEADS = 16
BUCKETS = 32
SEQ = 1024
D = 1024
FF = 2816
BLK = 128
NB = SEQ // BLK
STRIP = (2 * NB - 1) * BLK
EPS = 1e-06
NEG = -1e30
VLIM = 60 * 1024 * 1024
AXES = ("dp", "fsdp")
GROUP = 512
PIECES = (768, 1024, 1024)
TILE = 512
FT = 256
ANY = pl.BlockSpec(memory_space=pl.ANY)
SMEM = pl.BlockSpec(memory_space=pltpu.SMEM)
HIGHEST = lax.Precision.HIGHEST
RATE = 2e7
GELU_A = 0.7978845608028654
GELU_B = 0.044715


def params(grid=1):
    return pltpu.CompilerParams(vmem_limit_bytes=VLIM, dimension_semantics=("arbitrary",) * grid)


def cost(flops, moved, trans=0):
    return pl.CostEstimate(flops=int(flops), bytes_accessed=int(moved / 50), transcendentals=int(trans))


def after(kernel, used, deps):
    if not deps:
        return kernel
    return lambda *refs: kernel(*refs[:used], *refs[used + len(deps) :])


def nt(a,b): return lax.dot_general(a,b,(((1,),(1,)),((),())),preferred_element_type=F32)
def nn(a,b): return lax.dot_general(a,b,(((1,),(0,)),((),())),preferred_element_type=F32)

def build_strip(rev_ref, strip):
    for h in range(2):
        row=jnp.broadcast_to(rev_ref[h:h+1,:],(8,2*SEQ))
        base=pltpu.roll(row,0,1,stride=1,stride_axis=0)
        for m in range(BLK//8):
            turned=pltpu.roll(base,(8*m-(BLK-1))%(2*SEQ),1)
            for d in range(2*NB-1):
                e=2*NB-2-d
                strip[d*BLK+8*m:d*BLK+8*m+8,h*BLK:(h+1)*BLK]=turned[:,e*BLK:(e+1)*BLK]

def fold_strip(strip, out_ref):
    for h in range(2):
        total=jnp.zeros((8,2*SEQ),F32)
        for m in range(BLK//8):
            parts=[strip[(2*NB-2-e)*BLK+8*m:(2*NB-2-e)*BLK+8*m+8,h*BLK:(h+1)*BLK] for e in range(2*NB-1)]
            parts.append(jnp.zeros((8,BLK),F32))
            total=total+pltpu.roll(jnp.concatenate(parts,axis=1),(BLK-1-8*m)%(2*SEQ),1)
        row=total[0:1]
        for s in range(1,8):
            row=row+pltpu.roll(total[s:s+1],2*SEQ-s,1)
        out_ref[h:h+1,:]=row

def lanes_mask():
    lane=lax.broadcasted_iota(jnp.int32,(1,BLK),1)
    return lane<64

def stack_heads(x, first):
    zero=jnp.zeros_like(x)
    return jnp.concatenate([jnp.where(first,x,zero),jnp.where(first,zero,x)],axis=0)


def strip_kernel(rev_ref, strip):
    build_strip(rev_ref, strip)

def make_strips(rev, deps=()):
    return pl.pallas_call(after(strip_kernel, 1, deps),grid=(8,),
        in_specs=[pl.BlockSpec((None,2,2*SEQ),lambda p:(p,0,0))]+[ANY]*len(deps),
        out_specs=pl.BlockSpec((None,STRIP,2*BLK),lambda p:(p,0,0)),
        out_shape=jax.ShapeDtypeStruct((8,STRIP,2*BLK),F32),
        compiler_params=pltpu.CompilerParams(vmem_limit_bytes=VLIM),
        name="bias_strips")(rev, *deps)

def attn_fwd_kernel(UNIT, rng_ref, segk_ref, segq_ref, strip, q_ref, k_ref, v_ref, o_ref, lse_ref, vt):
    first=lanes_mask()
    for u in range(UNIT):
        vt[u]=v_ref[:,u*BLK:(u+1)*BLK].T
    mean=jnp.sum(v_ref[...].astype(F32),axis=0,keepdims=True)*(1.0/SEQ)

    def block(qi, carry):
        q0=pl.multiple_of(qi*BLK,BLK)
        lo=rng_ref[qi]; width=rng_ref[NB+qi]
        k0=pl.multiple_of(lo*BLK,BLK)
        b0=pl.multiple_of((lo-qi+NB-1)*BLK,BLK)
        segq=segq_ref[pl.ds(qi,1),:]
        @pl.when(width==0)
        def _():
            o_ref[pl.ds(q0,BLK),:]=jnp.broadcast_to(mean,(BLK,UNIT*BLK)).astype(BF)
            for u in range(UNIT):
                lse_ref[u,pl.ds(qi,1),:]=jnp.zeros((1,2*BLK),F32)
        for w in range(1,NB+1):
            @pl.when(width==w)
            def _():
                rows=w*BLK
                allowed=segk_ref[pl.ds(k0,rows),:]==segq
                live_row=segq>0
                live_row=jnp.concatenate([live_row,live_row],axis=1)
                live_col=segk_ref[pl.ds(q0,BLK),:]>0
                units=[slice(u*BLK,(u+1)*BLK) for u in range(UNIT)]
                qcats=[stack_heads(q_ref[pl.ds(q0,BLK),lanes],first) for lanes in units]
                scores=[nt(k_ref[pl.ds(k0,rows),lanes],qcat) for lanes,qcat in zip(units,qcats)]
                probs=[]; stats=[]; totals=[]
                for u in range(UNIT):
                    both=[]; stat=[]; tot=[]
                    s=scores[u]+strip[u,pl.ds(b0,rows),:]
                    for h in range(2):
                        sh=jnp.where(allowed,s[:,h*BLK:(h+1)*BLK],NEG)
                        peak=jnp.max(sh,axis=0,keepdims=True)
                        e=jnp.exp(sh-peak)
                        t=jnp.sum(e,axis=0,keepdims=True)
                        both.append(e.astype(BF)); stat.append(peak+jnp.log(t)); tot.append(t)
                    probs.append(jnp.concatenate(both,axis=1)); stats.append(jnp.concatenate(stat,axis=1)); totals.append(jnp.concatenate(tot,axis=1))
                ots=[nn(vt[u,:,pl.ds(k0,rows)],probs[u]) for u in range(UNIT)]
                for u,lanes in enumerate(units):
                    ot=ots[u]*(1.0/totals[u])
                    o=jnp.concatenate([ot[:64,:BLK],ot[64:,BLK:]],axis=0).T
                    o_ref[pl.ds(q0,BLK),lanes]=jnp.where(live_col,o,mean[:,lanes]).astype(BF)
                    lse_ref[u,pl.ds(qi,1),:]=jnp.where(live_row,stats[u],0.0)
        return carry
    lax.fori_loop(0,NB,block,0)

def attn_bwd_kernel(UNIT, rng_ref, segk_ref, segq_ref, strip, q_ref, k_ref, v_ref, g_ref, lse_ref,
                    dq_ref, dk_ref, dv_ref, off_ref, dstrip, kt, dk, dv):
    first=lanes_mask()
    dstrip[...]=jnp.zeros_like(dstrip)
    dk[...]=jnp.zeros_like(dk)
    for u in range(UNIT):
        lanes=slice(u*BLK,(u+1)*BLK)
        kt[u]=k_ref[:,lanes].T
        padded=jnp.where(segk_ref[...]>0,0.0,g_ref[:,lanes].astype(F32))
        dv[:,lanes]=jnp.broadcast_to(jnp.sum(padded,axis=0,keepdims=True)*(1.0/SEQ),(SEQ,BLK))

    def block(qi, carry):
        q0=pl.multiple_of(qi*BLK,BLK)
        lo=rng_ref[qi]; width=rng_ref[NB+qi]
        k0=pl.multiple_of(lo*BLK,BLK)
        b0=pl.multiple_of((lo-qi+NB-1)*BLK,BLK)
        segq=segq_ref[pl.ds(qi,1),:]
        @pl.when(width==0)
        def _():
            dq_ref[pl.ds(q0,BLK),:]=jnp.zeros((BLK,UNIT*BLK),BF)
        for w in range(1,NB+1):
            @pl.when(width==w)
            def _():
                rows=w*BLK
                allowed=segk_ref[pl.ds(k0,rows),:]==segq
                units=[slice(u*BLK,(u+1)*BLK) for u in range(UNIT)]
                qcats=[stack_heads(q_ref[pl.ds(q0,BLK),lanes],first) for lanes in units]
                gcats=[stack_heads(g_ref[pl.ds(q0,BLK),lanes],first) for lanes in units]
                scores=[nt(k_ref[pl.ds(k0,rows),lanes],qcat) for lanes,qcat in zip(units,qcats)]
                dps=[nt(v_ref[pl.ds(k0,rows),lanes],gcat) for lanes,gcat in zip(units,gcats)]
                probs=[]; grads=[]
                for u in range(UNIT):
                    lse=lse_ref[u,pl.ds(qi,1),:]
                    s=scores[u]+strip[u,pl.ds(b0,rows),:]
                    ps=[]; ds=[]
                    for h in range(2):
                        cols=slice(h*BLK,(h+1)*BLK)
                        prob=jnp.exp(jnp.where(allowed,s[:,cols],NEG)-lse[:,cols])
                        t=prob*dps[u][:,cols]
                        inner=jnp.sum(t,axis=0,keepdims=True)
                        d=t-prob*inner
                        dstrip[u,pl.ds(b0,rows),cols]+=d
                        ps.append(prob.astype(BF)); ds.append(d.astype(BF))
                    probs.append(jnp.concatenate(ps,axis=1)); grads.append(jnp.concatenate(ds,axis=1))
                for u,lanes in enumerate(units):
                    dv[pl.ds(k0,rows),lanes]+=nn(probs[u],gcats[u])
                dqts=[nn(kt[u,:,pl.ds(k0,rows)],grads[u]) for u in range(UNIT)]
                for u,lanes in enumerate(units):
                    dk[pl.ds(k0,rows),lanes]+=nn(grads[u],qcats[u])
                for u,lanes in enumerate(units):
                    dq_ref[pl.ds(q0,BLK),lanes]=jnp.concatenate([dqts[u][:64,:BLK],dqts[u][64:,BLK:]],axis=0).T.astype(BF)
        return carry
    lax.fori_loop(0,NB,block,0)
    dk_ref[...]=dk[...].astype(BF)
    dv_ref[...]=dv[...].astype(BF)
    for u in range(UNIT):
        fold_strip(dstrip.at[u], off_ref.at[u])

def attn_fwd(rng, segk, segq, strips, qkv, first_pair, deps=()):
    unit = 4
    wide = unit * BLK
    c = lambda o: pl.BlockSpec((SEQ, wide), lambda p, r: (0, o))
    gs = pltpu.PrefetchScalarGridSpec(
        num_scalar_prefetch=1,
        grid=(1,),
        in_specs=[
            pl.BlockSpec((SEQ, BLK), lambda p, r: (0, 0)),
            pl.BlockSpec((NB, BLK), lambda p, r: (0, 0)),
            pl.BlockSpec((unit, STRIP, 2 * BLK), lambda p, r: (first_pair // unit, 0, 0)),
            c(0), c(1), c(2),
        ] + [ANY] * len(deps),
        out_specs=[c(0), pl.BlockSpec((unit, NB, 2 * BLK), lambda p, r: (0, 0, 0))],
        scratch_shapes=[pltpu.VMEM((unit, BLK, SEQ), BF)],
    )
    return pl.pallas_call(
        after(functools.partial(attn_fwd_kernel, unit), 7, deps),
        grid_spec=gs,
        out_shape=[jax.ShapeDtypeStruct((SEQ, wide), BF), jax.ShapeDtypeStruct((unit, NB, 2 * BLK), F32)],
        compiler_params=params(),
        cost_estimate=cost(13 * RATE, 4 * SEQ * wide * 2),
        name="attention_forward",
    )(rng, segk, segq, strips, qkv, qkv, qkv, *deps)


def attn_bwd(rng, segk, segq, strips, qkv, g, lse, first_pair):
    unit, steps = 2, 2
    wide = unit * BLK
    f = first_pair // unit
    c = lambda o: pl.BlockSpec((SEQ, wide), lambda p, r: (0, o + p))
    gs = pltpu.PrefetchScalarGridSpec(
        num_scalar_prefetch=1,
        grid=(steps,),
        in_specs=[
            pl.BlockSpec((SEQ, BLK), lambda p, r: (0, 0)),
            pl.BlockSpec((NB, BLK), lambda p, r: (0, 0)),
            pl.BlockSpec((unit, STRIP, 2 * BLK), lambda p, r: (f + p, 0, 0)),
            c(0), c(steps), c(2 * steps), c(f),
            pl.BlockSpec((unit, NB, 2 * BLK), lambda p, r: (p, 0, 0)),
        ],
        out_specs=[c(0), c(0), c(0), pl.BlockSpec((unit, 2, 2 * SEQ), lambda p, r: (p, 0, 0))],
        scratch_shapes=[
            pltpu.VMEM((unit, STRIP, 2 * BLK), F32), pltpu.VMEM((unit, BLK, SEQ), BF),
            pltpu.VMEM((SEQ, wide), F32), pltpu.VMEM((SEQ, wide), F32),
        ],
    )
    sh = jax.ShapeDtypeStruct((SEQ, steps * wide), BF)
    return pl.pallas_call(
        functools.partial(attn_bwd_kernel, unit),
        grid_spec=gs,
        out_shape=[sh, sh, sh, jax.ShapeDtypeStruct((steps * unit, 2, 2 * SEQ), F32)],
        compiler_params=params(),
        cost_estimate=cost(24 * RATE, 16 * SEQ * wide * 2),
        name="attention_backward",
    )(rng, segk, segq, strips, qkv, qkv, qkv, g, lse)


def ranges(seg):
    s=seg.reshape(NB,BLK)
    least=s[:,0]; most=jnp.max(s,axis=1)
    lo=jnp.sum((most[None,:]<least[:,None])&(least[None,:]>0),axis=1)
    hi=jnp.sum((least[None,:]<=most[:,None])&(least[None,:]>0),axis=1)
    w=jnp.where(least>0,hi-lo,0)
    return jnp.concatenate([jnp.where(least>0,lo,0),w]).astype(jnp.int32)


def prep_kernel(c_ref, seg_ref, out_ref, turned_ref):
    low = jnp.where(jnp.concatenate([seg_ref[...] > 0] * (D // BLK), axis=1), c_ref[...].astype(F32), 0.0).astype(BF)
    out_ref[...] = low
    turned_ref[...] = low.T


def prepare(c, segk):
    rows = 256
    blk = pl.BlockSpec((rows, D), lambda i: (i, 0))
    return pl.pallas_call(
        prep_kernel,
        grid=(SEQ // rows,),
        in_specs=[blk, pl.BlockSpec((rows, BLK), lambda i: (i, 0))],
        out_specs=[blk, pl.BlockSpec((D, rows), lambda i: (0, i))],
        out_shape=[jax.ShapeDtypeStruct((SEQ, D), BF), jax.ShapeDtypeStruct((D, SEQ), BF)],
        compiler_params=params(),
        cost_estimate=cost(4 * RATE, 6 * SEQ * D),
        name="prepare",
    )(c, segk)


def pack_kernel(spans, count, *refs):
    ins, outs = refs[:count], refs[count:]
    for out, cols in zip(outs, spans):
        at = 0
        for n, lo, hi in cols:
            out[:, at : at + hi - lo] = ins[n][:, lo:hi]
            at += hi - lo


def pack(shards, spans, deps=()):
    rows = shards[0].shape[0]
    widths = [sum(hi - lo for _, lo, hi in cols) for cols in spans]
    whole = pl.BlockSpec(memory_space=pltpu.VMEM)
    return pl.pallas_call(
        after(functools.partial(pack_kernel, spans, len(shards)), len(shards), deps),
        in_specs=[whole] * len(shards) + [ANY] * len(deps),
        out_specs=[whole] * len(widths),
        out_shape=[jax.ShapeDtypeStruct((rows, w), BF) for w in widths],
        name="pack_shards",
    )(*shards, *deps)


def join(*parts):
    return jnp.concatenate(parts, axis=0)


def add_terms(terms, rows):
    return sum(t[off : off + rows].astype(F32) for t, off in terms).astype(BF)


def finish_kernel(counts, *refs):
    sums, at = [], 0
    for n in counts:
        total = refs[at][...].astype(F32)
        for ref in refs[at + 1 : at + n]:
            total = total + ref[...].astype(F32)
        sums.append(total)
        at += n
    outs = refs[at:]
    for j in range(3):
        outs[j][:, :GROUP] = sums[0][:, D + j * GROUP : D + (j + 1) * GROUP]
        outs[j][:, GROUP:] = sums[1][:, j * GROUP : (j + 1) * GROUP]
    outs[3][...] = sums[0][:, :D]
    at = 0
    for s, width in zip(sums[2:], PIECES):
        for j in range(3):
            outs[4 + j][:, at : at + width] = s[:, j * width : (j + 1) * width]
        at += width


def finish(sets, rows, deps=()):
    flat = [x for terms in sets for x in terms]
    widths = (D,) * 4 + (FF,) * 3
    return pl.pallas_call(
        after(functools.partial(finish_kernel, tuple(len(t) for t in sets)), len(flat), deps),
        grid=(1,),
        in_specs=[pl.BlockSpec((rows, x.shape[1]), lambda i: (0, 0)) for x in flat] + [ANY] * len(deps),
        out_specs=[pl.BlockSpec((rows, w), lambda i: (0, 0)) for w in widths],
        out_shape=[jax.ShapeDtypeStruct((rows, w), F32) for w in widths],
        compiler_params=params(),
        name="weight_gradients",
    )(*flat, *deps)


def place_blocks(source_ref, blocks, start, cols, dst, at, sem):
    rows = blocks[0].shape[0]
    size = D // source_ref.shape[0]
    per = rows // size
    for n, ref in enumerate(blocks):

        def one(i, carry):
            row = pl.multiple_of(source_ref[n * per + i] * size, size)
            pltpu.make_async_copy(
                ref.at[pl.ds(pl.multiple_of(i * size, size), size), pl.ds(start, cols)],
                dst.at[pl.ds(row, size), pl.ds(at, cols)],
                sem,
            ).start()
            return carry

        lax.fori_loop(0, per, one, 0)


def wait_whole(dst, sem):
    pltpu.make_async_copy(dst, dst, sem).wait()


def order_rows(source_ref, src, dst, sem):
    size = D // source_ref.shape[0]

    def one(p, carry):
        row = pl.multiple_of(source_ref[p] * size, size)
        pltpu.make_async_copy(
            src.at[pl.ds(row, size)], dst.at[pl.ds(pl.multiple_of(p * size, size), size)], sem
        ).start()
        return carry

    lax.fori_loop(0, D // size, one, 0)


def scaled_rows(x):
    return lax.rsqrt(jnp.mean(x * x, axis=-1, keepdims=True) + EPS)


def qkv_kernel(lead, *refs):
    source, x_ref, blocks, refs = refs[0], refs[1], refs[2:10], refs[10:]
    if lead:
        out_ref, normed_ref, turned_ref, gains_ref, w, sem = refs
    else:
        out_ref, w, sem = refs
        normed_ref = x_ref
    j = pl.program_id(0)

    @pl.when(j == 0)
    def _():
        place_blocks(source, blocks, 0, w.shape[1], w, 0, sem.at[0])
        wait_whole(w, sem.at[0])
        if lead:
            gains_ref[...] = w[:, 3 * GROUP :].astype(F32).T[:8]

            def rows_of(i, carry):
                at = pl.multiple_of(i * 256, 256)
                x = x_ref[pl.ds(at, 256), :].astype(F32)
                low = (x * scaled_rows(x) * gains_ref[0:1, :]).astype(BF)
                normed_ref[pl.ds(at, 256), :] = low
                turned_ref[:, pl.ds(at, 256)] = low.T
                return carry

            lax.fori_loop(0, SEQ // 256, rows_of, 0)

    out_ref[...] = nn(normed_ref[...], w[:, pl.ds(pl.multiple_of(j * GROUP, GROUP), GROUP)]).astype(BF)


def project(source, x, blocks, lead):
    width = 3 * GROUP + (BLK if lead else 0)
    whole = lambda r, c: pl.BlockSpec((r, c), lambda j: (0, 0))
    out_specs = [pl.BlockSpec((SEQ, GROUP), lambda j: (0, j))]
    out_shape = [jax.ShapeDtypeStruct((SEQ, 3 * GROUP), BF)]
    if lead:
        out_specs += [whole(SEQ, D), whole(D, SEQ), whole(8, D)]
        out_shape += [
            jax.ShapeDtypeStruct((SEQ, D), BF),
            jax.ShapeDtypeStruct((D, SEQ), BF),
            jax.ShapeDtypeStruct((8, D), F32),
        ]
    return pl.pallas_call(
        functools.partial(qkv_kernel, lead),
        grid=(3,),
        in_specs=[SMEM, whole(SEQ, D)] + [ANY] * len(blocks),
        out_specs=out_specs,
        out_shape=out_shape,
        scratch_shapes=[pltpu.VMEM((D, width), BF), pltpu.SemaphoreType.DMA((1,))],
        compiler_params=params(),
        cost_estimate=cost(6 * RATE, 2 * D * width + 4 * SEQ * D),
        name="query_key_value",
    )(source, x, *blocks)


def hidden_kernel(*refs):
    source, a0, a1, x_ref, gains_ref = refs[:5]
    h_ref, n2_ref, n2t_ref, w, sem = refs[13:]

    @pl.when(pl.program_id(0) == 0)
    def _():
        place_blocks(source, refs[5:13], 3 * GROUP, D, w, 0, sem.at[0])
        wait_whole(w, sem.at[0])

    hidden = x_ref[...].astype(F32) + nt(jnp.concatenate([a0[...], a1[...]], axis=1), w[...])
    h_ref[...] = hidden
    normed = (hidden * scaled_rows(hidden) * gains_ref[1:2, :]).astype(BF)
    n2_ref[...] = normed
    n2t_ref[...] = normed.T


def hidden_units(source, a0, a1, x, gains, blocks):
    rows = TILE
    tok = lambda c: pl.BlockSpec((rows, c), lambda i: (i, 0))
    return pl.pallas_call(
        hidden_kernel,
        grid=(SEQ // rows,),
        in_specs=[SMEM, tok(GROUP), tok(GROUP), tok(D), pl.BlockSpec((8, D), lambda i: (0, 0))] + [ANY] * len(blocks),
        out_specs=[tok(D), tok(D), pl.BlockSpec((D, rows), lambda i: (0, i))],
        out_shape=[
            jax.ShapeDtypeStruct((SEQ, D), F32),
            jax.ShapeDtypeStruct((SEQ, D), BF),
            jax.ShapeDtypeStruct((D, SEQ), BF),
        ],
        scratch_shapes=[pltpu.VMEM((D, D), BF), pltpu.SemaphoreType.DMA((1,))],
        compiler_params=params(),
        cost_estimate=cost(6 * RATE, 16 * SEQ * D),
        name="hidden_units",
    )(source, a0, a1, x, gains, *blocks)


def feed_kernel(lead, final, width, base, *refs):
    source, n2, n2t, cot, cott, whole = refs[:6]
    refs = refs[6:]
    sums_from = () if lead else refs[:2]
    refs = refs[len(sums_from) :]
    if final:
        h_in, gains_ref, seg_in, blocks, refs = refs[0], refs[1], refs[2], refs[3:11], refs[11:]
    keep, send = refs[:2]
    outs, refs = (refs[2:7], refs[7:]) if final else (refs[2:4], refs[4:])
    n2_v, n2t_v, cot_v, cott_v, w, stage, bo, ng, mix_v, gu_v, sem_w, sem_o, sem_i = refs[:13]
    half = D // 2
    tiles = width // FT

    def weight_copies(f):
        out = []
        for j in range(3):
            col = pl.multiple_of(j * width + f * FT, FT)
            out.append(
                pltpu.make_async_copy(
                    whole.at[:, pl.ds(pl.multiple_of(base + col, BLK), FT)], w.at[:, pl.ds(col, FT)], sem_w.at[f, j]
                )
            )
        return out

    def term_copies(g):
        col = pl.multiple_of(g * FT, FT)
        return [
            pltpu.make_async_copy(
                stage.at[pl.ds(s * half, half), pl.ds(col, FT)], dst.at[:, pl.ds(col, FT)], sem_o.at[g, s]
            )
            for s, dst in enumerate((keep, send))
        ]

    first = [pltpu.make_async_copy(n2, n2_v, sem_i.at[0]), pltpu.make_async_copy(cot, cot_v, sem_i.at[1])]
    sums_in = [pltpu.make_async_copy(a, b, sem_i.at[4 + n]) for n, (a, b) in enumerate(zip(sums_from, (bo, ng)))]
    if final:
        h_v, wo, ag_v, bt_v, out_v, gain_v, seg_v = refs[13:]
        sums_in += [pltpu.make_async_copy(h_in, h_v, sem_i.at[6]), pltpu.make_async_copy(seg_in, seg_v, sem_i.at[7])]
        sources = (out_v, ng, bt_v, ag_v, gain_v)
    else:
        sources = (bo, ng)
    results = [pltpu.make_async_copy(a, b, sem_i.at[8 + n]) for n, (a, b) in enumerate(zip(sources, outs))]
    for c in weight_copies(0) + first:
        c.start()
    for f in range(1, tiles):
        for c in weight_copies(f):
            c.start()
    for c in sums_in:
        c.start()
    for c in first:
        c.wait()

    def units(f, carry):
        for c in weight_copies(f):
            c.wait()
        at = [pl.ds(pl.multiple_of(j * width + f * FT, FT), FT) for j in range(3)]

        def tokens(i, inner):
            rows = pl.ds(pl.multiple_of(i * TILE, TILE), TILE)
            n = n2_v[rows, :]
            gate = nn(n, w[:, at[0]])
            upward = nn(n, w[:, at[1]])
            mixed_grad = nn(cot_v[rows, :], w[:, at[2]])
            square = gate * gate
            bend = jnp.tanh(gate * (GELU_A + (GELU_A * GELU_B) * square))
            curve = 0.5 * (1.0 + bend)
            active = gate * curve
            slope = curve + (0.5 * gate) * (1.0 - bend * bend) * (GELU_A + (3.0 * GELU_A * GELU_B) * square)
            mix_v[rows, at[0]] = (active * upward).astype(BF)
            gu_v[rows, at[0]] = (mixed_grad * upward * slope).astype(BF)
            gu_v[rows, at[1]] = (mixed_grad * active).astype(BF)
            return inner

        for i in range(SEQ // TILE):
            tokens(i, 0)
        return carry

    lax.fori_loop(0, tiles, units, 0)
    order_rows(source, n2t, n2t_v, sem_i.at[2])
    order_rows(source, cott, cott_v, sem_i.at[3])
    if final:
        place_blocks(source, blocks, 3 * GROUP, D, wo, 0, sem_i.at[13])
    for c in sums_in:
        c.wait()

    def sums(i, carry):
        rows = pl.ds(pl.multiple_of(i * TILE, TILE), TILE)
        for j in range(2):
            cols = slice(j * TILE, (j + 1) * TILE)
            one = nt(mix_v[rows, :], w[cols, 2 * width :])
            two = nt(gu_v[rows, :], w[cols, : 2 * width])
            bo[rows, cols] = one if lead else bo[rows, cols] + one
            ng[rows, cols] = two if lead else ng[rows, cols] + two
        return carry

    lax.fori_loop(0, SEQ // TILE, sums, 0)
    if final:
        wait_whole(wo, sem_i.at[13])
        gain_v[...] = jnp.zeros_like(gain_v)

        def close(i, carry):
            rows = pl.ds(pl.multiple_of(i * 256, 256), 256)
            hidden = h_v[rows, :]
            live = jnp.concatenate([seg_v[rows, :] > 0] * (D // BLK), axis=1)
            out_v[rows, :] = jnp.where(live, hidden + bo[rows, :], 0.0).astype(BF)
            grad = ng[rows, :]
            scale = scaled_rows(hidden)
            gain_v[0:1, :] += jnp.sum(grad * hidden * scale, axis=0, keepdims=True)
            grad = grad * gains_ref[1:2, :]
            mean = jnp.mean(grad * hidden, axis=-1, keepdims=True)
            out = cot_v[rows, :].astype(F32) + (scale * grad - hidden * (scale * scale * scale * mean))
            ng[rows, :] = out
            low = out.astype(BF)
            mix_low[rows, :] = low
            bt_v[:, rows] = low.T
            return carry

        mix_low = n2_v
        lax.fori_loop(0, SEQ // 256, close, 0)

        def attended(i, carry):
            cols = pl.ds(pl.multiple_of(i * FT, FT), FT)
            ag_v[:, cols] = nn(mix_low[...], wo[:, cols]).astype(BF)
            return carry

        lax.fori_loop(0, D // FT, attended, 0)
    for c in results:
        c.start()
    wait_whole(n2t_v, sem_i.at[2])
    wait_whole(cott_v, sem_i.at[3])

    def terms(left, right, start):
        def one(f, carry):
            cols = pl.ds(pl.multiple_of(f * FT, FT), FT)
            out = pl.ds(pl.multiple_of(start * FT + f * FT, FT), FT)
            stage[:, out] = nn(left[...], right[:, cols]).astype(BF)
            for c in term_copies(start + f):
                c.start()
            return carry

        return one

    lax.fori_loop(0, 2 * tiles, terms(n2t_v, gu_v, 0), 0)
    lax.fori_loop(0, tiles, terms(cott_v, mix_v, 2 * tiles), 0)
    for c in results:
        c.wait()

    def drain(g, carry):
        for c in term_copies(g):
            c.wait()
        return carry

    lax.fori_loop(0, 3 * tiles, drain, 0)


def feed(source, acts, whole, base, width, sums, closing=None):
    lead, final = sums is None, closing is not None
    tiles = width // FT
    args = [source, *acts, whole] + ([] if lead else list(sums))
    specs = [SMEM] + [ANY] * (len(args) - 1)
    if final:
        hidden, gains, segk, blocks = closing
        args += [hidden, gains, segk, *blocks]
        specs += [ANY, pl.BlockSpec(memory_space=pltpu.VMEM), ANY] + [ANY] * len(blocks)
    half = jax.ShapeDtypeStruct((D // 2, 3 * width), BF)
    shape = lambda t, *s: jax.ShapeDtypeStruct(s, t)
    total = shape(F32, SEQ, D)
    outs = [shape(BF, SEQ, D), total, shape(BF, D, SEQ), shape(BF, SEQ, D), shape(F32, 8, D)] if final else [total, total]
    bf = lambda *s: pltpu.VMEM(s, BF)
    scratch = [
        bf(SEQ, D), bf(D, SEQ), bf(SEQ, D), bf(D, SEQ), bf(D, 3 * width), bf(D, 3 * width),
        pltpu.VMEM((SEQ, D), F32), pltpu.VMEM((SEQ, D), F32),
        bf(SEQ, width), bf(SEQ, 2 * width),
        pltpu.SemaphoreType.DMA((tiles, 3)), pltpu.SemaphoreType.DMA((3 * tiles, 2)), pltpu.SemaphoreType.DMA((14,)),
    ]
    if final:
        scratch += [
            pltpu.VMEM((SEQ, D), F32), bf(D, D), bf(SEQ, D), bf(D, SEQ), bf(SEQ, D),
            pltpu.VMEM((8, D), F32), pltpu.VMEM((SEQ, BLK), jnp.int32),
        ]
    return pl.pallas_call(
        functools.partial(feed_kernel, lead, final, width, base),
        in_specs=specs,
        out_specs=[ANY] * (2 + len(outs)),
        out_shape=[half, half] + outs,
        scratch_shapes=scratch,
        compiler_params=pltpu.CompilerParams(vmem_limit_bytes=VLIM),
        cost_estimate=cost((30 * width / 1024 + (6 if final else 0)) * RATE, 12 * D * width + 24 * SEQ * D, SEQ * width),
        name="feed_forward",
    )(*args)


def terms_kernel(counts, *refs):
    source, lefts, rights = refs[0], refs[1 : 1 + len(counts)], refs[1 + len(counts) : 1 + len(counts) + sum(counts)]
    keep, send, held, sem = refs[1 + len(counts) + sum(counts) :]
    half = D // 2

    @pl.when(pl.program_id(0) == 0)
    def _():
        for n, left in enumerate(lefts):
            order_rows(source, left, held.at[n], sem.at[n])
        for n in range(len(lefts)):
            wait_whole(held.at[n], sem.at[n])

    def work(out, rows):
        at, r = 0, 0
        for n, count in enumerate(counts):
            for right in rights[r : r + count]:
                wide = right.shape[1]
                out[:, at : at + wide] = nn(held[n, rows, :], right[...]).astype(BF)
                at += wide
            r += count

    pl.when(pl.program_id(0) == 0)(lambda: work(send, slice(half, None)))
    pl.when(pl.program_id(0) == 1)(lambda: work(keep, slice(0, half)))


def weight_terms(source, sets):
    lefts = [t[0] for t in sets]
    rights = [r for t in sets for r in t[1]]
    counts = tuple(len(t[1]) for t in sets)
    width = sum(r.shape[1] for r in rights)
    half = D // 2
    sh = jax.ShapeDtypeStruct((half, width), BF)
    out = pl.BlockSpec((half, width), lambda i: (0, 0))
    return pl.pallas_call(
        functools.partial(terms_kernel, counts),
        grid=(2,),
        in_specs=[SMEM] + [ANY] * len(lefts) + [pl.BlockSpec(r.shape, lambda i: (0, 0)) for r in rights],
        out_specs=[out, out],
        out_shape=[sh, sh],
        scratch_shapes=[pltpu.VMEM((len(lefts), D, SEQ), BF), pltpu.SemaphoreType.DMA((len(lefts),))],
        compiler_params=params(),
        cost_estimate=cost(4 * RATE * width / 1536, 4 * SEQ * D + 4 * D * width),
        name="weight_terms",
    )(source, *lefts, *rights)


def last_kernel(count, part, *refs):
    source, x_ref, hg_ref, gains_ref = refs[:4]
    grads = refs[4 : 4 + count]
    blocks = refs[4 + count : 20 + count]
    out_ref, gain_ref, w, sem = refs[-4:]
    half = 3 * GROUP
    for n in range(2):
        place_blocks(source, blocks[8 * n : 8 * n + 8], 0, half, w, n * half, sem.at[n])
    for n in range(2):
        wait_whole(w.at[:, pl.ds(n * half, half)], sem.at[n])
    grad = nt(jnp.concatenate([g[...] for g in grads], axis=1), w[...])
    x = x_ref[...].astype(F32)
    scale = scaled_rows(x)
    gain_ref[...] = jnp.broadcast_to(jnp.sum(grad * x * scale, axis=0, keepdims=True), gain_ref.shape)
    grad = grad * gains_ref[0:1, :]
    mean = jnp.mean(grad * x, axis=-1, keepdims=True)
    out_ref[...] = hg_ref[...] + (scale * grad - x * (scale * scale * scale * mean))


def last(source, x, hg, gains, grads, blocks, part, so_far=None):
    rows = SEQ // 2
    tok = lambda c: pl.BlockSpec((rows, c), lambda i: (part, 0))
    whole = pl.BlockSpec((8, D), lambda i: (0, 0))
    args = [source, x, hg, gains, *grads, *blocks] + ([] if so_far is None else [so_far])
    return pl.pallas_call(
        functools.partial(last_kernel, len(grads), part),
        grid=(1,),
        in_specs=[SMEM, tok(D), tok(D), whole] + [tok(g.shape[1]) for g in grads]
        + [ANY] * (len(args) - 4 - len(grads)),
        out_specs=[tok(D), whole],
        out_shape=[jax.ShapeDtypeStruct((SEQ, D), F32), jax.ShapeDtypeStruct((8, D), F32)],
        scratch_shapes=[pltpu.VMEM((D, 6 * GROUP), BF), pltpu.SemaphoreType.DMA((2,))],
        input_output_aliases={} if so_far is None else {len(args) - 1: 0},
        compiler_params=params(),
        cost_estimate=cost(7 * RATE, 14 * SEQ * D),
        name="input_gradient",
    )(*args)


class Slice:
    def __init__(self, mesh):
        self.count = mesh.shape["dp"] * mesh.shape["fsdp"]
        self.inner = mesh.shape["fsdp"]
        self.core = self.inner
        bits = [1 << b for b in range(self.count.bit_length() - 1)]
        self.rest = [b for b in reversed(bits) if b not in (1, 2, self.core)]
        self.order = [self.core, 2, 1] + self.rest[::-1]
        self.size = D // self.count

    def place(self, index):
        p = index * 0
        for b in self.order:
            p = 2 * p + (index // b) % 2
        return p

    def swap(self, x, bit):
        return lax.ppermute(x, AXES, [(i, i ^ bit) for i in range(self.count)])

    @staticmethod
    def masks(bits):
        return [sum(b for j, b in enumerate(bits) if n >> j & 1) for n in range(1, 1 << len(bits))]


class Order:
    def __init__(self):
        self.token = None

    def hold(self, args):
        leaves, tree = jax.tree.flatten(args)
        at = [i for i, x in enumerate(leaves) if hasattr(x, "aval")]
        if self.token is not None:
            held = lax.optimization_barrier([leaves[i] for i in at] + [self.token])
            for i, x in zip(at, held):
                leaves[i] = x
        return jax.tree.unflatten(tree, leaves)

    def __call__(self, f, *args):
        out = f(*self.hold(args))
        self.token = jax.tree.leaves(out)[0]
        return out


class Chain:
    def __init__(self, links, run):
        self.links, self.run, self.pending = links, run, []


def meet(run, *chains):
    arrays = run.hold([c.pending for c in chains] + [run.token])
    run.token = arrays.pop()
    for c, got in zip(chains, arrays):
        c.met(got)
        c.pending = []


class Gather(Chain):
    def __init__(self, links, run, shard):
        super().__init__(links, run)
        self.line = run.hold(shard)
        self.pending = [links.swap(self.line, m) for m in links.masks(links.rest)]

    def met(self, got):
        self.got = got

    def square(self):
        self.line = self.run(join, self.line, *self.got)
        self.others = [self.links.swap(self.line, self.links.core)]
        self.pending = [self.links.swap(self.line, m) for m in (1, 2, 3)]

    def end(self):
        self.others += [self.links.swap(b, self.links.core) for b in self.got]
        return (self.line, *self.got, *self.others)


class Total(Chain):
    def __init__(self, links, run, x):
        super().__init__(links, run)
        self.x = run.hold(x)
        self.groups = [links.masks(b) for b in (links.rest, [1, 2], [links.core])]
        self.step()

    def met(self, got):
        self.x = self.x + sum(got)

    def step(self):
        self.pending = [self.links.swap(self.x, m) for m in self.groups.pop(0)]


class Scatter(Chain):
    def __init__(self, links, run, keep, send):
        super().__init__(links, run)
        self.terms, self.rows, self.bits = [keep], D // 2, links.rest[::-1]
        self.pending = [links.swap(run.hold(send), links.core)]

    def met(self, got):
        self.got = got

    def spread(self, masks):
        self.terms += self.got
        rows = self.rows // (len(masks) + 1)
        self.pending = []
        for n in list(range(len(masks)))[::-1]:
            send = self.run(add_terms, [(t, (n + 1) * rows) for t in self.terms], rows)
            self.pending.insert(0, self.links.swap(send, masks[n]))
        self.rows = rows

    def square(self):
        self.spread((1, 2, 3))

    def line(self):
        self.spread(self.links.masks(self.links.rest))
        self.bits = []

    def step(self):
        self.spread((self.bits.pop(0),))


def on_device(
    links,
    layer_input,
    segment_ids,
    relative_buckets,
    first_gain,
    query_weight,
    key_weight,
    value_weight,
    output_projection,
    relative_table,
    second_gain,
    gate_weight,
    up_weight,
    down_projection,
    output_cotangent,
):
    size = links.size
    me = lax.axis_index("dp") * links.inner + lax.axis_index("fsdp")
    place = np.array([links.place(i) for i in range(links.count)], np.int32)
    source = jnp.asarray(np.argsort(place).astype(np.int32)) ^ me

    gains_shard = jnp.pad(jnp.stack([first_gain, second_gain], axis=1), ((0, 0), (0, BLK - 2)))
    w1, w2, w3 = PIECES
    feed_shards = (gate_weight, up_weight, down_projection)
    qkv_shards = (query_weight, key_weight, value_weight)
    triple = lambda lo, hi: tuple((n, lo, hi) for n in range(3))
    run = Order()
    segk = jnp.broadcast_to(segment_ids[:, None], (SEQ, BLK))
    segq = jnp.where(segment_ids > 0, segment_ids, -1).reshape(NB, BLK)
    spans = ranges(segment_ids)
    one_hot = (relative_buckets[::-1][:, None] == jnp.arange(BUCKETS)[None, :]).astype(BF)
    one_hot = jnp.pad(one_hot, ((0, 1), (0, 0)))
    offsets = lax.dot_general(relative_table, one_hot, (((0,), (1,)), ((), ())), preferred_element_type=F32)

    (first_shard,) = run(pack, qkv_shards + (gains_shard,), (triple(0, GROUP) + ((3, 0, BLK),),))
    first = Gather(links, run, first_shard)
    (second_shard,) = run(pack, qkv_shards + (output_projection,), (triple(GROUP, 2 * GROUP) + ((3, 0, D),),))
    cot, cott = run(prepare, output_cotangent, segk)
    meet(run, first)
    first.square()
    second = Gather(links, run, second_shard)
    early_shard, late_shard = run(
        pack,
        feed_shards,
        (tuple((n, lo, lo + w) for lo, w in ((0, w1), (w1, w2)) for n in range(3)), triple(w1 + w2, FF)),
    )
    early = lax.all_gather(early_shard, AXES, axis=0, tiled=True)
    strips = run(make_strips, offsets.reshape(HEADS // 2, 2, 2 * SEQ))
    meet(run, second)
    second.square()
    meet(run, first)
    lead_blocks = first.end()
    qkv0, normed, turned, gains = run(project, source, layer_input, lead_blocks, True)
    att0, lse0 = run(attn_fwd, spans, segk, segq, strips, qkv0, 0)
    meet(run, second)
    next_blocks = second.end()
    (qkv1,) = run(project, source, normed, next_blocks, False)
    late = lax.all_gather(late_shard, AXES, axis=0, tiled=True)
    att1, lse1 = run(attn_fwd, spans, segk, segq, strips, qkv1, 4)
    hidden, n2, n2t = run(hidden_units, source, att0, att1, layer_input, gains, next_blocks)
    acts = (n2, n2t, cot, cott)
    keep, send, *sums = run(feed, source, acts, early, 0, w1, None)
    s1 = Scatter(links, run, keep, send)
    meet(run, s1)
    s1.square()
    keep, send, *sums = run(feed, source, acts, early, 3 * w1, w2, sums)
    meet(run, s1)
    s2 = Scatter(links, run, keep, send)
    s1.step()
    meet(run, s2)
    s2.square()
    keep, send, block_output, hidden_grad, branch_t, attended_grad, second_term = run(
        feed, source, acts, late, 0, w3, sums, (hidden, gains, segk, next_blocks)
    )
    meet(run, s1, s2)
    s3 = Scatter(links, run, keep, send)
    s2.step()
    s1.step()
    meet(run, s3)
    s3.square()
    g0 = run(attn_bwd, spans, segk, segq, strips, qkv0, attended_grad, lse0, 0)
    meet(run, s1, s2)
    s2.step()
    keep, send = run(weight_terms, source, [(branch_t, [att0, att1]), (turned, g0[:3])])
    meet(run, s2, s3)
    s4 = Scatter(links, run, keep, send)
    s3.step()
    meet(run, s4)
    s4.square()
    g1 = run(attn_bwd, spans, segk, segq, strips, qkv1, attended_grad, lse1, 4)
    meet(run, s3, s4)
    s3.step()
    keep, send = run(weight_terms, source, [(turned, g1[:3])])
    meet(run, s3)
    s5 = Scatter(links, run, keep, send)
    s4.step()
    meet(run, s5)
    s5.square()
    ends = (layer_input, hidden_grad, gains, [*g0[:3], *g1[:3]], lead_blocks + next_blocks)
    input_gradient, first_term = run(last, source, *ends, 0)
    meet(run, s4)
    s4.step()
    input_gradient, other_term = run(last, source, *ends, 1, input_gradient)
    meet(run, s4, s5)
    s5.line()
    offset_grads = jnp.concatenate([g0[3], g1[3]], axis=0).reshape(HEADS, 2 * SEQ)
    table_term = lax.dot_general(
        one_hot.astype(F32), offset_grads, (((0,), (1,)), ((), ())), precision=HIGHEST, preferred_element_type=F32
    )
    first_term = (first_term[0] + other_term[0]).reshape(-1, BLK)
    small = jnp.concatenate([first_term, second_term[0].reshape(-1, BLK), table_term.reshape(-1, BLK)], axis=0)
    total = Total(links, run, small)
    meet(run, s5, total)
    total.step()
    grads = run(finish, [s.terms + s.got for s in (s4, s5, s1, s2, s3)], size)
    meet(run, total)
    total.step()
    meet(run, total)
    small = total.x
    gain_sums = small[: 2 * D // BLK].reshape(2, D)
    mine = lax.dynamic_slice_in_dim(gain_sums, me * size, size, 1)
    table_gradient = small[2 * D // BLK :].reshape(BUCKETS, HEADS)
    return (block_output, input_gradient, *grads, mine[0], mine[1], table_gradient)


def solution(mesh):
    rows, flat, full = P(AXES, None), P(AXES), P()
    return jax.shard_map(
        functools.partial(on_device, Slice(mesh)),
        mesh=mesh,
        in_specs=(rows, flat, full, flat, rows, rows, rows, rows, full, flat, rows, rows, rows, rows),
        out_specs=(rows,) * 9 + (flat, flat, full),
        check_vma=False,
    )
```

```python
import functools

import jax
import jax.numpy as jnp
import numpy as np
from jax import lax
from jax.experimental import pallas as pl
from jax.experimental.pallas import tpu as pltpu
from jax.sharding import PartitionSpec as P

F32 = jnp.float32
BF = jnp.bfloat16
HEADS = 16
BUCKETS = 32
SEQ = 1024
D = 1024
FF = 2816
BLK = 128
NB = SEQ // BLK
STRIP = (2 * NB - 1) * BLK
EPS = 1e-06
NEG = -1e30
VLIM = 60 * 1024 * 1024
AXES = ("dp", "fsdp")
GROUP = 512
PIECES = (768, 1024, 1024)
TILE = 512
FT = 256
ANY = pl.BlockSpec(memory_space=pl.ANY)
SMEM = pl.BlockSpec(memory_space=pltpu.SMEM)
HIGHEST = lax.Precision.HIGHEST
RATE = 2e7
GELU_A = 0.7978845608028654
GELU_B = 0.044715


def params(grid=1):
    return pltpu.CompilerParams(vmem_limit_bytes=VLIM, dimension_semantics=("arbitrary",) * grid)


def cost(flops, moved, trans=0):
    return pl.CostEstimate(flops=int(flops), bytes_accessed=int(moved / 50), transcendentals=int(trans))


def after(kernel, used, deps):
    if not deps:
        return kernel
    return lambda *refs: kernel(*refs[:used], *refs[used + len(deps) :])


def nt(a,b): return lax.dot_general(a,b,(((1,),(1,)),((),())),preferred_element_type=F32)
def nn(a,b): return lax.dot_general(a,b,(((1,),(0,)),((),())),preferred_element_type=F32)

def build_strip(rev_ref, strip):
    for h in range(2):
        row=jnp.broadcast_to(rev_ref[h:h+1,:],(8,2*SEQ))
        base=pltpu.roll(row,0,1,stride=1,stride_axis=0)
        for m in range(BLK//8):
            turned=pltpu.roll(base,(8*m-(BLK-1))%(2*SEQ),1)
            for d in range(2*NB-1):
                e=2*NB-2-d
                strip[d*BLK+8*m:d*BLK+8*m+8,h*BLK:(h+1)*BLK]=turned[:,e*BLK:(e+1)*BLK]

def fold_strip(strip, out_ref):
    for h in range(2):
        total=jnp.zeros((8,2*SEQ),F32)
        for m in range(BLK//8):
            parts=[strip[(2*NB-2-e)*BLK+8*m:(2*NB-2-e)*BLK+8*m+8,h*BLK:(h+1)*BLK] for e in range(2*NB-1)]
            parts.append(jnp.zeros((8,BLK),F32))
            total=total+pltpu.roll(jnp.concatenate(parts,axis=1),(BLK-1-8*m)%(2*SEQ),1)
        row=total[0:1]
        for s in range(1,8):
            row=row+pltpu.roll(total[s:s+1],2*SEQ-s,1)
        out_ref[h:h+1,:]=row

def lanes_mask():
    lane=lax.broadcasted_iota(jnp.int32,(1,BLK),1)
    return lane<64

def stack_heads(x, first):
    zero=jnp.zeros_like(x)
    return jnp.concatenate([jnp.where(first,x,zero),jnp.where(first,zero,x)],axis=0)


def strip_kernel(rev_ref, strip):
    build_strip(rev_ref, strip)

def make_strips(rev, deps=()):
    return pl.pallas_call(after(strip_kernel, 1, deps),grid=(8,),
        in_specs=[pl.BlockSpec((None,2,2*SEQ),lambda p:(p,0,0))]+[ANY]*len(deps),
        out_specs=pl.BlockSpec((None,STRIP,2*BLK),lambda p:(p,0,0)),
        out_shape=jax.ShapeDtypeStruct((8,STRIP,2*BLK),F32),
        compiler_params=pltpu.CompilerParams(vmem_limit_bytes=VLIM),
        name="bias_strips")(rev, *deps)

def attn_fwd_kernel(UNIT, rng_ref, segk_ref, segq_ref, strip, qkv, o_ref, lse_ref, vt):
    first=lanes_mask()
    for u in range(UNIT):
        vt[u]=qkv[:,2*GROUP+u*BLK:2*GROUP+(u+1)*BLK].T
    mean=jnp.sum(qkv[:,2*GROUP:].astype(F32),axis=0,keepdims=True)*(1.0/SEQ)

    def block(qi, carry):
        q0=pl.multiple_of(qi*BLK,BLK)
        lo=rng_ref[qi]; width=rng_ref[NB+qi]
        k0=pl.multiple_of(lo*BLK,BLK)
        b0=pl.multiple_of((lo-qi+NB-1)*BLK,BLK)
        segq=segq_ref[pl.ds(qi,1),:]
        @pl.when(width==0)
        def _():
            o_ref[pl.ds(q0,BLK),:]=jnp.broadcast_to(mean,(BLK,UNIT*BLK)).astype(BF)
            for u in range(UNIT):
                lse_ref[u,pl.ds(qi,1),:]=jnp.zeros((1,2*BLK),F32)
        for w in range(1,NB+1):
            @pl.when(width==w)
            def _():
                rows=w*BLK
                allowed=segk_ref[pl.ds(k0,rows),:]==segq
                live_row=segq>0
                live_row=jnp.concatenate([live_row,live_row],axis=1)
                live_col=segk_ref[pl.ds(q0,BLK),:]>0
                units=[slice(u*BLK,(u+1)*BLK) for u in range(UNIT)]
                qcats=[stack_heads(qkv[pl.ds(q0,BLK),lanes],first) for lanes in units]
                scores=[nt(qkv[pl.ds(k0,rows),GROUP+lanes.start:GROUP+lanes.stop],qcat) for lanes,qcat in zip(units,qcats)]
                probs=[]; stats=[]; totals=[]
                for u in range(UNIT):
                    both=[]; stat=[]; tot=[]
                    s=scores[u]+strip[u,pl.ds(b0,rows),:]
                    for h in range(2):
                        sh=jnp.where(allowed,s[:,h*BLK:(h+1)*BLK],NEG)
                        peak=jnp.max(sh,axis=0,keepdims=True)
                        e=jnp.exp(sh-peak)
                        t=jnp.sum(e,axis=0,keepdims=True)
                        both.append(e.astype(BF)); stat.append(peak+jnp.log(t)); tot.append(t)
                    probs.append(jnp.concatenate(both,axis=1)); stats.append(jnp.concatenate(stat,axis=1)); totals.append(jnp.concatenate(tot,axis=1))
                ots=[nn(vt[u,:,pl.ds(k0,rows)],probs[u]) for u in range(UNIT)]
                for u,lanes in enumerate(units):
                    ot=ots[u]*(1.0/totals[u])
                    o=jnp.concatenate([ot[:64,:BLK],ot[64:,BLK:]],axis=0).T
                    o_ref[pl.ds(q0,BLK),lanes]=jnp.where(live_col,o,mean[:,lanes]).astype(BF)
                    lse_ref[u,pl.ds(qi,1),:]=jnp.where(live_row,stats[u],0.0)
        return carry
    lax.fori_loop(0,NB,block,0)

def attn_bwd_kernel(UNIT, rng_ref, segk_ref, segq_ref, strip, q_ref, k_ref, v_ref, g_ref, lse_ref,
                    dq_ref, dk_ref, dv_ref, off_ref, dstrip, kt, dk, dv):
    first=lanes_mask()
    dstrip[...]=jnp.zeros_like(dstrip)
    dk[...]=jnp.zeros_like(dk)
    for u in range(UNIT):
        lanes=slice(u*BLK,(u+1)*BLK)
        kt[u]=k_ref[:,lanes].T
        padded=jnp.where(segk_ref[...]>0,0.0,g_ref[:,lanes].astype(F32))
        dv[:,lanes]=jnp.broadcast_to(jnp.sum(padded,axis=0,keepdims=True)*(1.0/SEQ),(SEQ,BLK))

    def block(qi, carry):
        q0=pl.multiple_of(qi*BLK,BLK)
        lo=rng_ref[qi]; width=rng_ref[NB+qi]
        k0=pl.multiple_of(lo*BLK,BLK)
        b0=pl.multiple_of((lo-qi+NB-1)*BLK,BLK)
        segq=segq_ref[pl.ds(qi,1),:]
        @pl.when(width==0)
        def _():
            dq_ref[pl.ds(q0,BLK),:]=jnp.zeros((BLK,UNIT*BLK),BF)
        for w in range(1,NB+1):
            @pl.when(width==w)
            def _():
                rows=w*BLK
                allowed=segk_ref[pl.ds(k0,rows),:]==segq
                units=[slice(u*BLK,(u+1)*BLK) for u in range(UNIT)]
                qcats=[stack_heads(q_ref[pl.ds(q0,BLK),lanes],first) for lanes in units]
                gcats=[stack_heads(g_ref[pl.ds(q0,BLK),lanes],first) for lanes in units]
                scores=[nt(k_ref[pl.ds(k0,rows),lanes],qcat) for lanes,qcat in zip(units,qcats)]
                dps=[nt(v_ref[pl.ds(k0,rows),lanes],gcat) for lanes,gcat in zip(units,gcats)]
                probs=[]; grads=[]
                for u in range(UNIT):
                    lse=lse_ref[u,pl.ds(qi,1),:]
                    s=scores[u]+strip[u,pl.ds(b0,rows),:]
                    ps=[]; ds=[]
                    for h in range(2):
                        cols=slice(h*BLK,(h+1)*BLK)
                        prob=jnp.exp(jnp.where(allowed,s[:,cols],NEG)-lse[:,cols])
                        t=prob*dps[u][:,cols]
                        inner=jnp.sum(t,axis=0,keepdims=True)
                        d=t-prob*inner
                        dstrip[u,pl.ds(b0,rows),cols]+=d
                        ps.append(prob.astype(BF)); ds.append(d.astype(BF))
                    probs.append(jnp.concatenate(ps,axis=1)); grads.append(jnp.concatenate(ds,axis=1))
                for u,lanes in enumerate(units):
                    dv[pl.ds(k0,rows),lanes]+=nn(probs[u],gcats[u])
                dqts=[nn(kt[u,:,pl.ds(k0,rows)],grads[u]) for u in range(UNIT)]
                for u,lanes in enumerate(units):
                    dk[pl.ds(k0,rows),lanes]+=nn(grads[u],qcats[u])
                for u,lanes in enumerate(units):
                    dq_ref[pl.ds(q0,BLK),lanes]=jnp.concatenate([dqts[u][:64,:BLK],dqts[u][64:,BLK:]],axis=0).T.astype(BF)
        return carry
    lax.fori_loop(0,NB,block,0)
    dk_ref[...]=dk[...].astype(BF)
    dv_ref[...]=dv[...].astype(BF)
    for u in range(UNIT):
        fold_strip(dstrip.at[u], off_ref.at[u])

def backward_kernel(unit, lead, rng, source, segk, segq, strip, q, k, v, grad, lse, *refs):
    lefts, rights, refs = refs[: 1 + lead], refs[1 + lead : 1 + 3 * lead], refs[1 + 3 * lead :]
    dq, dk, dv, off, keep, send, dstrip, kt, dk_sum, dv_sum, held, sem = refs
    p = pl.program_id(0)

    @pl.when(p == 0)
    def _():
        for n, left in enumerate(lefts):
            order_rows(source, left, held.at[n], sem.at[n])

    attn_bwd_kernel(
        unit, rng, segk, segq, strip, q, k, v, grad, lse, dq, dk, dv, off, dstrip, kt, dk_sum, dv_sum
    )

    @pl.when(p == 0)
    def _():
        for n in range(1 + lead):
            wait_whole(held.at[n], sem.at[n])

    half, wide = D // 2, unit * BLK
    for j, right in enumerate((dq, dk, dv)):
        part = nn(held[0], right[...]).astype(BF)
        keep[:, j * wide : (j + 1) * wide] = part[:half]
        send[:, j * wide : (j + 1) * wide] = part[half:]
    for n, right in enumerate(rights):

        @pl.when(p == n)
        def _():
            for j in range(GROUP // wide):
                part = nn(held[1], right[:, j * wide : (j + 1) * wide]).astype(BF)
                cols = slice((3 + j) * wide, (4 + j) * wide)
                keep[:, cols] = part[:half]
                send[:, cols] = part[half:]


def attn_bwd(rng, source, segk, segq, strips, qkv, g, lse, turned, more, first_pair):
    unit, steps = 2, 2
    wide = unit * BLK
    lead = int(len(more) > 0)
    f = first_pair // unit
    c = lambda o: pl.BlockSpec((SEQ, wide), lambda p, r, s: (0, o + p))
    whole = lambda *s: pl.BlockSpec(s, lambda p, r, s: (0, 0))
    width = 3 * wide + lead * GROUP
    out = pl.BlockSpec((D // 2, width), lambda p, r, s: (0, p))
    gs = pltpu.PrefetchScalarGridSpec(
        num_scalar_prefetch=2,
        grid=(steps,),
        in_specs=[
            whole(SEQ, BLK), whole(NB, BLK),
            pl.BlockSpec((unit, STRIP, 2 * BLK), lambda p, r, s: (f + p, 0, 0)),
            c(0), c(steps), c(2 * steps), c(f),
            pl.BlockSpec((unit, NB, 2 * BLK), lambda p, r, s: (p, 0, 0)),
        ] + [ANY] * (1 + lead) + [whole(SEQ, GROUP)] * (2 * lead),
        out_specs=[c(0), c(0), c(0), pl.BlockSpec((unit, 2, 2 * SEQ), lambda p, r, s: (p, 0, 0)), out, out],
        scratch_shapes=[
            pltpu.VMEM((unit, STRIP, 2 * BLK), F32), pltpu.VMEM((unit, BLK, SEQ), BF),
            pltpu.VMEM((SEQ, wide), F32), pltpu.VMEM((SEQ, wide), F32),
            pltpu.VMEM((1 + lead, D, SEQ), BF), pltpu.SemaphoreType.DMA((1 + lead,)),
        ],
    )
    sh = jax.ShapeDtypeStruct((SEQ, steps * wide), BF)
    term = jax.ShapeDtypeStruct((D // 2, steps * width), BF)
    return pl.pallas_call(
        functools.partial(backward_kernel, unit, lead),
        grid_spec=gs,
        out_shape=[sh, sh, sh, jax.ShapeDtypeStruct((steps * unit, 2, 2 * SEQ), F32), term, term],
        compiler_params=params(),
        cost_estimate=cost(24 * RATE, 16 * SEQ * wide * 2),
        name="attention_backward",
    )(rng, source, segk, segq, strips, qkv, qkv, qkv, g, lse, turned, *more)


def ranges(seg):
    s=seg.reshape(NB,BLK)
    least=s[:,0]; most=jnp.max(s,axis=1)
    lo=jnp.sum((most[None,:]<least[:,None])&(least[None,:]>0),axis=1)
    hi=jnp.sum((least[None,:]<=most[:,None])&(least[None,:]>0),axis=1)
    w=jnp.where(least>0,hi-lo,0)
    return jnp.concatenate([jnp.where(least>0,lo,0),w]).astype(jnp.int32)


def prep_kernel(c_ref, seg_ref, out_ref, turned_ref):
    low = jnp.where(jnp.concatenate([seg_ref[...] > 0] * (D // BLK), axis=1), c_ref[...].astype(F32), 0.0).astype(BF)
    out_ref[...] = low
    turned_ref[...] = low.T


def prepare(c, segk):
    rows = 256
    blk = pl.BlockSpec((rows, D), lambda i: (i, 0))
    return pl.pallas_call(
        prep_kernel,
        grid=(SEQ // rows,),
        in_specs=[blk, pl.BlockSpec((rows, BLK), lambda i: (i, 0))],
        out_specs=[blk, pl.BlockSpec((D, rows), lambda i: (0, i))],
        out_shape=[jax.ShapeDtypeStruct((SEQ, D), BF), jax.ShapeDtypeStruct((D, SEQ), BF)],
        compiler_params=params(),
        cost_estimate=cost(4 * RATE, 6 * SEQ * D),
        name="prepare",
    )(c, segk)


def pack_kernel(spans, count, *refs):
    ins, outs = refs[:count], refs[count:]
    for out, cols in zip(outs, spans):
        at = 0
        for n, lo, hi in cols:
            out[:, at : at + hi - lo] = ins[n][:, lo:hi]
            at += hi - lo


def pack(shards, spans, deps=()):
    rows = shards[0].shape[0]
    widths = [sum(hi - lo for _, lo, hi in cols) for cols in spans]
    whole = pl.BlockSpec(memory_space=pltpu.VMEM)
    return pl.pallas_call(
        after(functools.partial(pack_kernel, spans, len(shards)), len(shards), deps),
        in_specs=[whole] * len(shards) + [ANY] * len(deps),
        out_specs=[whole] * len(widths),
        out_shape=[jax.ShapeDtypeStruct((rows, w), BF) for w in widths],
        name="pack_shards",
    )(*shards, *deps)


def join(*parts):
    return jnp.concatenate(parts, axis=0)


def add_terms(terms, rows):
    return sum(t[off : off + rows].astype(F32) for t, off in terms).astype(BF)


def finish_kernel(counts, *refs):
    weights, gains, refs = refs[:5], refs[5], refs[6:]
    sums, at = [], 0
    for n in counts:
        total = refs[at][...].astype(F32)
        for ref in refs[at + 1 : at + n]:
            total = total + ref[...].astype(F32)
        sums.append(total)
        at += n
    outs = refs[at:]
    wide = GROUP // 2
    for g, step in ((0, 3 * wide + GROUP), (1, 3 * wide)):
        for p in range(2):
            for j in range(3):
                col = g * GROUP + p * wide
                outs[j][:, col : col + wide] = sums[g][:, p * step + j * wide : p * step + (j + 1) * wide]
    for p in range(2):
        start = (p + 1) * (3 * wide + GROUP) - GROUP
        outs[3][:, p * GROUP : (p + 1) * GROUP] = sums[0][:, start : start + GROUP]
    at = 0
    for s, width in zip(sums[2:], PIECES):
        for j in range(3):
            outs[4 + j][:, at : at + width] = s[:, j * width : (j + 1) * width]
        at += width
    match = lambda w, out: jnp.sum(w[...].astype(F32) * out[...], axis=1, keepdims=True)
    one = match(weights[0], outs[0]) + match(weights[1], outs[1]) + match(weights[2], outs[2])
    two = match(weights[3], outs[4]) + match(weights[4], outs[5])
    lane = lax.broadcasted_iota(jnp.int32, gains.shape, 1)
    outs[7][...] = jnp.where(lane == 0, one, two) / jnp.where(lane < 2, gains[...].astype(F32), 1.0)


def finish(sets, weights, gains):
    rows = gains.shape[0]
    flat = [x for terms in sets for x in terms]
    widths = (D,) * 4 + (FF,) * 3 + (BLK,)
    top = lambda w: pl.BlockSpec((rows, w), lambda i: (0, 0))
    return pl.pallas_call(
        functools.partial(finish_kernel, tuple(len(t) for t in sets)),
        grid=(1,),
        in_specs=[top(x.shape[1]) for x in (*weights, gains, *flat)],
        out_specs=[top(w) for w in widths],
        out_shape=[jax.ShapeDtypeStruct((rows, w), F32) for w in widths],
        compiler_params=params(),
        name="weight_gradients",
    )(*weights, gains, *flat)


def place_blocks(source_ref, blocks, start, cols, dst, at, sem):
    rows = blocks[0].shape[0]
    size = D // source_ref.shape[0]
    per = rows // size
    for n, ref in enumerate(blocks):

        def one(i, carry):
            row = pl.multiple_of(source_ref[n * per + i] * size, size)
            pltpu.make_async_copy(
                ref.at[pl.ds(pl.multiple_of(i * size, size), size), pl.ds(start, cols)],
                dst.at[pl.ds(row, size), pl.ds(at, cols)],
                sem,
            ).start()
            return carry

        lax.fori_loop(0, per, one, 0)


def wait_whole(dst, sem):
    pltpu.make_async_copy(dst, dst, sem).wait()


def order_rows(source_ref, src, dst, sem):
    size = D // source_ref.shape[0]

    def one(p, carry):
        row = pl.multiple_of(source_ref[p] * size, size)
        pltpu.make_async_copy(
            src.at[pl.ds(row, size)], dst.at[pl.ds(pl.multiple_of(p * size, size), size)], sem
        ).start()
        return carry

    lax.fori_loop(0, D // size, one, 0)


def scaled_rows(x):
    return lax.rsqrt(jnp.mean(x * x, axis=-1, keepdims=True) + EPS)


def attend_kernel(lead, first_pair, *refs):
    rng, source, segk, segq, x, strips = refs[:6]
    blocks, refs = refs[6:14], refs[14:]
    if lead:
        qkv_out, o_ref, lse_ref, gains_ref, normed_out, turned_out = refs[:6]
        qkv, w, strip, normed, vt, sem, turned = refs[6:]
    else:
        qkv_out, o_ref, lse_ref = refs[:3]
        qkv, w, strip, normed, vt, sem = refs[3:]
    unit = vt.shape[0]
    bring = pltpu.make_async_copy(x, normed, sem.at[0])
    bring.start()
    place_blocks(source, blocks, 0, w.shape[1], w, 0, sem.at[1])
    pads = pltpu.make_async_copy(strips.at[pl.ds(first_pair, unit)], strip, sem.at[2])
    pads.start()
    outs = [pltpu.make_async_copy(qkv, qkv_out, sem.at[3])]
    bring.wait()
    wait_whole(w, sem.at[1])
    if lead:
        gains_ref[...] = w[:, 3 * GROUP :].astype(F32).T[:8]

        def rows_of(i, carry):
            at = pl.multiple_of(i * 256, 256)
            rows = normed[pl.ds(at, 256), :].astype(F32)
            low = (rows * scaled_rows(rows) * gains_ref[0:1, :]).astype(BF)
            normed[pl.ds(at, 256), :] = low
            turned[:, pl.ds(at, 256)] = low.T
            return carry

        lax.fori_loop(0, SEQ // 256, rows_of, 0)
        outs += [pltpu.make_async_copy(normed, normed_out, sem.at[4]), pltpu.make_async_copy(turned, turned_out, sem.at[5])]
        for c in outs[1:]:
            c.start()

    def columns(j, carry):
        cols = pl.ds(pl.multiple_of(j * FT, FT), FT)
        qkv[:, cols] = nn(normed[...], w[:, cols]).astype(BF)
        return carry

    lax.fori_loop(0, 3 * GROUP // FT, columns, 0)
    outs[0].start()
    pads.wait()
    attn_fwd_kernel(unit, rng, segk, segq, strip, qkv, o_ref, lse_ref, vt)
    for c in outs:
        c.wait()


def attend(rng, source, segk, segq, strips, x, blocks, lead):
    unit = 4
    width = 3 * GROUP + (BLK if lead else 0)
    vmem = pl.BlockSpec(memory_space=pltpu.VMEM)
    shape = lambda t, *s: jax.ShapeDtypeStruct(s, t)
    out_specs = [ANY, vmem, vmem] + ([vmem, ANY, ANY] if lead else [])
    out_shape = [shape(BF, SEQ, 3 * GROUP), shape(BF, SEQ, GROUP), shape(F32, unit, NB, 2 * BLK)]
    out_shape += [shape(F32, 8, D), shape(BF, SEQ, D), shape(BF, D, SEQ)] if lead else []
    return pl.pallas_call(
        functools.partial(attend_kernel, lead, 0 if lead else unit),
        in_specs=[SMEM, SMEM, vmem, vmem, ANY, ANY] + [ANY] * len(blocks),
        out_specs=out_specs,
        out_shape=out_shape,
        scratch_shapes=[
            pltpu.VMEM((SEQ, 3 * GROUP), BF), pltpu.VMEM((D, width), BF), pltpu.VMEM((unit, STRIP, 2 * BLK), F32),
            pltpu.VMEM((SEQ, D), BF), pltpu.VMEM((unit, BLK, SEQ), BF), pltpu.SemaphoreType.DMA((6,)),
        ] + ([pltpu.VMEM((D, SEQ), BF)] if lead else []),
        compiler_params=pltpu.CompilerParams(vmem_limit_bytes=VLIM),
        cost_estimate=cost(20 * RATE, 2 * D * width + 4 * SEQ * D),
        name="attention_forward",
    )(rng, source, segk, segq, x, strips, *blocks)


def hidden_kernel(*refs):
    source, a0, a1, x_ref, gains_ref = refs[:5]
    h_ref, n2_ref, n2t_ref, w, sem = refs[13:]

    @pl.when(pl.program_id(0) == 0)
    def _():
        place_blocks(source, refs[5:13], 3 * GROUP, D, w, 0, sem.at[0])
        wait_whole(w, sem.at[0])

    hidden = x_ref[...].astype(F32) + nt(jnp.concatenate([a0[...], a1[...]], axis=1), w[...])
    h_ref[...] = hidden
    normed = (hidden * scaled_rows(hidden) * gains_ref[1:2, :]).astype(BF)
    n2_ref[...] = normed
    n2t_ref[...] = normed.T


def hidden_units(source, a0, a1, x, gains, blocks):
    rows = TILE
    tok = lambda c: pl.BlockSpec((rows, c), lambda i: (i, 0))
    return pl.pallas_call(
        hidden_kernel,
        grid=(SEQ // rows,),
        in_specs=[SMEM, tok(GROUP), tok(GROUP), tok(D), pl.BlockSpec((8, D), lambda i: (0, 0))] + [ANY] * len(blocks),
        out_specs=[tok(D), tok(D), pl.BlockSpec((D, rows), lambda i: (0, i))],
        out_shape=[
            jax.ShapeDtypeStruct((SEQ, D), F32),
            jax.ShapeDtypeStruct((SEQ, D), BF),
            jax.ShapeDtypeStruct((D, SEQ), BF),
        ],
        scratch_shapes=[pltpu.VMEM((D, D), BF), pltpu.SemaphoreType.DMA((1,))],
        compiler_params=params(),
        cost_estimate=cost(6 * RATE, 16 * SEQ * D),
        name="hidden_units",
    )(source, a0, a1, x, gains, *blocks)


def feed_kernel(lead, final, width, base, *refs):
    source, n2, n2t, cot, cott, whole = refs[:6]
    refs = refs[6:]
    sums_from = () if lead else refs[:2]
    refs = refs[len(sums_from) :]
    if final:
        h_in, gains_ref, seg_in, blocks, refs = refs[0], refs[1], refs[2], refs[3:11], refs[11:]
    keep, send = refs[:2]
    outs, refs = (refs[2:6], refs[6:]) if final else (refs[2:4], refs[4:])
    n2_v, n2t_v, cot_v, cott_v, w, stage, bo, ng, mix_v, gu_v, sem_w, sem_o, sem_i = refs[:13]
    half = D // 2
    tiles = width // FT

    def weight_copies(f):
        out = []
        for j in range(3):
            col = pl.multiple_of(j * width + f * FT, FT)
            out.append(
                pltpu.make_async_copy(
                    whole.at[:, pl.ds(pl.multiple_of(base + col, BLK), FT)], w.at[:, pl.ds(col, FT)], sem_w.at[f, j]
                )
            )
        return out

    def term_copies(g):
        col = pl.multiple_of(g * FT, FT)
        return [
            pltpu.make_async_copy(
                stage.at[pl.ds(s * half, half), pl.ds(col, FT)], dst.at[:, pl.ds(col, FT)], sem_o.at[g, s]
            )
            for s, dst in enumerate((keep, send))
        ]

    first = [pltpu.make_async_copy(n2, n2_v, sem_i.at[0]), pltpu.make_async_copy(cot, cot_v, sem_i.at[1])]
    sums_in = [pltpu.make_async_copy(a, b, sem_i.at[4 + n]) for n, (a, b) in enumerate(zip(sums_from, (bo, ng)))]
    if final:
        h_v, wo, ag_v, bt_v, out_v, seg_v = refs[13:]
        sums_in += [pltpu.make_async_copy(h_in, h_v, sem_i.at[6]), pltpu.make_async_copy(seg_in, seg_v, sem_i.at[7])]
        sources = (out_v, ng, bt_v, ag_v)
    else:
        sources = (bo, ng)
    results = [pltpu.make_async_copy(a, b, sem_i.at[8 + n]) for n, (a, b) in enumerate(zip(sources, outs))]
    for c in weight_copies(0) + first:
        c.start()
    for f in range(1, tiles):
        for c in weight_copies(f):
            c.start()
    for c in sums_in:
        c.start()
    for c in first:
        c.wait()

    def units(f, carry):
        for c in weight_copies(f):
            c.wait()
        at = [pl.ds(pl.multiple_of(j * width + f * FT, FT), FT) for j in range(3)]

        def tokens(i, inner):
            rows = pl.ds(pl.multiple_of(i * TILE, TILE), TILE)
            n = n2_v[rows, :]
            gate = nn(n, w[:, at[0]])
            upward = nn(n, w[:, at[1]])
            mixed_grad = nn(cot_v[rows, :], w[:, at[2]])
            square = gate * gate
            bend = jnp.tanh(gate * (GELU_A + (GELU_A * GELU_B) * square))
            curve = 0.5 * (1.0 + bend)
            active = gate * curve
            slope = curve + (0.5 * gate) * (1.0 - bend * bend) * (GELU_A + (3.0 * GELU_A * GELU_B) * square)
            mix_v[rows, at[0]] = (active * upward).astype(BF)
            gu_v[rows, at[0]] = (mixed_grad * upward * slope).astype(BF)
            gu_v[rows, at[1]] = (mixed_grad * active).astype(BF)
            return inner

        for i in range(SEQ // TILE):
            tokens(i, 0)
        return carry

    lax.fori_loop(0, tiles, units, 0)
    order_rows(source, n2t, n2t_v, sem_i.at[2])
    order_rows(source, cott, cott_v, sem_i.at[3])
    if final:
        place_blocks(source, blocks, 3 * GROUP, D, wo, 0, sem_i.at[13])
    for c in sums_in:
        c.wait()

    def sums(i, carry):
        rows = pl.ds(pl.multiple_of(i * TILE, TILE), TILE)
        for j in range(2):
            cols = slice(j * TILE, (j + 1) * TILE)
            one = nt(mix_v[rows, :], w[cols, 2 * width :])
            two = nt(gu_v[rows, :], w[cols, : 2 * width])
            bo[rows, cols] = one if lead else bo[rows, cols] + one
            ng[rows, cols] = two if lead else ng[rows, cols] + two
        return carry

    lax.fori_loop(0, SEQ // TILE, sums, 0)
    if final:
        wait_whole(wo, sem_i.at[13])

        def close(i, carry):
            rows = pl.ds(pl.multiple_of(i * 256, 256), 256)
            hidden = h_v[rows, :]
            live = jnp.concatenate([seg_v[rows, :] > 0] * (D // BLK), axis=1)
            out_v[rows, :] = jnp.where(live, hidden + bo[rows, :], 0.0).astype(BF)
            grad = ng[rows, :]
            scale = scaled_rows(hidden)
            grad = grad * gains_ref[1:2, :]
            mean = jnp.mean(grad * hidden, axis=-1, keepdims=True)
            out = cot_v[rows, :].astype(F32) + (scale * grad - hidden * (scale * scale * scale * mean))
            ng[rows, :] = out
            low = out.astype(BF)
            mix_low[rows, :] = low
            bt_v[:, rows] = low.T
            return carry

        mix_low = n2_v
        lax.fori_loop(0, SEQ // 256, close, 0)

        def attended(i, carry):
            cols = pl.ds(pl.multiple_of(i * FT, FT), FT)
            ag_v[:, cols] = nn(mix_low[...], wo[:, cols]).astype(BF)
            return carry

        lax.fori_loop(0, D // FT, attended, 0)
    for c in results:
        c.start()
    wait_whole(n2t_v, sem_i.at[2])
    wait_whole(cott_v, sem_i.at[3])

    def terms(left, right, start):
        def one(f, carry):
            cols = pl.ds(pl.multiple_of(f * FT, FT), FT)
            out = pl.ds(pl.multiple_of(start * FT + f * FT, FT), FT)
            stage[:, out] = nn(left[...], right[:, cols]).astype(BF)
            for c in term_copies(start + f):
                c.start()
            return carry

        return one

    lax.fori_loop(0, 2 * tiles, terms(n2t_v, gu_v, 0), 0)
    lax.fori_loop(0, tiles, terms(cott_v, mix_v, 2 * tiles), 0)
    for c in results:
        c.wait()

    def drain(g, carry):
        for c in term_copies(g):
            c.wait()
        return carry

    lax.fori_loop(0, 3 * tiles, drain, 0)


def feed(source, acts, whole, base, width, sums, closing=None):
    lead, final = sums is None, closing is not None
    tiles = width // FT
    args = [source, *acts, whole] + ([] if lead else list(sums))
    specs = [SMEM] + [ANY] * (len(args) - 1)
    if final:
        hidden, gains, segk, blocks = closing
        args += [hidden, gains, segk, *blocks]
        specs += [ANY, pl.BlockSpec(memory_space=pltpu.VMEM), ANY] + [ANY] * len(blocks)
    half = jax.ShapeDtypeStruct((D // 2, 3 * width), BF)
    shape = lambda t, *s: jax.ShapeDtypeStruct(s, t)
    total = shape(F32, SEQ, D)
    outs = [shape(BF, SEQ, D), total, shape(BF, D, SEQ), shape(BF, SEQ, D)] if final else [total, total]
    bf = lambda *s: pltpu.VMEM(s, BF)
    scratch = [
        bf(SEQ, D), bf(D, SEQ), bf(SEQ, D), bf(D, SEQ), bf(D, 3 * width), bf(D, 3 * width),
        pltpu.VMEM((SEQ, D), F32), pltpu.VMEM((SEQ, D), F32),
        bf(SEQ, width), bf(SEQ, 2 * width),
        pltpu.SemaphoreType.DMA((tiles, 3)), pltpu.SemaphoreType.DMA((3 * tiles, 2)), pltpu.SemaphoreType.DMA((14,)),
    ]
    if final:
        scratch += [
            pltpu.VMEM((SEQ, D), F32), bf(D, D), bf(SEQ, D), bf(D, SEQ), bf(SEQ, D),
            pltpu.VMEM((SEQ, BLK), jnp.int32),
        ]
    return pl.pallas_call(
        functools.partial(feed_kernel, lead, final, width, base),
        in_specs=specs,
        out_specs=[ANY] * (2 + len(outs)),
        out_shape=[half, half] + outs,
        scratch_shapes=scratch,
        compiler_params=pltpu.CompilerParams(vmem_limit_bytes=VLIM),
        cost_estimate=cost((30 * width / 1024 + (6 if final else 0)) * RATE, 12 * D * width + 24 * SEQ * D, SEQ * width),
        name="feed_forward",
    )(*args)


def last_kernel(count, *refs):
    source, x_ref, hg_ref, gains_ref = refs[:4]
    grads = refs[4 : 4 + count]
    blocks = refs[4 + count : 20 + count]
    out_ref, w, sem = refs[-3:]
    half = 3 * GROUP

    @pl.when(pl.program_id(0) == 0)
    def _():
        for n in range(2):
            place_blocks(source, blocks[8 * n : 8 * n + 8], 0, half, w, n * half, sem.at[n])
        for n in range(2):
            wait_whole(w.at[:, pl.ds(n * half, half)], sem.at[n])

    grad = nt(jnp.concatenate([g[...] for g in grads], axis=1), w[...])
    x = x_ref[...].astype(F32)
    scale = scaled_rows(x)
    grad = grad * gains_ref[0:1, :]
    mean = jnp.mean(grad * x, axis=-1, keepdims=True)
    out_ref[...] = hg_ref[...] + (scale * grad - x * (scale * scale * scale * mean))


def last(source, x, hg, gains, grads, blocks):
    rows = 256
    tok = lambda c: pl.BlockSpec((rows, c), lambda i: (i, 0))
    whole = pl.BlockSpec((8, D), lambda i: (0, 0))
    return pl.pallas_call(
        functools.partial(last_kernel, len(grads)),
        grid=(SEQ // rows,),
        in_specs=[SMEM, tok(D), tok(D), whole] + [tok(g.shape[1]) for g in grads] + [ANY] * len(blocks),
        out_specs=tok(D),
        out_shape=jax.ShapeDtypeStruct((SEQ, D), F32),
        scratch_shapes=[pltpu.VMEM((D, 6 * GROUP), BF), pltpu.SemaphoreType.DMA((2,))],
        compiler_params=params(),
        cost_estimate=cost(14 * RATE, 14 * SEQ * D),
        name="input_gradient",
    )(source, x, hg, gains, *grads, *blocks)


class Slice:
    def __init__(self, mesh):
        self.count = mesh.shape["dp"] * mesh.shape["fsdp"]
        self.inner = mesh.shape["fsdp"]
        self.core = self.inner
        bits = [1 << b for b in range(self.count.bit_length() - 1)]
        self.rest = [b for b in reversed(bits) if b not in (1, 2, self.core)]
        self.order = [self.core, 2, 1] + self.rest[::-1]
        self.size = D // self.count

    def place(self, index):
        p = index * 0
        for b in self.order:
            p = 2 * p + (index // b) % 2
        return p

    def swap(self, x, bit):
        return lax.ppermute(x, AXES, [(i, i ^ bit) for i in range(self.count)])

    @staticmethod
    def masks(bits):
        return [sum(b for j, b in enumerate(bits) if n >> j & 1) for n in range(1, 1 << len(bits))]


class Order:
    def __init__(self):
        self.token = None

    def hold(self, args):
        leaves, tree = jax.tree.flatten(args)
        at = [i for i, x in enumerate(leaves) if hasattr(x, "aval")]
        if self.token is not None:
            held = lax.optimization_barrier([leaves[i] for i in at] + [self.token])
            for i, x in zip(at, held):
                leaves[i] = x
        return jax.tree.unflatten(tree, leaves)

    def __call__(self, f, *args):
        out = f(*self.hold(args))
        self.token = jax.tree.leaves(out)[0]
        return out


class Chain:
    def __init__(self, links, run):
        self.links, self.run, self.pending = links, run, []


def meet(run, *chains):
    arrays = run.hold([c.pending for c in chains] + [run.token])
    run.token = arrays.pop()
    for c, got in zip(chains, arrays):
        c.met(got)
        c.pending = []


class Gather(Chain):
    def __init__(self, links, run, shard):
        super().__init__(links, run)
        self.line = run.hold(shard)
        self.pending = [links.swap(self.line, m) for m in links.masks(links.rest)]

    def met(self, got):
        self.got = got

    def square(self):
        self.line = self.run(join, self.line, *self.got)
        self.others = [self.links.swap(self.line, self.links.core)]
        self.pending = [self.links.swap(self.line, m) for m in (1, 2, 3)]

    def end(self):
        self.others += [self.links.swap(b, self.links.core) for b in self.got]
        return (self.line, *self.got, *self.others)


class Total(Chain):
    def __init__(self, links, run, x):
        super().__init__(links, run)
        self.x = run.hold(x)
        self.groups = [links.masks(b) for b in (links.rest, [1, 2], [links.core])]
        self.step()

    def met(self, got):
        self.x = self.x + sum(got)

    def step(self):
        self.pending = [self.links.swap(self.x, m) for m in self.groups.pop(0)]


class Scatter(Chain):
    def __init__(self, links, run, keep, send):
        super().__init__(links, run)
        self.terms, self.rows, self.bits = [keep], D // 2, links.rest[::-1]
        self.pending = [links.swap(run.hold(send), links.core)]

    def met(self, got):
        self.got = got

    def spread(self, masks):
        self.terms += self.got
        rows = self.rows // (len(masks) + 1)
        self.pending = []
        for n in list(range(len(masks)))[::-1]:
            send = self.run(add_terms, [(t, (n + 1) * rows) for t in self.terms], rows)
            self.pending.insert(0, self.links.swap(send, masks[n]))
        self.rows = rows

    def square(self):
        self.spread((1, 2, 3))

    def line(self):
        self.spread(self.links.masks(self.links.rest))
        self.bits = []

    def step(self):
        self.spread((self.bits.pop(0),))


def on_device(
    links,
    layer_input,
    segment_ids,
    relative_buckets,
    first_gain,
    query_weight,
    key_weight,
    value_weight,
    output_projection,
    relative_table,
    second_gain,
    gate_weight,
    up_weight,
    down_projection,
    output_cotangent,
):
    size = links.size
    me = lax.axis_index("dp") * links.inner + lax.axis_index("fsdp")
    place = np.array([links.place(i) for i in range(links.count)], np.int32)
    source = jnp.asarray(np.argsort(place).astype(np.int32)) ^ me

    gains_shard = jnp.pad(jnp.stack([first_gain, second_gain], axis=1), ((0, 0), (0, BLK - 2)))
    w1, w2, w3 = PIECES
    feed_shards = (gate_weight, up_weight, down_projection)
    qkv_shards = (query_weight, key_weight, value_weight)
    triple = lambda lo, hi: tuple((n, lo, hi) for n in range(3))
    run = Order()
    segk = jnp.broadcast_to(segment_ids[:, None], (SEQ, BLK))
    segq = jnp.where(segment_ids > 0, segment_ids, -1).reshape(NB, BLK)
    spans = ranges(segment_ids)
    one_hot = (relative_buckets[::-1][:, None] == jnp.arange(BUCKETS)[None, :]).astype(BF)
    one_hot = jnp.pad(one_hot, ((0, 1), (0, 0)))
    offsets = lax.dot_general(relative_table, one_hot, (((0,), (1,)), ((), ())), preferred_element_type=F32)

    (first_shard,) = run(pack, qkv_shards + (gains_shard,), (triple(0, GROUP) + ((3, 0, BLK),),))
    first = Gather(links, run, first_shard)
    (second_shard,) = run(pack, qkv_shards + (output_projection,), (triple(GROUP, 2 * GROUP) + ((3, 0, D),),))
    cot, cott = run(prepare, output_cotangent, segk)
    meet(run, first)
    first.square()
    second = Gather(links, run, second_shard)
    early_shard, late_shard = run(
        pack,
        feed_shards,
        (tuple((n, lo, lo + w) for lo, w in ((0, w1), (w1, w2)) for n in range(3)), triple(w1 + w2, FF)),
    )
    early = lax.all_gather(early_shard, AXES, axis=0, tiled=True)
    strips = run(make_strips, offsets.reshape(HEADS // 2, 2, 2 * SEQ))
    meet(run, second)
    second.square()
    meet(run, first)
    lead_blocks = first.end()
    qkv0, att0, lse0, gains, normed, turned = run(attend, spans, source, segk, segq, strips, layer_input, lead_blocks, True)
    meet(run, second)
    next_blocks = second.end()
    late = lax.all_gather(late_shard, AXES, axis=0, tiled=True)
    qkv1, att1, lse1 = run(attend, spans, source, segk, segq, strips, normed, next_blocks, False)
    hidden, n2, n2t = run(hidden_units, source, att0, att1, layer_input, gains, next_blocks)
    acts = (n2, n2t, cot, cott)
    keep, send, *sums = run(feed, source, acts, early, 0, w1, None)
    s1 = Scatter(links, run, keep, send)
    meet(run, s1)
    s1.square()
    keep, send, *sums = run(feed, source, acts, early, 3 * w1, w2, sums)
    meet(run, s1)
    s2 = Scatter(links, run, keep, send)
    s1.step()
    meet(run, s2)
    s2.square()
    keep, send, block_output, hidden_grad, branch_t, attended_grad = run(
        feed, source, acts, late, 0, w3, sums, (hidden, gains, segk, next_blocks)
    )
    meet(run, s1, s2)
    s3 = Scatter(links, run, keep, send)
    s2.step()
    s1.step()
    meet(run, s3)
    s3.square()
    *g0, keep, send = run(
        attn_bwd, spans, source, segk, segq, strips, qkv0, attended_grad, lse0, turned, (branch_t, att0, att1), 0
    )
    meet(run, s1, s2, s3)
    s4 = Scatter(links, run, keep, send)
    s2.step()
    s3.step()
    meet(run, s4)
    s4.square()
    *g1, keep, send = run(attn_bwd, spans, source, segk, segq, strips, qkv1, attended_grad, lse1, turned, (), 4)
    meet(run, s2, s3, s4)
    s5 = Scatter(links, run, keep, send)
    offset_grads = jnp.concatenate([g0[3], g1[3]], axis=0).reshape(HEADS, 2 * SEQ)
    table_term = lax.dot_general(
        one_hot.astype(F32), offset_grads, (((0,), (1,)), ((), ())), precision=HIGHEST, preferred_element_type=F32
    )
    total = Total(links, run, table_term.reshape(-1, BLK))
    meet(run, s5, total)
    s5.square()
    s4.step()
    s3.step()
    total.step()
    input_gradient = run(
        last, source, layer_input, hidden_grad, gains, [*g0[:3], *g1[:3]], lead_blocks + next_blocks
    )
    meet(run, s3, s4, s5, total)
    s5.line()
    s4.step()
    total.step()
    meet(run, s4, s5)
    *grads, gain_grads = run(
        finish,
        [s.terms + s.got for s in (s4, s5, s1, s2, s3)],
        (query_weight, key_weight, value_weight, gate_weight, up_weight),
        gains_shard,
    )
    meet(run, total)
    table_gradient = total.x.reshape(BUCKETS, HEADS)
    return (block_output, input_gradient, *grads, gain_grads[:, 0], gain_grads[:, 1], table_gradient)


def solution(mesh):
    rows, flat, full = P(AXES, None), P(AXES), P()
    return jax.shard_map(
        functools.partial(on_device, Slice(mesh)),
        mesh=mesh,
        in_specs=(rows, flat, full, flat, rows, rows, rows, rows, full, flat, rows, rows, rows, rows),
        out_specs=(rows,) * 9 + (flat, flat, full),
        check_vma=False,
    )
```

```python
import functools

import jax
import jax.numpy as jnp
import numpy as np
from jax import lax
from jax.experimental import pallas as pl
from jax.experimental.pallas import tpu as pltpu
from jax.sharding import PartitionSpec as P

F32 = jnp.float32
BF = jnp.bfloat16
HEADS = 16
BUCKETS = 32
SEQ = 1024
D = 1024
FF = 2816
BLK = 128
NB = SEQ // BLK
STRIP = (2 * NB - 1) * BLK
EPS = 1e-06
NEG = -1e30
VLIM = 60 * 1024 * 1024
AXES = ("dp", "fsdp")
GROUP = 512
PIECES = (768, 1024, 1024)
TILE = 512
FT = 256
ANY = pl.BlockSpec(memory_space=pl.ANY)
SMEM = pl.BlockSpec(memory_space=pltpu.SMEM)
HIGHEST = lax.Precision.HIGHEST
RATE = 2e7
GELU_A = 0.7978845608028654
GELU_B = 0.044715


def params(grid=1):
    return pltpu.CompilerParams(vmem_limit_bytes=VLIM, dimension_semantics=("arbitrary",) * grid)


def cost(flops, moved, trans=0):
    return pl.CostEstimate(flops=int(flops), bytes_accessed=int(moved / 50), transcendentals=int(trans))


def after(kernel, used, deps):
    if not deps:
        return kernel
    return lambda *refs: kernel(*refs[:used], *refs[used + len(deps) :])


def nt(a,b): return lax.dot_general(a,b,(((1,),(1,)),((),())),preferred_element_type=F32)
def nn(a,b): return lax.dot_general(a,b,(((1,),(0,)),((),())),preferred_element_type=F32)

def build_strip(rev_ref, strip):
    for h in range(2):
        row=jnp.broadcast_to(rev_ref[h:h+1,:],(8,2*SEQ))
        base=pltpu.roll(row,0,1,stride=1,stride_axis=0)
        for m in range(BLK//8):
            turned=pltpu.roll(base,(8*m-(BLK-1))%(2*SEQ),1)
            for d in range(2*NB-1):
                e=2*NB-2-d
                strip[d*BLK+8*m:d*BLK+8*m+8,h*BLK:(h+1)*BLK]=turned[:,e*BLK:(e+1)*BLK]

def fold_strip(strip, out_ref):
    for h in range(2):
        total=jnp.zeros((8,2*SEQ),F32)
        for m in range(BLK//8):
            parts=[strip[(2*NB-2-e)*BLK+8*m:(2*NB-2-e)*BLK+8*m+8,h*BLK:(h+1)*BLK] for e in range(2*NB-1)]
            parts.append(jnp.zeros((8,BLK),F32))
            total=total+pltpu.roll(jnp.concatenate(parts,axis=1),(BLK-1-8*m)%(2*SEQ),1)
        row=total[0:1]
        for s in range(1,8):
            row=row+pltpu.roll(total[s:s+1],2*SEQ-s,1)
        out_ref[h:h+1,:]=row

def lanes_mask():
    lane=lax.broadcasted_iota(jnp.int32,(1,BLK),1)
    return lane<64

def stack_heads(x, first):
    zero=jnp.zeros_like(x)
    return jnp.concatenate([jnp.where(first,x,zero),jnp.where(first,zero,x)],axis=0)


def strip_kernel(rev_ref, strip):
    build_strip(rev_ref, strip)

def make_strips(rev, deps=()):
    return pl.pallas_call(after(strip_kernel, 1, deps),grid=(8,),
        in_specs=[pl.BlockSpec((None,2,2*SEQ),lambda p:(p,0,0))]+[ANY]*len(deps),
        out_specs=pl.BlockSpec((None,STRIP,2*BLK),lambda p:(p,0,0)),
        out_shape=jax.ShapeDtypeStruct((8,STRIP,2*BLK),F32),
        compiler_params=pltpu.CompilerParams(vmem_limit_bytes=VLIM),
        name="bias_strips")(rev, *deps)

def attn_fwd_kernel(UNIT, rng_ref, segk_ref, segq_ref, strip, qkv, o_ref, lse_ref, vt):
    first=lanes_mask()
    for u in range(UNIT):
        vt[u]=qkv[:,2*GROUP+u*BLK:2*GROUP+(u+1)*BLK].T
    mean=jnp.sum(qkv[:,2*GROUP:].astype(F32),axis=0,keepdims=True)*(1.0/SEQ)

    def block(qi, carry):
        q0=pl.multiple_of(qi*BLK,BLK)
        lo=rng_ref[qi]; width=rng_ref[NB+qi]
        k0=pl.multiple_of(lo*BLK,BLK)
        b0=pl.multiple_of((lo-qi+NB-1)*BLK,BLK)
        segq=segq_ref[pl.ds(qi,1),:]
        @pl.when(width==0)
        def _():
            o_ref[pl.ds(q0,BLK),:]=jnp.broadcast_to(mean,(BLK,UNIT*BLK)).astype(BF)
            for u in range(UNIT):
                lse_ref[u,pl.ds(qi,1),:]=jnp.zeros((1,2*BLK),F32)
        for w in range(1,NB+1):
            @pl.when(width==w)
            def _():
                rows=w*BLK
                allowed=segk_ref[pl.ds(k0,rows),:]==segq
                live_row=segq>0
                live_row=jnp.concatenate([live_row,live_row],axis=1)
                live_col=segk_ref[pl.ds(q0,BLK),:]>0
                units=[slice(u*BLK,(u+1)*BLK) for u in range(UNIT)]
                qcats=[stack_heads(qkv[pl.ds(q0,BLK),lanes],first) for lanes in units]
                scores=[nt(qkv[pl.ds(k0,rows),GROUP+lanes.start:GROUP+lanes.stop],qcat) for lanes,qcat in zip(units,qcats)]
                probs=[]; stats=[]; totals=[]
                for u in range(UNIT):
                    both=[]; stat=[]; tot=[]
                    s=scores[u]+strip[u,pl.ds(b0,rows),:]
                    for h in range(2):
                        sh=jnp.where(allowed,s[:,h*BLK:(h+1)*BLK],NEG)
                        peak=jnp.max(sh,axis=0,keepdims=True)
                        e=jnp.exp(sh-peak)
                        t=jnp.sum(e,axis=0,keepdims=True)
                        both.append(e.astype(BF)); stat.append(peak+jnp.log(t)); tot.append(t)
                    probs.append(jnp.concatenate(both,axis=1)); stats.append(jnp.concatenate(stat,axis=1)); totals.append(jnp.concatenate(tot,axis=1))
                ots=[nn(vt[u,:,pl.ds(k0,rows)],probs[u]) for u in range(UNIT)]
                for u,lanes in enumerate(units):
                    ot=ots[u]*(1.0/totals[u])
                    o=jnp.concatenate([ot[:64,:BLK],ot[64:,BLK:]],axis=0).T
                    o_ref[pl.ds(q0,BLK),lanes]=jnp.where(live_col,o,mean[:,lanes]).astype(BF)
                    lse_ref[u,pl.ds(qi,1),:]=jnp.where(live_row,stats[u],0.0)
        return carry
    lax.fori_loop(0,NB,block,0)

def attn_bwd_kernel(UNIT, rng_ref, segk_ref, segq_ref, strip, q_ref, k_ref, v_ref, g_ref, lse_ref,
                    dq_ref, dk_ref, dv_ref, off_ref, dstrip, kt, dk, dv):
    first=lanes_mask()
    dstrip[...]=jnp.zeros_like(dstrip)
    dk[...]=jnp.zeros_like(dk)
    for u in range(UNIT):
        lanes=slice(u*BLK,(u+1)*BLK)
        kt[u]=k_ref[:,lanes].T
        padded=jnp.where(segk_ref[...]>0,0.0,g_ref[:,lanes].astype(F32))
        dv[:,lanes]=jnp.broadcast_to(jnp.sum(padded,axis=0,keepdims=True)*(1.0/SEQ),(SEQ,BLK))

    def block(qi, carry):
        q0=pl.multiple_of(qi*BLK,BLK)
        lo=rng_ref[qi]; width=rng_ref[NB+qi]
        k0=pl.multiple_of(lo*BLK,BLK)
        b0=pl.multiple_of((lo-qi+NB-1)*BLK,BLK)
        segq=segq_ref[pl.ds(qi,1),:]
        @pl.when(width==0)
        def _():
            dq_ref[pl.ds(q0,BLK),:]=jnp.zeros((BLK,UNIT*BLK),BF)
        for w in range(1,NB+1):
            @pl.when(width==w)
            def _():
                rows=w*BLK
                allowed=segk_ref[pl.ds(k0,rows),:]==segq
                units=[slice(u*BLK,(u+1)*BLK) for u in range(UNIT)]
                qcats=[stack_heads(q_ref[pl.ds(q0,BLK),lanes],first) for lanes in units]
                gcats=[stack_heads(g_ref[pl.ds(q0,BLK),lanes],first) for lanes in units]
                scores=[nt(k_ref[pl.ds(k0,rows),lanes],qcat) for lanes,qcat in zip(units,qcats)]
                dps=[nt(v_ref[pl.ds(k0,rows),lanes],gcat) for lanes,gcat in zip(units,gcats)]
                probs=[]; grads=[]
                for u in range(UNIT):
                    lse=lse_ref[u,pl.ds(qi,1),:]
                    s=scores[u]+strip[u,pl.ds(b0,rows),:]
                    ps=[]; ds=[]
                    for h in range(2):
                        cols=slice(h*BLK,(h+1)*BLK)
                        prob=jnp.exp(jnp.where(allowed,s[:,cols],NEG)-lse[:,cols])
                        t=prob*dps[u][:,cols]
                        inner=jnp.sum(t,axis=0,keepdims=True)
                        d=t-prob*inner
                        dstrip[u,pl.ds(b0,rows),cols]+=d
                        ps.append(prob.astype(BF)); ds.append(d.astype(BF))
                    probs.append(jnp.concatenate(ps,axis=1)); grads.append(jnp.concatenate(ds,axis=1))
                for u,lanes in enumerate(units):
                    dv[pl.ds(k0,rows),lanes]+=nn(probs[u],gcats[u])
                dqts=[nn(kt[u,:,pl.ds(k0,rows)],grads[u]) for u in range(UNIT)]
                for u,lanes in enumerate(units):
                    dk[pl.ds(k0,rows),lanes]+=nn(grads[u],qcats[u])
                for u,lanes in enumerate(units):
                    dq_ref[pl.ds(q0,BLK),lanes]=jnp.concatenate([dqts[u][:64,:BLK],dqts[u][64:,BLK:]],axis=0).T.astype(BF)
        return carry
    lax.fori_loop(0,NB,block,0)
    dk_ref[...]=dk[...].astype(BF)
    dv_ref[...]=dv[...].astype(BF)
    for u in range(UNIT):
        fold_strip(dstrip.at[u], off_ref.at[u])

def backward_kernel(unit, lead, rng, source, segk, segq, strip, q, k, v, grad, lse, *refs):
    lefts, rights, refs = refs[: 1 + lead], refs[1 + lead : 1 + 3 * lead], refs[1 + 3 * lead :]
    dq, dk, dv, off, keep, send, dstrip, kt, dk_sum, dv_sum, held, sem = refs
    p = pl.program_id(0)

    @pl.when(p == 0)
    def _():
        for n, left in enumerate(lefts):
            order_rows(source, left, held.at[n], sem.at[n])

    attn_bwd_kernel(
        unit, rng, segk, segq, strip, q, k, v, grad, lse, dq, dk, dv, off, dstrip, kt, dk_sum, dv_sum
    )

    @pl.when(p == 0)
    def _():
        for n in range(1 + lead):
            wait_whole(held.at[n], sem.at[n])

    half, wide = D // 2, unit * BLK
    for j, right in enumerate((dq, dk, dv)):
        part = nn(held[0], right[...]).astype(BF)
        keep[:, j * wide : (j + 1) * wide] = part[:half]
        send[:, j * wide : (j + 1) * wide] = part[half:]
    for n, right in enumerate(rights):

        @pl.when(p == n)
        def _():
            for j in range(GROUP // wide):
                part = nn(held[1], right[:, j * wide : (j + 1) * wide]).astype(BF)
                cols = slice((3 + j) * wide, (4 + j) * wide)
                keep[:, cols] = part[:half]
                send[:, cols] = part[half:]


def attn_bwd(rng, source, segk, segq, strips, qkv, g, lse, turned, more, first_pair):
    unit, steps = 2, 2
    wide = unit * BLK
    lead = int(len(more) > 0)
    f = first_pair // unit
    c = lambda o: pl.BlockSpec((SEQ, wide), lambda p, r, s: (0, o + p))
    whole = lambda *s: pl.BlockSpec(s, lambda p, r, s: (0, 0))
    width = 3 * wide + lead * GROUP
    out = pl.BlockSpec((D // 2, width), lambda p, r, s: (0, p))
    gs = pltpu.PrefetchScalarGridSpec(
        num_scalar_prefetch=2,
        grid=(steps,),
        in_specs=[
            whole(SEQ, BLK), whole(NB, BLK),
            pl.BlockSpec((unit, STRIP, 2 * BLK), lambda p, r, s: (f + p, 0, 0)),
            c(0), c(steps), c(2 * steps), c(f),
            pl.BlockSpec((unit, NB, 2 * BLK), lambda p, r, s: (p, 0, 0)),
        ] + [ANY] * (1 + lead) + [whole(SEQ, GROUP)] * (2 * lead),
        out_specs=[c(0), c(0), c(0), pl.BlockSpec((unit, 2, 2 * SEQ), lambda p, r, s: (p, 0, 0)), out, out],
        scratch_shapes=[
            pltpu.VMEM((unit, STRIP, 2 * BLK), F32), pltpu.VMEM((unit, BLK, SEQ), BF),
            pltpu.VMEM((SEQ, wide), F32), pltpu.VMEM((SEQ, wide), F32),
            pltpu.VMEM((1 + lead, D, SEQ), BF), pltpu.SemaphoreType.DMA((1 + lead,)),
        ],
    )
    sh = jax.ShapeDtypeStruct((SEQ, steps * wide), BF)
    term = jax.ShapeDtypeStruct((D // 2, steps * width), BF)
    return pl.pallas_call(
        functools.partial(backward_kernel, unit, lead),
        grid_spec=gs,
        out_shape=[sh, sh, sh, jax.ShapeDtypeStruct((steps * unit, 2, 2 * SEQ), F32), term, term],
        compiler_params=params(),
        cost_estimate=cost(24 * RATE, 16 * SEQ * wide * 2),
        name="attention_backward",
    )(rng, source, segk, segq, strips, qkv, qkv, qkv, g, lse, turned, *more)


def ranges(seg):
    s=seg.reshape(NB,BLK)
    least=s[:,0]; most=jnp.max(s,axis=1)
    lo=jnp.sum((most[None,:]<least[:,None])&(least[None,:]>0),axis=1)
    hi=jnp.sum((least[None,:]<=most[:,None])&(least[None,:]>0),axis=1)
    w=jnp.where(least>0,hi-lo,0)
    return jnp.concatenate([jnp.where(least>0,lo,0),w]).astype(jnp.int32)


def prep_kernel(c_ref, seg_ref, out_ref, turned_ref):
    low = jnp.where(jnp.concatenate([seg_ref[...] > 0] * (D // BLK), axis=1), c_ref[...].astype(F32), 0.0).astype(BF)
    out_ref[...] = low
    turned_ref[...] = low.T


def prepare(c, segk):
    rows = 256
    blk = pl.BlockSpec((rows, D), lambda i: (i, 0))
    return pl.pallas_call(
        prep_kernel,
        grid=(SEQ // rows,),
        in_specs=[blk, pl.BlockSpec((rows, BLK), lambda i: (i, 0))],
        out_specs=[blk, pl.BlockSpec((D, rows), lambda i: (0, i))],
        out_shape=[jax.ShapeDtypeStruct((SEQ, D), BF), jax.ShapeDtypeStruct((D, SEQ), BF)],
        compiler_params=params(),
        cost_estimate=cost(4 * RATE, 6 * SEQ * D),
        name="prepare",
    )(c, segk)


def pack_kernel(spans, count, *refs):
    ins, outs = refs[:count], refs[count:]
    for out, cols in zip(outs, spans):
        at = 0
        for n, lo, hi in cols:
            out[:, at : at + hi - lo] = ins[n][:, lo:hi]
            at += hi - lo


def pack(shards, spans, deps=()):
    rows = shards[0].shape[0]
    widths = [sum(hi - lo for _, lo, hi in cols) for cols in spans]
    whole = pl.BlockSpec(memory_space=pltpu.VMEM)
    return pl.pallas_call(
        after(functools.partial(pack_kernel, spans, len(shards)), len(shards), deps),
        in_specs=[whole] * len(shards) + [ANY] * len(deps),
        out_specs=[whole] * len(widths),
        out_shape=[jax.ShapeDtypeStruct((rows, w), BF) for w in widths],
        name="pack_shards",
    )(*shards, *deps)


def join(*parts):
    return jnp.concatenate(parts, axis=0)


def add_terms(terms, rows):
    return sum(t[off : off + rows].astype(F32) for t, off in terms).astype(BF)


def finish_kernel(counts, *refs):
    weights, gains, refs = refs[:5], refs[5], refs[6:]
    sums, at = [], 0
    for n in counts:
        total = refs[at][...].astype(F32)
        for ref in refs[at + 1 : at + n]:
            total = total + ref[...].astype(F32)
        sums.append(total)
        at += n
    outs = refs[at:]
    wide = GROUP // 2
    for g, step in ((0, 3 * wide + GROUP), (1, 3 * wide)):
        for p in range(2):
            for j in range(3):
                col = g * GROUP + p * wide
                outs[j][:, col : col + wide] = sums[g][:, p * step + j * wide : p * step + (j + 1) * wide]
    for p in range(2):
        start = (p + 1) * (3 * wide + GROUP) - GROUP
        outs[3][:, p * GROUP : (p + 1) * GROUP] = sums[0][:, start : start + GROUP]
    at = 0
    for s, width in zip(sums[2:], PIECES):
        for j in range(3):
            outs[4 + j][:, at : at + width] = s[:, j * width : (j + 1) * width]
        at += width
    match = lambda w, out: jnp.sum(w[...].astype(F32) * out[...], axis=1, keepdims=True)
    one = match(weights[0], outs[0]) + match(weights[1], outs[1]) + match(weights[2], outs[2])
    two = match(weights[3], outs[4]) + match(weights[4], outs[5])
    lane = lax.broadcasted_iota(jnp.int32, gains.shape, 1)
    outs[7][...] = jnp.where(lane == 0, one, two) / jnp.where(lane < 2, gains[...].astype(F32), 1.0)


def finish(sets, weights, gains):
    rows = gains.shape[0]
    flat = [x for terms in sets for x in terms]
    widths = (D,) * 4 + (FF,) * 3 + (BLK,)
    top = lambda w: pl.BlockSpec((rows, w), lambda i: (0, 0))
    return pl.pallas_call(
        functools.partial(finish_kernel, tuple(len(t) for t in sets)),
        grid=(1,),
        in_specs=[top(x.shape[1]) for x in (*weights, gains, *flat)],
        out_specs=[top(w) for w in widths],
        out_shape=[jax.ShapeDtypeStruct((rows, w), F32) for w in widths],
        compiler_params=params(),
        name="weight_gradients",
    )(*weights, gains, *flat)


def place_blocks(source_ref, blocks, start, cols, dst, at, sem):
    rows = blocks[0].shape[0]
    size = D // source_ref.shape[0]
    per = rows // size
    for n, ref in enumerate(blocks):

        def one(i, carry):
            row = pl.multiple_of(source_ref[n * per + i] * size, size)
            pltpu.make_async_copy(
                ref.at[pl.ds(pl.multiple_of(i * size, size), size), pl.ds(start, cols)],
                dst.at[pl.ds(row, size), pl.ds(at, cols)],
                sem,
            ).start()
            return carry

        lax.fori_loop(0, per, one, 0)


def wait_whole(dst, sem):
    pltpu.make_async_copy(dst, dst, sem).wait()


def order_rows(source_ref, src, dst, sem):
    size = D // source_ref.shape[0]

    def one(p, carry):
        row = pl.multiple_of(source_ref[p] * size, size)
        pltpu.make_async_copy(
            src.at[pl.ds(row, size)], dst.at[pl.ds(pl.multiple_of(p * size, size), size)], sem
        ).start()
        return carry

    lax.fori_loop(0, D // size, one, 0)


def scaled_rows(x):
    return lax.rsqrt(jnp.mean(x * x, axis=-1, keepdims=True) + EPS)


def attend_kernel(lead, first_pair, *refs):
    rng, source, segk, segq, x, strips = refs[:6]
    blocks, refs = refs[6:14], refs[14:]
    if lead:
        qkv_out, o_ref, lse_ref, gains_ref, normed_out, turned_out = refs[:6]
        qkv, w, strip, normed, vt, sem, turned = refs[6:]
    else:
        qkv_out, o_ref, lse_ref = refs[:3]
        qkv, w, strip, normed, vt, sem = refs[3:]
    unit = vt.shape[0]
    bring = pltpu.make_async_copy(x, normed, sem.at[0])
    bring.start()
    place_blocks(source, blocks, 0, w.shape[1], w, 0, sem.at[1])
    pads = pltpu.make_async_copy(strips.at[pl.ds(first_pair, unit)], strip, sem.at[2])
    pads.start()
    outs = [pltpu.make_async_copy(qkv, qkv_out, sem.at[3])]
    bring.wait()
    wait_whole(w, sem.at[1])
    if lead:
        gains_ref[...] = w[:, 3 * GROUP :].astype(F32).T[:8]

        def rows_of(i, carry):
            at = pl.multiple_of(i * 256, 256)
            rows = normed[pl.ds(at, 256), :].astype(F32)
            low = (rows * scaled_rows(rows) * gains_ref[0:1, :]).astype(BF)
            normed[pl.ds(at, 256), :] = low
            turned[:, pl.ds(at, 256)] = low.T
            return carry

        lax.fori_loop(0, SEQ // 256, rows_of, 0)
        outs += [pltpu.make_async_copy(normed, normed_out, sem.at[4]), pltpu.make_async_copy(turned, turned_out, sem.at[5])]
        for c in outs[1:]:
            c.start()

    def columns(j, carry):
        cols = pl.ds(pl.multiple_of(j * FT, FT), FT)
        qkv[:, cols] = nn(normed[...], w[:, cols]).astype(BF)
        return carry

    lax.fori_loop(0, 3 * GROUP // FT, columns, 0)
    outs[0].start()
    pads.wait()
    attn_fwd_kernel(unit, rng, segk, segq, strip, qkv, o_ref, lse_ref, vt)
    for c in outs:
        c.wait()


def attend(rng, source, segk, segq, strips, x, blocks, lead):
    unit = 4
    width = 3 * GROUP + (BLK if lead else 0)
    vmem = pl.BlockSpec(memory_space=pltpu.VMEM)
    shape = lambda t, *s: jax.ShapeDtypeStruct(s, t)
    out_specs = [ANY, vmem, vmem] + ([vmem, ANY, ANY] if lead else [])
    out_shape = [shape(BF, SEQ, 3 * GROUP), shape(BF, SEQ, GROUP), shape(F32, unit, NB, 2 * BLK)]
    out_shape += [shape(F32, 8, D), shape(BF, SEQ, D), shape(BF, D, SEQ)] if lead else []
    return pl.pallas_call(
        functools.partial(attend_kernel, lead, 0 if lead else unit),
        in_specs=[SMEM, SMEM, vmem, vmem, ANY, ANY] + [ANY] * len(blocks),
        out_specs=out_specs,
        out_shape=out_shape,
        scratch_shapes=[
            pltpu.VMEM((SEQ, 3 * GROUP), BF), pltpu.VMEM((D, width), BF), pltpu.VMEM((unit, STRIP, 2 * BLK), F32),
            pltpu.VMEM((SEQ, D), BF), pltpu.VMEM((unit, BLK, SEQ), BF), pltpu.SemaphoreType.DMA((6,)),
        ] + ([pltpu.VMEM((D, SEQ), BF)] if lead else []),
        compiler_params=pltpu.CompilerParams(vmem_limit_bytes=VLIM),
        cost_estimate=cost(20 * RATE, 2 * D * width + 4 * SEQ * D),
        name="attention_forward",
    )(rng, source, segk, segq, x, strips, *blocks)


def hidden_kernel(*refs):
    source, a0, a1, x_ref, gains_ref = refs[:5]
    h_ref, n2_ref, n2t_ref, w, sem = refs[13:]

    @pl.when(pl.program_id(0) == 0)
    def _():
        place_blocks(source, refs[5:13], 3 * GROUP, D, w, 0, sem.at[0])
        wait_whole(w, sem.at[0])

    hidden = x_ref[...].astype(F32) + nt(jnp.concatenate([a0[...], a1[...]], axis=1), w[...])
    h_ref[...] = hidden
    normed = (hidden * scaled_rows(hidden) * gains_ref[1:2, :]).astype(BF)
    n2_ref[...] = normed
    n2t_ref[...] = normed.T


def hidden_units(source, a0, a1, x, gains, blocks):
    rows = TILE
    tok = lambda c: pl.BlockSpec((rows, c), lambda i: (i, 0))
    return pl.pallas_call(
        hidden_kernel,
        grid=(SEQ // rows,),
        in_specs=[SMEM, tok(GROUP), tok(GROUP), tok(D), pl.BlockSpec((8, D), lambda i: (0, 0))] + [ANY] * len(blocks),
        out_specs=[tok(D), tok(D), pl.BlockSpec((D, rows), lambda i: (0, i))],
        out_shape=[
            jax.ShapeDtypeStruct((SEQ, D), F32),
            jax.ShapeDtypeStruct((SEQ, D), BF),
            jax.ShapeDtypeStruct((D, SEQ), BF),
        ],
        scratch_shapes=[pltpu.VMEM((D, D), BF), pltpu.SemaphoreType.DMA((1,))],
        compiler_params=params(),
        cost_estimate=cost(6 * RATE, 16 * SEQ * D),
        name="hidden_units",
    )(source, a0, a1, x, gains, *blocks)


def feed_kernel(lead, final, width, base, *refs):
    source, n2, n2t, cot, cott, whole = refs[:6]
    refs = refs[6:]
    sums_from = () if lead else refs[:2]
    refs = refs[len(sums_from) :]
    if final:
        h_in, gains_ref, seg_in, blocks, refs = refs[0], refs[1], refs[2], refs[3:11], refs[11:]
    keep, send = refs[:2]
    outs, refs = (refs[2:6], refs[6:]) if final else (refs[2:4], refs[4:])
    n2_v, n2t_v, cot_v, cott_v, w, stage, bo, ng, mix_v, gu_v, sem_w, sem_o, sem_i = refs[:13]
    half = D // 2
    tiles = width // FT

    def weight_copies(f):
        out = []
        for j in range(3):
            col = pl.multiple_of(j * width + f * FT, FT)
            out.append(
                pltpu.make_async_copy(
                    whole.at[:, pl.ds(pl.multiple_of(base + col, BLK), FT)], w.at[:, pl.ds(col, FT)], sem_w.at[f, j]
                )
            )
        return out

    def term_copies(g):
        col = pl.multiple_of(g * FT, FT)
        return [
            pltpu.make_async_copy(
                stage.at[pl.ds(s * half, half), pl.ds(col, FT)], dst.at[:, pl.ds(col, FT)], sem_o.at[g, s]
            )
            for s, dst in enumerate((keep, send))
        ]

    first = [pltpu.make_async_copy(n2, n2_v, sem_i.at[0]), pltpu.make_async_copy(cot, cot_v, sem_i.at[1])]
    sums_in = [pltpu.make_async_copy(a, b, sem_i.at[4 + n]) for n, (a, b) in enumerate(zip(sums_from, (bo, ng)))]
    if final:
        h_v, wo, ag_v, bt_v, out_v, seg_v = refs[13:]
        sums_in += [pltpu.make_async_copy(h_in, h_v, sem_i.at[6]), pltpu.make_async_copy(seg_in, seg_v, sem_i.at[7])]
        sources = (out_v, ng, bt_v, ag_v)
    else:
        sources = (bo, ng)
    results = [pltpu.make_async_copy(a, b, sem_i.at[8 + n]) for n, (a, b) in enumerate(zip(sources, outs))]
    for c in weight_copies(0) + first:
        c.start()
    for c in first:
        c.wait()
    for f in range(1, tiles):
        for c in weight_copies(f):
            c.start()
    for c in sums_in:
        c.start()

    def units(f, carry):
        for c in weight_copies(f):
            c.wait()
        at = [pl.ds(pl.multiple_of(j * width + f * FT, FT), FT) for j in range(3)]

        gate = nn(n2_v[...], w[:, at[0]])
        upward = nn(n2_v[...], w[:, at[1]])
        mixed_grad = nn(cot_v[...], w[:, at[2]])
        square = gate * gate
        bend = jnp.tanh(gate * (GELU_A + (GELU_A * GELU_B) * square))
        curve = 0.5 * (1.0 + bend)
        active = gate * curve
        slope = curve + (0.5 * gate) * (1.0 - bend * bend) * (GELU_A + (3.0 * GELU_A * GELU_B) * square)
        mix_v[:, at[0]] = (active * upward).astype(BF)
        gu_v[:, at[0]] = (mixed_grad * upward * slope).astype(BF)
        gu_v[:, at[1]] = (mixed_grad * active).astype(BF)
        return carry

    lax.fori_loop(0, tiles, units, 0)
    order_rows(source, n2t, n2t_v, sem_i.at[2])
    order_rows(source, cott, cott_v, sem_i.at[3])
    if final:
        place_blocks(source, blocks, 3 * GROUP, D, wo, 0, sem_i.at[13])
    for c in sums_in:
        c.wait()

    for j in range(D // FT):
        cols = slice(j * FT, (j + 1) * FT)
        one = nt(mix_v[...], w[cols, 2 * width :])
        two = nt(gu_v[...], w[cols, : 2 * width])
        bo[:, cols] = one if lead else bo[:, cols] + one
        ng[:, cols] = two if lead else ng[:, cols] + two
    if final:
        wait_whole(wo, sem_i.at[13])

        def close(i, carry):
            rows = pl.ds(pl.multiple_of(i * 256, 256), 256)
            hidden = h_v[rows, :]
            live = jnp.concatenate([seg_v[rows, :] > 0] * (D // BLK), axis=1)
            out_v[rows, :] = jnp.where(live, hidden + bo[rows, :], 0.0).astype(BF)
            grad = ng[rows, :]
            scale = scaled_rows(hidden)
            grad = grad * gains_ref[1:2, :]
            mean = jnp.mean(grad * hidden, axis=-1, keepdims=True)
            out = cot_v[rows, :].astype(F32) + (scale * grad - hidden * (scale * scale * scale * mean))
            ng[rows, :] = out
            low = out.astype(BF)
            mix_low[rows, :] = low
            bt_v[:, rows] = low.T
            return carry

        mix_low = n2_v
        lax.fori_loop(0, SEQ // 256, close, 0)

        def attended(i, carry):
            cols = pl.ds(pl.multiple_of(i * FT, FT), FT)
            ag_v[:, cols] = nn(mix_low[...], wo[:, cols]).astype(BF)
            return carry

        lax.fori_loop(0, D // FT, attended, 0)
    for c in results:
        c.start()
    wait_whole(n2t_v, sem_i.at[2])
    wait_whole(cott_v, sem_i.at[3])

    def term(left, right, f, start):
        cols = pl.ds(pl.multiple_of(f * FT, FT), FT)
        out = pl.ds(pl.multiple_of((start + f) * FT, FT), FT)
        stage[:, out] = nn(left[...], right[:, cols]).astype(BF)
        for c in term_copies(start + f):
            c.start()

    def pair(f, carry):
        term(n2t_v, gu_v, 2 * f, 0)
        term(n2t_v, gu_v, 2 * f + 1, 0)
        return carry

    lax.fori_loop(0, tiles, pair, 0)
    for f in range(tiles):
        term(cott_v, mix_v, f, 2 * tiles)
    for c in results:
        c.wait()

    def drain(g, carry):
        for c in term_copies(g):
            c.wait()
        return carry

    lax.fori_loop(0, 3 * tiles, drain, 0)


def feed(source, acts, whole, base, width, sums, closing=None):
    lead, final = sums is None, closing is not None
    tiles = width // FT
    args = [source, *acts, whole] + ([] if lead else list(sums))
    specs = [SMEM] + [ANY] * (len(args) - 1)
    if final:
        hidden, gains, segk, blocks = closing
        args += [hidden, gains, segk, *blocks]
        specs += [ANY, pl.BlockSpec(memory_space=pltpu.VMEM), ANY] + [ANY] * len(blocks)
    half = jax.ShapeDtypeStruct((D // 2, 3 * width), BF)
    shape = lambda t, *s: jax.ShapeDtypeStruct(s, t)
    total = shape(F32, SEQ, D)
    outs = [shape(BF, SEQ, D), total, shape(BF, D, SEQ), shape(BF, SEQ, D)] if final else [total, total]
    bf = lambda *s: pltpu.VMEM(s, BF)
    scratch = [
        bf(SEQ, D), bf(D, SEQ), bf(SEQ, D), bf(D, SEQ), bf(D, 3 * width), bf(D, 3 * width),
        pltpu.VMEM((SEQ, D), F32), pltpu.VMEM((SEQ, D), F32),
        bf(SEQ, width), bf(SEQ, 2 * width),
        pltpu.SemaphoreType.DMA((tiles, 3)), pltpu.SemaphoreType.DMA((3 * tiles, 2)), pltpu.SemaphoreType.DMA((14,)),
    ]
    if final:
        scratch += [
            pltpu.VMEM((SEQ, D), F32), bf(D, D), bf(SEQ, D), bf(D, SEQ), bf(SEQ, D),
            pltpu.VMEM((SEQ, BLK), jnp.int32),
        ]
    return pl.pallas_call(
        functools.partial(feed_kernel, lead, final, width, base),
        in_specs=specs,
        out_specs=[ANY] * (2 + len(outs)),
        out_shape=[half, half] + outs,
        scratch_shapes=scratch,
        compiler_params=pltpu.CompilerParams(vmem_limit_bytes=VLIM),
        cost_estimate=cost((30 * width / 1024 + (6 if final else 0)) * RATE, 12 * D * width + 24 * SEQ * D, SEQ * width),
        name="feed_forward",
    )(*args)


def last_kernel(count, *refs):
    source, x_ref, hg_ref, gains_ref = refs[:4]
    grads = refs[4 : 4 + count]
    blocks = refs[4 + count : 20 + count]
    out_ref, w, sem = refs[-3:]
    half = 3 * GROUP

    @pl.when(pl.program_id(0) == 0)
    def _():
        for n in range(2):
            place_blocks(source, blocks[8 * n : 8 * n + 8], 0, half, w, n * half, sem.at[n])
        for n in range(2):
            wait_whole(w.at[:, pl.ds(n * half, half)], sem.at[n])

    grad = nt(jnp.concatenate([g[...] for g in grads], axis=1), w[...])
    x = x_ref[...].astype(F32)
    scale = scaled_rows(x)
    grad = grad * gains_ref[0:1, :]
    mean = jnp.mean(grad * x, axis=-1, keepdims=True)
    out_ref[...] = hg_ref[...] + (scale * grad - x * (scale * scale * scale * mean))


def last(source, x, hg, gains, grads, blocks):
    rows = 256
    tok = lambda c: pl.BlockSpec((rows, c), lambda i: (i, 0))
    whole = pl.BlockSpec((8, D), lambda i: (0, 0))
    return pl.pallas_call(
        functools.partial(last_kernel, len(grads)),
        grid=(SEQ // rows,),
        in_specs=[SMEM, tok(D), tok(D), whole] + [tok(g.shape[1]) for g in grads] + [ANY] * len(blocks),
        out_specs=tok(D),
        out_shape=jax.ShapeDtypeStruct((SEQ, D), F32),
        scratch_shapes=[pltpu.VMEM((D, 6 * GROUP), BF), pltpu.SemaphoreType.DMA((2,))],
        compiler_params=params(),
        cost_estimate=cost(14 * RATE, 14 * SEQ * D),
        name="input_gradient",
    )(source, x, hg, gains, *grads, *blocks)


class Slice:
    def __init__(self, mesh):
        self.count = mesh.shape["dp"] * mesh.shape["fsdp"]
        self.inner = mesh.shape["fsdp"]
        self.core = self.inner
        bits = [1 << b for b in range(self.count.bit_length() - 1)]
        self.rest = [b for b in reversed(bits) if b not in (1, 2, self.core)]
        self.order = [self.core, 2, 1] + self.rest[::-1]
        self.size = D // self.count

    def place(self, index):
        p = index * 0
        for b in self.order:
            p = 2 * p + (index // b) % 2
        return p

    def swap(self, x, bit):
        return lax.ppermute(x, AXES, [(i, i ^ bit) for i in range(self.count)])

    @staticmethod
    def masks(bits):
        return [sum(b for j, b in enumerate(bits) if n >> j & 1) for n in range(1, 1 << len(bits))]


class Order:
    def __init__(self):
        self.token = None

    def hold(self, args):
        leaves, tree = jax.tree.flatten(args)
        at = [i for i, x in enumerate(leaves) if hasattr(x, "aval")]
        if self.token is not None:
            held = lax.optimization_barrier([leaves[i] for i in at] + [self.token])
            for i, x in zip(at, held):
                leaves[i] = x
        return jax.tree.unflatten(tree, leaves)

    def __call__(self, f, *args):
        out = f(*self.hold(args))
        self.token = jax.tree.leaves(out)[0]
        return out


class Chain:
    def __init__(self, links, run):
        self.links, self.run, self.pending = links, run, []


def meet(run, *chains):
    arrays = run.hold([c.pending for c in chains] + [run.token])
    run.token = arrays.pop()
    for c, got in zip(chains, arrays):
        c.met(got)
        c.pending = []


class Gather(Chain):
    def __init__(self, links, run, shard):
        super().__init__(links, run)
        self.line = run.hold(shard)
        self.pending = [links.swap(self.line, m) for m in links.masks(links.rest)]

    def met(self, got):
        self.got = got

    def square(self):
        self.line = self.run(join, self.line, *self.got)
        self.others = [self.links.swap(self.line, self.links.core)]
        self.pending = [self.links.swap(self.line, m) for m in (1, 2, 3)]

    def end(self):
        self.others += [self.links.swap(b, self.links.core) for b in self.got]
        return (self.line, *self.got, *self.others)


class Total(Chain):
    def __init__(self, links, run, x):
        super().__init__(links, run)
        self.x = run.hold(x)
        self.groups = [links.masks(b) for b in (links.rest, [1, 2], [links.core])]
        self.step()

    def met(self, got):
        self.x = self.x + sum(got)

    def step(self):
        self.pending = [self.links.swap(self.x, m) for m in self.groups.pop(0)]


class Scatter(Chain):
    def __init__(self, links, run, keep, send):
        super().__init__(links, run)
        self.terms, self.rows, self.bits = [keep], D // 2, links.rest[::-1]
        self.pending = [links.swap(run.hold(send), links.core)]

    def met(self, got):
        self.got = got

    def spread(self, masks):
        self.terms += self.got
        rows = self.rows // (len(masks) + 1)
        self.pending = []
        for n in list(range(len(masks)))[::-1]:
            send = self.run(add_terms, [(t, (n + 1) * rows) for t in self.terms], rows)
            self.pending.insert(0, self.links.swap(send, masks[n]))
        self.rows = rows

    def square(self):
        self.spread((1, 2, 3))

    def line(self):
        self.spread(self.links.masks(self.links.rest))
        self.bits = []

    def step(self):
        self.spread((self.bits.pop(0),))


def on_device(
    links,
    layer_input,
    segment_ids,
    relative_buckets,
    first_gain,
    query_weight,
    key_weight,
    value_weight,
    output_projection,
    relative_table,
    second_gain,
    gate_weight,
    up_weight,
    down_projection,
    output_cotangent,
):
    size = links.size
    me = lax.axis_index("dp") * links.inner + lax.axis_index("fsdp")
    place = np.array([links.place(i) for i in range(links.count)], np.int32)
    source = jnp.asarray(np.argsort(place).astype(np.int32)) ^ me

    gains_shard = jnp.pad(jnp.stack([first_gain, second_gain], axis=1), ((0, 0), (0, BLK - 2)))
    w1, w2, w3 = PIECES
    feed_shards = (gate_weight, up_weight, down_projection)
    qkv_shards = (query_weight, key_weight, value_weight)
    triple = lambda lo, hi: tuple((n, lo, hi) for n in range(3))
    run = Order()
    segk = jnp.broadcast_to(segment_ids[:, None], (SEQ, BLK))
    segq = jnp.where(segment_ids > 0, segment_ids, -1).reshape(NB, BLK)
    spans = ranges(segment_ids)
    one_hot = (relative_buckets[::-1][:, None] == jnp.arange(BUCKETS)[None, :]).astype(BF)
    one_hot = jnp.pad(one_hot, ((0, 1), (0, 0)))
    offsets = lax.dot_general(relative_table, one_hot, (((0,), (1,)), ((), ())), preferred_element_type=F32)

    (first_shard,) = run(pack, qkv_shards + (gains_shard,), (triple(0, GROUP) + ((3, 0, BLK),),))
    first = Gather(links, run, first_shard)
    (second_shard,) = run(pack, qkv_shards + (output_projection,), (triple(GROUP, 2 * GROUP) + ((3, 0, D),),))
    cot, cott = run(prepare, output_cotangent, segk)
    meet(run, first)
    first.square()
    second = Gather(links, run, second_shard)
    early_shard, late_shard = run(
        pack,
        feed_shards,
        (tuple((n, lo, lo + w) for lo, w in ((0, w1), (w1, w2)) for n in range(3)), triple(w1 + w2, FF)),
    )
    early = lax.all_gather(early_shard, AXES, axis=0, tiled=True)
    strips = run(make_strips, offsets.reshape(HEADS // 2, 2, 2 * SEQ))
    meet(run, second)
    second.square()
    meet(run, first)
    lead_blocks = first.end()
    qkv0, att0, lse0, gains, normed, turned = run(attend, spans, source, segk, segq, strips, layer_input, lead_blocks, True)
    meet(run, second)
    next_blocks = second.end()
    late = lax.all_gather(late_shard, AXES, axis=0, tiled=True)
    qkv1, att1, lse1 = run(attend, spans, source, segk, segq, strips, normed, next_blocks, False)
    hidden, n2, n2t = run(hidden_units, source, att0, att1, layer_input, gains, next_blocks)
    acts = (n2, n2t, cot, cott)
    keep, send, *sums = run(feed, source, acts, early, 0, w1, None)
    s1 = Scatter(links, run, keep, send)
    meet(run, s1)
    s1.square()
    keep, send, *sums = run(feed, source, acts, early, 3 * w1, w2, sums)
    meet(run, s1)
    s2 = Scatter(links, run, keep, send)
    s1.step()
    meet(run, s2)
    s2.square()
    keep, send, block_output, hidden_grad, branch_t, attended_grad = run(
        feed, source, acts, late, 0, w3, sums, (hidden, gains, segk, next_blocks)
    )
    meet(run, s1, s2)
    s3 = Scatter(links, run, keep, send)
    s2.step()
    s1.step()
    meet(run, s3)
    s3.square()
    *g0, keep, send = run(
        attn_bwd, spans, source, segk, segq, strips, qkv0, attended_grad, lse0, turned, (branch_t, att0, att1), 0
    )
    meet(run, s1, s2, s3)
    s4 = Scatter(links, run, keep, send)
    s2.step()
    s3.step()
    meet(run, s4)
    s4.square()
    *g1, keep, send = run(attn_bwd, spans, source, segk, segq, strips, qkv1, attended_grad, lse1, turned, (), 4)
    meet(run, s2, s3, s4)
    s5 = Scatter(links, run, keep, send)
    offset_grads = jnp.concatenate([g0[3], g1[3]], axis=0).reshape(HEADS, 2 * SEQ)
    table_term = lax.dot_general(
        one_hot.astype(F32), offset_grads, (((0,), (1,)), ((), ())), precision=HIGHEST, preferred_element_type=F32
    )
    total = Total(links, run, table_term.reshape(-1, BLK))
    meet(run, s5, total)
    s5.square()
    s4.step()
    s3.step()
    total.step()
    input_gradient = run(
        last, source, layer_input, hidden_grad, gains, [*g0[:3], *g1[:3]], lead_blocks + next_blocks
    )
    meet(run, s3, s4, s5, total)
    s5.line()
    s4.step()
    total.step()
    meet(run, s4, s5)
    *grads, gain_grads = run(
        finish,
        [s.terms + s.got for s in (s4, s5, s1, s2, s3)],
        (query_weight, key_weight, value_weight, gate_weight, up_weight),
        gains_shard,
    )
    meet(run, total)
    table_gradient = total.x.reshape(BUCKETS, HEADS)
    return (block_output, input_gradient, *grads, gain_grads[:, 0], gain_grads[:, 1], table_gradient)


def solution(mesh):
    rows, flat, full = P(AXES, None), P(AXES), P()
    return jax.shard_map(
        functools.partial(on_device, Slice(mesh)),
        mesh=mesh,
        in_specs=(rows, flat, full, flat, rows, rows, rows, rows, full, flat, rows, rows, rows, rows),
        out_specs=(rows,) * 9 + (flat, flat, full),
        check_vma=False,
    )
```

```python
import functools

import jax
import jax.numpy as jnp
import numpy as np
from jax import lax
from jax.experimental import pallas as pl
from jax.experimental.pallas import tpu as pltpu
from jax.sharding import PartitionSpec as P

F32 = jnp.float32
BF = jnp.bfloat16
HEADS = 16
BUCKETS = 32
SEQ = 1024
D = 1024
FF = 2816
BLK = 128
NB = SEQ // BLK
STRIP = (2 * NB - 1) * BLK
EPS = 1e-06
NEG = -1e30
VLIM = 60 * 1024 * 1024
AXES = ("dp", "fsdp")
GROUP = 512
PIECES = (512, 1280, 1024)
TILE = 512
FT = 256
ANY = pl.BlockSpec(memory_space=pl.ANY)
SMEM = pl.BlockSpec(memory_space=pltpu.SMEM)
HIGHEST = lax.Precision.HIGHEST
RATE = 2e7
GELU_A = 0.7978845608028654
GELU_B = 0.044715


def params(grid=1):
    return pltpu.CompilerParams(vmem_limit_bytes=VLIM, dimension_semantics=("arbitrary",) * grid)


def cost(flops, moved, trans=0):
    return pl.CostEstimate(flops=int(flops), bytes_accessed=int(moved / 50), transcendentals=int(trans))


def after(kernel, used, deps):
    if not deps:
        return kernel
    return lambda *refs: kernel(*refs[:used], *refs[used + len(deps) :])


def nt(a,b): return lax.dot_general(a,b,(((1,),(1,)),((),())),preferred_element_type=F32)
def nn(a,b): return lax.dot_general(a,b,(((1,),(0,)),((),())),preferred_element_type=F32)

def build_strip(rev_ref, strip):
    for h in range(2):
        row=jnp.broadcast_to(rev_ref[h:h+1,:],(8,2*SEQ))
        base=pltpu.roll(row,0,1,stride=1,stride_axis=0)
        for m in range(BLK//8):
            turned=pltpu.roll(base,(8*m-(BLK-1))%(2*SEQ),1)
            for d in range(2*NB-1):
                e=2*NB-2-d
                strip[d*BLK+8*m:d*BLK+8*m+8,h*BLK:(h+1)*BLK]=turned[:,e*BLK:(e+1)*BLK]

def fold_strip(strip, out_ref):
    for h in range(2):
        total=jnp.zeros((8,2*SEQ),F32)
        for m in range(BLK//8):
            parts=[strip[(2*NB-2-e)*BLK+8*m:(2*NB-2-e)*BLK+8*m+8,h*BLK:(h+1)*BLK] for e in range(2*NB-1)]
            parts.append(jnp.zeros((8,BLK),F32))
            total=total+pltpu.roll(jnp.concatenate(parts,axis=1),(BLK-1-8*m)%(2*SEQ),1)
        row=total[0:1]
        for s in range(1,8):
            row=row+pltpu.roll(total[s:s+1],2*SEQ-s,1)
        out_ref[h:h+1,:]=row

def lanes_mask():
    lane=lax.broadcasted_iota(jnp.int32,(1,BLK),1)
    return lane<64

def stack_heads(x, first):
    zero=jnp.zeros_like(x)
    return jnp.concatenate([jnp.where(first,x,zero),jnp.where(first,zero,x)],axis=0)


def strip_kernel(rev_ref, strip):
    build_strip(rev_ref, strip)

def make_strips(rev, deps=()):
    return pl.pallas_call(after(strip_kernel, 1, deps),grid=(8,),
        in_specs=[pl.BlockSpec((None,2,2*SEQ),lambda p:(p,0,0))]+[ANY]*len(deps),
        out_specs=pl.BlockSpec((None,STRIP,2*BLK),lambda p:(p,0,0)),
        out_shape=jax.ShapeDtypeStruct((8,STRIP,2*BLK),F32),
        compiler_params=pltpu.CompilerParams(vmem_limit_bytes=VLIM),
        name="bias_strips")(rev, *deps)

def attn_fwd_kernel(UNIT, rng_ref, segk_ref, segq_ref, strip, qkv, o_ref, lse_ref, vt):
    first=lanes_mask()
    for u in range(UNIT):
        vt[u]=qkv[:,2*GROUP+u*BLK:2*GROUP+(u+1)*BLK].T
    mean=jnp.sum(qkv[:,2*GROUP:].astype(F32),axis=0,keepdims=True)*(1.0/SEQ)

    def block(qi, carry):
        q0=pl.multiple_of(qi*BLK,BLK)
        lo=rng_ref[qi]; width=rng_ref[NB+qi]
        k0=pl.multiple_of(lo*BLK,BLK)
        b0=pl.multiple_of((lo-qi+NB-1)*BLK,BLK)
        segq=segq_ref[pl.ds(qi,1),:]
        @pl.when(width==0)
        def _():
            o_ref[pl.ds(q0,BLK),:]=jnp.broadcast_to(mean,(BLK,UNIT*BLK)).astype(BF)
            for u in range(UNIT):
                lse_ref[u,pl.ds(qi,1),:]=jnp.zeros((1,2*BLK),F32)
        for w in range(1,NB+1):
            @pl.when(width==w)
            def _():
                rows=w*BLK
                allowed=segk_ref[pl.ds(k0,rows),:]==segq
                live_row=segq>0
                live_row=jnp.concatenate([live_row,live_row],axis=1)
                live_col=segk_ref[pl.ds(q0,BLK),:]>0
                units=[slice(u*BLK,(u+1)*BLK) for u in range(UNIT)]
                qcats=[stack_heads(qkv[pl.ds(q0,BLK),lanes],first) for lanes in units]
                scores=[nt(qkv[pl.ds(k0,rows),GROUP+lanes.start:GROUP+lanes.stop],qcat) for lanes,qcat in zip(units,qcats)]
                probs=[]; stats=[]; totals=[]
                for u in range(UNIT):
                    both=[]; stat=[]; tot=[]
                    s=scores[u]+strip[u,pl.ds(b0,rows),:]
                    for h in range(2):
                        sh=jnp.where(allowed,s[:,h*BLK:(h+1)*BLK],NEG)
                        peak=jnp.max(sh,axis=0,keepdims=True)
                        e=jnp.exp(sh-peak)
                        t=jnp.sum(e,axis=0,keepdims=True)
                        both.append(e.astype(BF)); stat.append(peak+jnp.log(t)); tot.append(t)
                    probs.append(jnp.concatenate(both,axis=1)); stats.append(jnp.concatenate(stat,axis=1)); totals.append(jnp.concatenate(tot,axis=1))
                ots=[nn(vt[u,:,pl.ds(k0,rows)],probs[u]) for u in range(UNIT)]
                for u,lanes in enumerate(units):
                    ot=ots[u]*(1.0/totals[u])
                    o=jnp.concatenate([ot[:64,:BLK],ot[64:,BLK:]],axis=0).T
                    o_ref[pl.ds(q0,BLK),lanes]=jnp.where(live_col,o,mean[:,lanes]).astype(BF)
                    lse_ref[u,pl.ds(qi,1),:]=jnp.where(live_row,stats[u],0.0)
        return carry
    lax.fori_loop(0,NB,block,0)

def attn_bwd_kernel(UNIT, rng_ref, segk_ref, segq_ref, strip, q_ref, k_ref, v_ref, g_ref, lse_ref,
                    dq_ref, dk_ref, dv_ref, off_ref, dstrip, kt, dk, dv):
    first=lanes_mask()
    dstrip[...]=jnp.zeros_like(dstrip)
    dk[...]=jnp.zeros_like(dk)
    for u in range(UNIT):
        lanes=slice(u*BLK,(u+1)*BLK)
        kt[u]=k_ref[:,lanes].T
        padded=jnp.where(segk_ref[...]>0,0.0,g_ref[:,lanes].astype(F32))
        dv[:,lanes]=jnp.broadcast_to(jnp.sum(padded,axis=0,keepdims=True)*(1.0/SEQ),(SEQ,BLK))

    def block(qi, carry):
        q0=pl.multiple_of(qi*BLK,BLK)
        lo=rng_ref[qi]; width=rng_ref[NB+qi]
        k0=pl.multiple_of(lo*BLK,BLK)
        b0=pl.multiple_of((lo-qi+NB-1)*BLK,BLK)
        segq=segq_ref[pl.ds(qi,1),:]
        @pl.when(width==0)
        def _():
            dq_ref[pl.ds(q0,BLK),:]=jnp.zeros((BLK,UNIT*BLK),BF)
        for w in range(1,NB+1):
            @pl.when(width==w)
            def _():
                rows=w*BLK
                allowed=segk_ref[pl.ds(k0,rows),:]==segq
                units=[slice(u*BLK,(u+1)*BLK) for u in range(UNIT)]
                qcats=[stack_heads(q_ref[pl.ds(q0,BLK),lanes],first) for lanes in units]
                gcats=[stack_heads(g_ref[pl.ds(q0,BLK),lanes],first) for lanes in units]
                scores=[nt(k_ref[pl.ds(k0,rows),lanes],qcat) for lanes,qcat in zip(units,qcats)]
                dps=[nt(v_ref[pl.ds(k0,rows),lanes],gcat) for lanes,gcat in zip(units,gcats)]
                probs=[]; grads=[]
                for u in range(UNIT):
                    lse=lse_ref[u,pl.ds(qi,1),:]
                    s=scores[u]+strip[u,pl.ds(b0,rows),:]
                    ps=[]; ds=[]
                    for h in range(2):
                        cols=slice(h*BLK,(h+1)*BLK)
                        prob=jnp.exp(jnp.where(allowed,s[:,cols],NEG)-lse[:,cols])
                        t=prob*dps[u][:,cols]
                        inner=jnp.sum(t,axis=0,keepdims=True)
                        d=t-prob*inner
                        dstrip[u,pl.ds(b0,rows),cols]+=d
                        ps.append(prob.astype(BF)); ds.append(d.astype(BF))
                    probs.append(jnp.concatenate(ps,axis=1)); grads.append(jnp.concatenate(ds,axis=1))
                for u,lanes in enumerate(units):
                    dv[pl.ds(k0,rows),lanes]+=nn(probs[u],gcats[u])
                dqts=[nn(kt[u,:,pl.ds(k0,rows)],grads[u]) for u in range(UNIT)]
                for u,lanes in enumerate(units):
                    dk[pl.ds(k0,rows),lanes]+=nn(grads[u],qcats[u])
                for u,lanes in enumerate(units):
                    dq_ref[pl.ds(q0,BLK),lanes]=jnp.concatenate([dqts[u][:64,:BLK],dqts[u][64:,BLK:]],axis=0).T.astype(BF)
        return carry
    lax.fori_loop(0,NB,block,0)
    dk_ref[...]=dk[...].astype(BF)
    dv_ref[...]=dv[...].astype(BF)
    for u in range(UNIT):
        fold_strip(dstrip.at[u], off_ref.at[u])

def backward_kernel(unit, lead, rng, source, segk, segq, strip, q, k, v, grad, lse, *refs):
    lefts, rights, refs = refs[: 1 + lead], refs[1 + lead : 1 + 3 * lead], refs[1 + 3 * lead :]
    dq, dk, dv, off, keep, send, dstrip, kt, dk_sum, dv_sum, held, sem = refs
    p = pl.program_id(0)

    @pl.when(p == 0)
    def _():
        for n, left in enumerate(lefts):
            order_rows(source, left, held.at[n], sem.at[n])

    attn_bwd_kernel(
        unit, rng, segk, segq, strip, q, k, v, grad, lse, dq, dk, dv, off, dstrip, kt, dk_sum, dv_sum
    )

    @pl.when(p == 0)
    def _():
        for n in range(1 + lead):
            wait_whole(held.at[n], sem.at[n])

    half, wide = D // 2, unit * BLK
    for j, right in enumerate((dq, dk, dv)):
        part = nn(held[0], right[...]).astype(BF)
        keep[:, j * wide : (j + 1) * wide] = part[:half]
        send[:, j * wide : (j + 1) * wide] = part[half:]
    for n, right in enumerate(rights):

        @pl.when(p == n)
        def _():
            for j in range(GROUP // wide):
                part = nn(held[1], right[:, j * wide : (j + 1) * wide]).astype(BF)
                cols = slice((3 + j) * wide, (4 + j) * wide)
                keep[:, cols] = part[:half]
                send[:, cols] = part[half:]


def attn_bwd(rng, source, segk, segq, strips, qkv, g, lse, turned, more, first_pair):
    unit, steps = 2, 2
    wide = unit * BLK
    lead = int(len(more) > 0)
    f = first_pair // unit
    c = lambda o: pl.BlockSpec((SEQ, wide), lambda p, r, s: (0, o + p))
    whole = lambda *s: pl.BlockSpec(s, lambda p, r, s: (0, 0))
    width = 3 * wide + lead * GROUP
    out = pl.BlockSpec((D // 2, width), lambda p, r, s: (0, p))
    gs = pltpu.PrefetchScalarGridSpec(
        num_scalar_prefetch=2,
        grid=(steps,),
        in_specs=[
            whole(SEQ, BLK), whole(NB, BLK),
            pl.BlockSpec((unit, STRIP, 2 * BLK), lambda p, r, s: (f + p, 0, 0)),
            c(0), c(steps), c(2 * steps), c(f),
            pl.BlockSpec((unit, NB, 2 * BLK), lambda p, r, s: (p, 0, 0)),
        ] + [ANY] * (1 + lead) + [whole(SEQ, GROUP)] * (2 * lead),
        out_specs=[c(0), c(0), c(0), pl.BlockSpec((unit, 2, 2 * SEQ), lambda p, r, s: (p, 0, 0)), out, out],
        scratch_shapes=[
            pltpu.VMEM((unit, STRIP, 2 * BLK), F32), pltpu.VMEM((unit, BLK, SEQ), BF),
            pltpu.VMEM((SEQ, wide), F32), pltpu.VMEM((SEQ, wide), F32),
            pltpu.VMEM((1 + lead, D, SEQ), BF), pltpu.SemaphoreType.DMA((1 + lead,)),
        ],
    )
    sh = jax.ShapeDtypeStruct((SEQ, steps * wide), BF)
    term = jax.ShapeDtypeStruct((D // 2, steps * width), BF)
    return pl.pallas_call(
        functools.partial(backward_kernel, unit, lead),
        grid_spec=gs,
        out_shape=[sh, sh, sh, jax.ShapeDtypeStruct((steps * unit, 2, 2 * SEQ), F32), term, term],
        compiler_params=params(),
        cost_estimate=cost(24 * RATE, 16 * SEQ * wide * 2),
        name="attention_backward",
    )(rng, source, segk, segq, strips, qkv, qkv, qkv, g, lse, turned, *more)


def ranges(seg):
    s=seg.reshape(NB,BLK)
    least=s[:,0]; most=jnp.max(s,axis=1)
    lo=jnp.sum((most[None,:]<least[:,None])&(least[None,:]>0),axis=1)
    hi=jnp.sum((least[None,:]<=most[:,None])&(least[None,:]>0),axis=1)
    w=jnp.where(least>0,hi-lo,0)
    return jnp.concatenate([jnp.where(least>0,lo,0),w]).astype(jnp.int32)


def prep_kernel(c_ref, seg_ref, out_ref, turned_ref):
    low = jnp.where(jnp.concatenate([seg_ref[...] > 0] * (D // BLK), axis=1), c_ref[...].astype(F32), 0.0).astype(BF)
    out_ref[...] = low
    turned_ref[...] = low.T


def prepare(c, segk):
    rows = 256
    blk = pl.BlockSpec((rows, D), lambda i: (i, 0))
    return pl.pallas_call(
        prep_kernel,
        grid=(SEQ // rows,),
        in_specs=[blk, pl.BlockSpec((rows, BLK), lambda i: (i, 0))],
        out_specs=[blk, pl.BlockSpec((D, rows), lambda i: (0, i))],
        out_shape=[jax.ShapeDtypeStruct((SEQ, D), BF), jax.ShapeDtypeStruct((D, SEQ), BF)],
        compiler_params=params(),
        cost_estimate=cost(4 * RATE, 6 * SEQ * D),
        name="prepare",
    )(c, segk)


def pack_kernel(spans, count, *refs):
    ins, outs = refs[:count], refs[count:]
    for out, cols in zip(outs, spans):
        at = 0
        for n, lo, hi in cols:
            out[:, at : at + hi - lo] = ins[n][:, lo:hi]
            at += hi - lo


def pack(shards, spans, deps=()):
    rows = shards[0].shape[0]
    widths = [sum(hi - lo for _, lo, hi in cols) for cols in spans]
    whole = pl.BlockSpec(memory_space=pltpu.VMEM)
    return pl.pallas_call(
        after(functools.partial(pack_kernel, spans, len(shards)), len(shards), deps),
        in_specs=[whole] * len(shards) + [ANY] * len(deps),
        out_specs=[whole] * len(widths),
        out_shape=[jax.ShapeDtypeStruct((rows, w), BF) for w in widths],
        name="pack_shards",
    )(*shards, *deps)


def join(*parts):
    return jnp.concatenate(parts, axis=0)


def add_terms(terms, rows):
    return sum(t[off : off + rows].astype(F32) for t, off in terms).astype(BF)


def finish_kernel(counts, *refs):
    weights, gains, refs = refs[:5], refs[5], refs[6:]
    sums, at = [], 0
    for n in counts:
        total = refs[at][...].astype(F32)
        for ref in refs[at + 1 : at + n]:
            total = total + ref[...].astype(F32)
        sums.append(total)
        at += n
    outs = refs[at:]
    wide = GROUP // 2
    for g, step in ((0, 3 * wide + GROUP), (1, 3 * wide)):
        for p in range(2):
            for j in range(3):
                col = g * GROUP + p * wide
                outs[j][:, col : col + wide] = sums[g][:, p * step + j * wide : p * step + (j + 1) * wide]
    for p in range(2):
        start = (p + 1) * (3 * wide + GROUP) - GROUP
        outs[3][:, p * GROUP : (p + 1) * GROUP] = sums[0][:, start : start + GROUP]
    at = 0
    for s, width in zip(sums[2:], PIECES):
        for j in range(3):
            outs[4 + j][:, at : at + width] = s[:, j * width : (j + 1) * width]
        at += width
    match = lambda w, out: jnp.sum(w[...].astype(F32) * out[...], axis=1, keepdims=True)
    one = match(weights[0], outs[0]) + match(weights[1], outs[1]) + match(weights[2], outs[2])
    two = match(weights[3], outs[4]) + match(weights[4], outs[5])
    lane = lax.broadcasted_iota(jnp.int32, gains.shape, 1)
    outs[7][...] = jnp.where(lane == 0, one, two) / jnp.where(lane < 2, gains[...].astype(F32), 1.0)


def finish(sets, weights, gains):
    rows = gains.shape[0]
    flat = [x for terms in sets for x in terms]
    widths = (D,) * 4 + (FF,) * 3 + (BLK,)
    top = lambda w: pl.BlockSpec((rows, w), lambda i: (0, 0))
    return pl.pallas_call(
        functools.partial(finish_kernel, tuple(len(t) for t in sets)),
        grid=(1,),
        in_specs=[top(x.shape[1]) for x in (*weights, gains, *flat)],
        out_specs=[top(w) for w in widths],
        out_shape=[jax.ShapeDtypeStruct((rows, w), F32) for w in widths],
        compiler_params=params(),
        name="weight_gradients",
    )(*weights, gains, *flat)


def place_blocks(source_ref, blocks, start, cols, dst, at, sem):
    rows = blocks[0].shape[0]
    size = D // source_ref.shape[0]
    per = rows // size
    for n, ref in enumerate(blocks):

        def one(i, carry):
            row = pl.multiple_of(source_ref[n * per + i] * size, size)
            pltpu.make_async_copy(
                ref.at[pl.ds(pl.multiple_of(i * size, size), size), pl.ds(start, cols)],
                dst.at[pl.ds(row, size), pl.ds(at, cols)],
                sem,
            ).start()
            return carry

        lax.fori_loop(0, per, one, 0)


def wait_whole(dst, sem):
    pltpu.make_async_copy(dst, dst, sem).wait()


def order_rows(source_ref, src, dst, sem):
    size = D // source_ref.shape[0]

    def one(p, carry):
        row = pl.multiple_of(source_ref[p] * size, size)
        pltpu.make_async_copy(
            src.at[pl.ds(row, size)], dst.at[pl.ds(pl.multiple_of(p * size, size), size)], sem
        ).start()
        return carry

    lax.fori_loop(0, D // size, one, 0)


def scaled_rows(x):
    return lax.rsqrt(jnp.mean(x * x, axis=-1, keepdims=True) + EPS)


def attend_kernel(lead, first_pair, *refs):
    rng, source, segk, segq, x, strips = refs[:6]
    blocks, refs = refs[6:14], refs[14:]
    if lead:
        qkv_out, o_ref, lse_ref, gains_ref, normed_out, turned_out = refs[:6]
        qkv, w, strip, normed, vt, sem, turned = refs[6:]
    else:
        qkv_out, o_ref, lse_ref = refs[:3]
        qkv, w, strip, normed, vt, sem = refs[3:]
    unit = vt.shape[0]
    bring = pltpu.make_async_copy(x, normed, sem.at[0])
    bring.start()
    place_blocks(source, blocks, 0, w.shape[1], w, 0, sem.at[1])
    pads = pltpu.make_async_copy(strips.at[pl.ds(first_pair, unit)], strip, sem.at[2])
    pads.start()
    outs = [pltpu.make_async_copy(qkv, qkv_out, sem.at[3])]
    bring.wait()
    wait_whole(w, sem.at[1])
    if lead:
        gains_ref[...] = w[:, 3 * GROUP :].astype(F32).T[:8]

        def rows_of(i, carry):
            at = pl.multiple_of(i * 256, 256)
            rows = normed[pl.ds(at, 256), :].astype(F32)
            low = (rows * scaled_rows(rows) * gains_ref[0:1, :]).astype(BF)
            normed[pl.ds(at, 256), :] = low
            turned[:, pl.ds(at, 256)] = low.T
            return carry

        lax.fori_loop(0, SEQ // 256, rows_of, 0)
        outs += [pltpu.make_async_copy(normed, normed_out, sem.at[4]), pltpu.make_async_copy(turned, turned_out, sem.at[5])]
        for c in outs[1:]:
            c.start()

    def columns(j, carry):
        cols = pl.ds(pl.multiple_of(j * FT, FT), FT)
        qkv[:, cols] = nn(normed[...], w[:, cols]).astype(BF)
        return carry

    lax.fori_loop(0, 3 * GROUP // FT, columns, 0)
    outs[0].start()
    pads.wait()
    attn_fwd_kernel(unit, rng, segk, segq, strip, qkv, o_ref, lse_ref, vt)
    for c in outs:
        c.wait()


def attend(rng, source, segk, segq, strips, x, blocks, lead):
    unit = 4
    width = 3 * GROUP + (BLK if lead else 0)
    vmem = pl.BlockSpec(memory_space=pltpu.VMEM)
    shape = lambda t, *s: jax.ShapeDtypeStruct(s, t)
    out_specs = [ANY, vmem, vmem] + ([vmem, ANY, ANY] if lead else [])
    out_shape = [shape(BF, SEQ, 3 * GROUP), shape(BF, SEQ, GROUP), shape(F32, unit, NB, 2 * BLK)]
    out_shape += [shape(F32, 8, D), shape(BF, SEQ, D), shape(BF, D, SEQ)] if lead else []
    return pl.pallas_call(
        functools.partial(attend_kernel, lead, 0 if lead else unit),
        in_specs=[SMEM, SMEM, vmem, vmem, ANY, ANY] + [ANY] * len(blocks),
        out_specs=out_specs,
        out_shape=out_shape,
        scratch_shapes=[
            pltpu.VMEM((SEQ, 3 * GROUP), BF), pltpu.VMEM((D, width), BF), pltpu.VMEM((unit, STRIP, 2 * BLK), F32),
            pltpu.VMEM((SEQ, D), BF), pltpu.VMEM((unit, BLK, SEQ), BF), pltpu.SemaphoreType.DMA((6,)),
        ] + ([pltpu.VMEM((D, SEQ), BF)] if lead else []),
        compiler_params=pltpu.CompilerParams(vmem_limit_bytes=VLIM),
        cost_estimate=cost(20 * RATE, 2 * D * width + 4 * SEQ * D),
        name="attention_forward",
    )(rng, source, segk, segq, x, strips, *blocks)


def hidden_kernel(*refs):
    source, a0, a1, x_ref, gains_ref = refs[:5]
    h_ref, n2_ref, n2t_ref, w, sem = refs[13:]

    @pl.when(pl.program_id(0) == 0)
    def _():
        place_blocks(source, refs[5:13], 3 * GROUP, D, w, 0, sem.at[0])
        wait_whole(w, sem.at[0])

    hidden = x_ref[...].astype(F32) + nt(jnp.concatenate([a0[...], a1[...]], axis=1), w[...])
    h_ref[...] = hidden
    normed = (hidden * scaled_rows(hidden) * gains_ref[1:2, :]).astype(BF)
    n2_ref[...] = normed
    n2t_ref[...] = normed.T


def hidden_units(source, a0, a1, x, gains, blocks):
    rows = TILE
    tok = lambda c: pl.BlockSpec((rows, c), lambda i: (i, 0))
    return pl.pallas_call(
        hidden_kernel,
        grid=(SEQ // rows,),
        in_specs=[SMEM, tok(GROUP), tok(GROUP), tok(D), pl.BlockSpec((8, D), lambda i: (0, 0))] + [ANY] * len(blocks),
        out_specs=[tok(D), tok(D), pl.BlockSpec((D, rows), lambda i: (0, i))],
        out_shape=[
            jax.ShapeDtypeStruct((SEQ, D), F32),
            jax.ShapeDtypeStruct((SEQ, D), BF),
            jax.ShapeDtypeStruct((D, SEQ), BF),
        ],
        scratch_shapes=[pltpu.VMEM((D, D), BF), pltpu.SemaphoreType.DMA((1,))],
        compiler_params=params(),
        cost_estimate=cost(6 * RATE, 16 * SEQ * D),
        name="hidden_units",
    )(source, a0, a1, x, gains, *blocks)


def feed_kernel(lead, final, width, base, *refs):
    source, n2, n2t, cot, cott, whole = refs[:6]
    refs = refs[6:]
    sums_from = () if lead else refs[:2]
    refs = refs[len(sums_from) :]
    if final:
        h_in, gains_ref, seg_in, blocks, refs = refs[0], refs[1], refs[2], refs[3:11], refs[11:]
    keep, send = refs[:2]
    outs, refs = (refs[2:6], refs[6:]) if final else (refs[2:4], refs[4:])
    n2_v, n2t_v, cot_v, cott_v, w, stage, bo, ng, mix_v, gu_v, sem_w, sem_o, sem_i = refs[:13]
    half = D // 2
    tiles = width // FT

    def weight_copies(f):
        out = []
        for j in range(3):
            col = pl.multiple_of(j * width + f * FT, FT)
            out.append(
                pltpu.make_async_copy(
                    whole.at[:, pl.ds(pl.multiple_of(base + col, BLK), FT)], w.at[:, pl.ds(col, FT)], sem_w.at[f, j]
                )
            )
        return out

    def term_copies(g):
        col = pl.multiple_of(g * FT, FT)
        return [
            pltpu.make_async_copy(
                stage.at[pl.ds(s * half, half), pl.ds(col, FT)], dst.at[:, pl.ds(col, FT)], sem_o.at[g, s]
            )
            for s, dst in enumerate((keep, send))
        ]

    first = [pltpu.make_async_copy(n2, n2_v, sem_i.at[0]), pltpu.make_async_copy(cot, cot_v, sem_i.at[1])]
    sums_in = [pltpu.make_async_copy(a, b, sem_i.at[4 + n]) for n, (a, b) in enumerate(zip(sums_from, (bo, ng)))]
    if final:
        h_v, wo, ag_v, bt_v, out_v, seg_v = refs[13:]
        sums_in += [pltpu.make_async_copy(h_in, h_v, sem_i.at[6]), pltpu.make_async_copy(seg_in, seg_v, sem_i.at[7])]
        sources = (out_v, ng, bt_v, ag_v)
    else:
        sources = (bo, ng)
    results = [pltpu.make_async_copy(a, b, sem_i.at[8 + n]) for n, (a, b) in enumerate(zip(sources, outs))]
    for c in weight_copies(0) + first:
        c.start()
    for c in first:
        c.wait()
    for f in range(1, tiles):
        for c in weight_copies(f):
            c.start()
    for c in sums_in:
        c.start()

    def units(f, carry):
        for c in weight_copies(f):
            c.wait()
        at = [pl.ds(pl.multiple_of(j * width + f * FT, FT), FT) for j in range(3)]

        gate = nn(n2_v[...], w[:, at[0]])
        upward = nn(n2_v[...], w[:, at[1]])
        mixed_grad = nn(cot_v[...], w[:, at[2]])
        square = gate * gate
        bend = jnp.tanh(gate * (GELU_A + (GELU_A * GELU_B) * square))
        curve = 0.5 * (1.0 + bend)
        active = gate * curve
        slope = curve + (0.5 * gate) * (1.0 - bend * bend) * (GELU_A + (3.0 * GELU_A * GELU_B) * square)
        mix_v[:, at[0]] = (active * upward).astype(BF)
        gu_v[:, at[0]] = (mixed_grad * upward * slope).astype(BF)
        gu_v[:, at[1]] = (mixed_grad * active).astype(BF)
        return carry

    lax.fori_loop(0, tiles, units, 0)
    order_rows(source, n2t, n2t_v, sem_i.at[2])
    order_rows(source, cott, cott_v, sem_i.at[3])
    if final:
        place_blocks(source, blocks, 3 * GROUP, D, wo, 0, sem_i.at[13])
    for c in sums_in:
        c.wait()

    for j in range(D // FT):
        cols = slice(j * FT, (j + 1) * FT)
        one = nt(mix_v[...], w[cols, 2 * width :])
        two = nt(gu_v[...], w[cols, : 2 * width])
        bo[:, cols] = one if lead else bo[:, cols] + one
        ng[:, cols] = two if lead else ng[:, cols] + two
    if final:
        wait_whole(wo, sem_i.at[13])

        def close(i, carry):
            rows = pl.ds(pl.multiple_of(i * 256, 256), 256)
            hidden = h_v[rows, :]
            live = jnp.concatenate([seg_v[rows, :] > 0] * (D // BLK), axis=1)
            out_v[rows, :] = jnp.where(live, hidden + bo[rows, :], 0.0).astype(BF)
            grad = ng[rows, :]
            scale = scaled_rows(hidden)
            grad = grad * gains_ref[1:2, :]
            mean = jnp.mean(grad * hidden, axis=-1, keepdims=True)
            out = cot_v[rows, :].astype(F32) + (scale * grad - hidden * (scale * scale * scale * mean))
            ng[rows, :] = out
            low = out.astype(BF)
            mix_low[rows, :] = low
            bt_v[:, rows] = low.T
            return carry

        mix_low = n2_v
        lax.fori_loop(0, SEQ // 256, close, 0)

        def attended(i, carry):
            cols = pl.ds(pl.multiple_of(i * FT, FT), FT)
            ag_v[:, cols] = nn(mix_low[...], wo[:, cols]).astype(BF)
            return carry

        lax.fori_loop(0, D // FT, attended, 0)
    for c in results:
        c.start()
    wait_whole(n2t_v, sem_i.at[2])
    wait_whole(cott_v, sem_i.at[3])

    def term(left, right, f, start):
        cols = pl.ds(pl.multiple_of(f * FT, FT), FT)
        out = pl.ds(pl.multiple_of((start + f) * FT, FT), FT)
        stage[:, out] = nn(left[...], right[:, cols]).astype(BF)
        for c in term_copies(start + f):
            c.start()

    def pair(f, carry):
        term(n2t_v, gu_v, 2 * f, 0)
        term(n2t_v, gu_v, 2 * f + 1, 0)
        return carry

    lax.fori_loop(0, tiles, pair, 0)
    for f in range(tiles):
        term(cott_v, mix_v, f, 2 * tiles)
    for c in results:
        c.wait()

    def drain(g, carry):
        for c in term_copies(g):
            c.wait()
        return carry

    lax.fori_loop(0, 3 * tiles, drain, 0)


def feed(source, acts, whole, base, width, sums, closing=None):
    lead, final = sums is None, closing is not None
    tiles = width // FT
    args = [source, *acts, whole] + ([] if lead else list(sums))
    specs = [SMEM] + [ANY] * (len(args) - 1)
    if final:
        hidden, gains, segk, blocks = closing
        args += [hidden, gains, segk, *blocks]
        specs += [ANY, pl.BlockSpec(memory_space=pltpu.VMEM), ANY] + [ANY] * len(blocks)
    half = jax.ShapeDtypeStruct((D // 2, 3 * width), BF)
    shape = lambda t, *s: jax.ShapeDtypeStruct(s, t)
    total = shape(F32, SEQ, D)
    outs = [shape(BF, SEQ, D), total, shape(BF, D, SEQ), shape(BF, SEQ, D)] if final else [total, total]
    bf = lambda *s: pltpu.VMEM(s, BF)
    scratch = [
        bf(SEQ, D), bf(D, SEQ), bf(SEQ, D), bf(D, SEQ), bf(D, 3 * width), bf(D, 3 * width),
        pltpu.VMEM((SEQ, D), F32), pltpu.VMEM((SEQ, D), F32),
        bf(SEQ, width), bf(SEQ, 2 * width),
        pltpu.SemaphoreType.DMA((tiles, 3)), pltpu.SemaphoreType.DMA((3 * tiles, 2)), pltpu.SemaphoreType.DMA((14,)),
    ]
    if final:
        scratch += [
            pltpu.VMEM((SEQ, D), F32), bf(D, D), bf(SEQ, D), bf(D, SEQ), bf(SEQ, D),
            pltpu.VMEM((SEQ, BLK), jnp.int32),
        ]
    return pl.pallas_call(
        functools.partial(feed_kernel, lead, final, width, base),
        in_specs=specs,
        out_specs=[ANY] * (2 + len(outs)),
        out_shape=[half, half] + outs,
        scratch_shapes=scratch,
        compiler_params=pltpu.CompilerParams(vmem_limit_bytes=VLIM),
        cost_estimate=cost((30 * width / 1024 + (6 if final else 0)) * RATE, 12 * D * width + 24 * SEQ * D, SEQ * width),
        name="feed_forward",
    )(*args)


def last_kernel(count, *refs):
    source, x_ref, hg_ref, gains_ref = refs[:4]
    grads = refs[4 : 4 + count]
    blocks = refs[4 + count : 20 + count]
    out_ref, w, sem = refs[-3:]
    half = 3 * GROUP

    @pl.when(pl.program_id(0) == 0)
    def _():
        for n in range(2):
            place_blocks(source, blocks[8 * n : 8 * n + 8], 0, half, w, n * half, sem.at[n])
        for n in range(2):
            wait_whole(w.at[:, pl.ds(n * half, half)], sem.at[n])

    grad = nt(jnp.concatenate([g[...] for g in grads], axis=1), w[...])
    x = x_ref[...].astype(F32)
    scale = scaled_rows(x)
    grad = grad * gains_ref[0:1, :]
    mean = jnp.mean(grad * x, axis=-1, keepdims=True)
    out_ref[...] = hg_ref[...] + (scale * grad - x * (scale * scale * scale * mean))


def last(source, x, hg, gains, grads, blocks):
    rows = 256
    tok = lambda c: pl.BlockSpec((rows, c), lambda i: (i, 0))
    whole = pl.BlockSpec((8, D), lambda i: (0, 0))
    return pl.pallas_call(
        functools.partial(last_kernel, len(grads)),
        grid=(SEQ // rows,),
        in_specs=[SMEM, tok(D), tok(D), whole] + [tok(g.shape[1]) for g in grads] + [ANY] * len(blocks),
        out_specs=tok(D),
        out_shape=jax.ShapeDtypeStruct((SEQ, D), F32),
        scratch_shapes=[pltpu.VMEM((D, 6 * GROUP), BF), pltpu.SemaphoreType.DMA((2,))],
        compiler_params=params(),
        cost_estimate=cost(14 * RATE, 14 * SEQ * D),
        name="input_gradient",
    )(source, x, hg, gains, *grads, *blocks)


class Slice:
    def __init__(self, mesh):
        self.count = mesh.shape["dp"] * mesh.shape["fsdp"]
        self.inner = mesh.shape["fsdp"]
        self.core = self.inner
        bits = [1 << b for b in range(self.count.bit_length() - 1)]
        self.rest = [b for b in reversed(bits) if b not in (1, 2, self.core)]
        self.order = [self.core, 2, 1] + self.rest[::-1]
        self.size = D // self.count

    def place(self, index):
        p = index * 0
        for b in self.order:
            p = 2 * p + (index // b) % 2
        return p

    def swap(self, x, bit):
        return lax.ppermute(x, AXES, [(i, i ^ bit) for i in range(self.count)])

    @staticmethod
    def masks(bits):
        return [sum(b for j, b in enumerate(bits) if n >> j & 1) for n in range(1, 1 << len(bits))]


class Order:
    def __init__(self):
        self.token = None

    def hold(self, args):
        leaves, tree = jax.tree.flatten(args)
        at = [i for i, x in enumerate(leaves) if hasattr(x, "aval")]
        if self.token is not None:
            held = lax.optimization_barrier([leaves[i] for i in at] + [self.token])
            for i, x in zip(at, held):
                leaves[i] = x
        return jax.tree.unflatten(tree, leaves)

    def __call__(self, f, *args):
        out = f(*self.hold(args))
        self.token = jax.tree.leaves(out)[0]
        return out


class Chain:
    def __init__(self, links, run):
        self.links, self.run, self.pending = links, run, []


def meet(run, *chains):
    arrays = run.hold([c.pending for c in chains] + [run.token])
    run.token = arrays.pop()
    for c, got in zip(chains, arrays):
        c.met(got)
        c.pending = []


class Gather(Chain):
    def __init__(self, links, run, shard):
        super().__init__(links, run)
        self.line = run.hold(shard)
        self.pending = [links.swap(self.line, m) for m in links.masks(links.rest)]

    def met(self, got):
        self.got = got

    def square(self):
        self.line = self.run(join, self.line, *self.got)
        self.others = [self.links.swap(self.line, self.links.core)]
        self.pending = [self.links.swap(self.line, m) for m in (1, 2, 3)]

    def end(self):
        self.others += [self.links.swap(b, self.links.core) for b in self.got]
        return (self.line, *self.got, *self.others)


class Total(Chain):
    def __init__(self, links, run, x):
        super().__init__(links, run)
        self.x = run.hold(x)
        self.groups = [links.masks(b) for b in (links.rest, [1, 2], [links.core])]
        self.step()

    def met(self, got):
        self.x = self.x + sum(got)

    def step(self):
        self.pending = [self.links.swap(self.x, m) for m in self.groups.pop(0)]


class Scatter(Chain):
    def __init__(self, links, run, keep, send):
        super().__init__(links, run)
        self.terms, self.rows, self.bits = [keep], D // 2, links.rest[::-1]
        self.pending = [links.swap(run.hold(send), links.core)]

    def met(self, got):
        self.got = got

    def spread(self, masks):
        self.terms += self.got
        rows = self.rows // (len(masks) + 1)
        self.pending = []
        for n in list(range(len(masks)))[::-1]:
            send = self.run(add_terms, [(t, (n + 1) * rows) for t in self.terms], rows)
            self.pending.insert(0, self.links.swap(send, masks[n]))
        self.rows = rows

    def square(self):
        self.spread((1, 2, 3))

    def line(self):
        self.spread(self.links.masks(self.links.rest))
        self.bits = []

    def step(self):
        self.spread((self.bits.pop(0),))


def on_device(
    links,
    layer_input,
    segment_ids,
    relative_buckets,
    first_gain,
    query_weight,
    key_weight,
    value_weight,
    output_projection,
    relative_table,
    second_gain,
    gate_weight,
    up_weight,
    down_projection,
    output_cotangent,
):
    size = links.size
    me = lax.axis_index("dp") * links.inner + lax.axis_index("fsdp")
    place = np.array([links.place(i) for i in range(links.count)], np.int32)
    source = jnp.asarray(np.argsort(place).astype(np.int32)) ^ me

    gains_shard = jnp.pad(jnp.stack([first_gain, second_gain], axis=1), ((0, 0), (0, BLK - 2)))
    w1, w2, w3 = PIECES
    feed_shards = (gate_weight, up_weight, down_projection)
    qkv_shards = (query_weight, key_weight, value_weight)
    triple = lambda lo, hi: tuple((n, lo, hi) for n in range(3))
    run = Order()
    segk = jnp.broadcast_to(segment_ids[:, None], (SEQ, BLK))
    segq = jnp.where(segment_ids > 0, segment_ids, -1).reshape(NB, BLK)
    spans = ranges(segment_ids)
    one_hot = (relative_buckets[::-1][:, None] == jnp.arange(BUCKETS)[None, :]).astype(BF)
    one_hot = jnp.pad(one_hot, ((0, 1), (0, 0)))
    offsets = lax.dot_general(relative_table, one_hot, (((0,), (1,)), ((), ())), preferred_element_type=F32)

    (first_shard,) = run(pack, qkv_shards + (gains_shard,), (triple(0, GROUP) + ((3, 0, BLK),),))
    first = Gather(links, run, first_shard)
    (second_shard,) = run(pack, qkv_shards + (output_projection,), (triple(GROUP, 2 * GROUP) + ((3, 0, D),),))
    cot, cott = run(prepare, output_cotangent, segk)
    meet(run, first)
    first.square()
    second = Gather(links, run, second_shard)
    early_shard, late_shard = run(
        pack,
        feed_shards,
        (tuple((n, lo, lo + w) for lo, w in ((0, w1), (w1, w2)) for n in range(3)), triple(w1 + w2, FF)),
    )
    early = lax.all_gather(early_shard, AXES, axis=0, tiled=True)
    strips = run(make_strips, offsets.reshape(HEADS // 2, 2, 2 * SEQ))
    meet(run, second)
    second.square()
    meet(run, first)
    lead_blocks = first.end()
    qkv0, att0, lse0, gains, normed, turned = run(attend, spans, source, segk, segq, strips, layer_input, lead_blocks, True)
    meet(run, second)
    next_blocks = second.end()
    late = lax.all_gather(late_shard, AXES, axis=0, tiled=True)
    qkv1, att1, lse1 = run(attend, spans, source, segk, segq, strips, normed, next_blocks, False)
    hidden, n2, n2t = run(hidden_units, source, att0, att1, layer_input, gains, next_blocks)
    acts = (n2, n2t, cot, cott)
    keep, send, *sums = run(feed, source, acts, early, 0, w1, None)
    s1 = Scatter(links, run, keep, send)
    meet(run, s1)
    s1.square()
    keep, send, *sums = run(feed, source, acts, early, 3 * w1, w2, sums)
    meet(run, s1)
    s2 = Scatter(links, run, keep, send)
    s1.step()
    meet(run, s2)
    s2.square()
    keep, send, block_output, hidden_grad, branch_t, attended_grad = run(
        feed, source, acts, late, 0, w3, sums, (hidden, gains, segk, next_blocks)
    )
    meet(run, s1, s2)
    s3 = Scatter(links, run, keep, send)
    s2.step()
    s1.step()
    meet(run, s3)
    s3.square()
    *g0, keep, send = run(
        attn_bwd, spans, source, segk, segq, strips, qkv0, attended_grad, lse0, turned, (branch_t, att0, att1), 0
    )
    meet(run, s1, s2, s3)
    s4 = Scatter(links, run, keep, send)
    s2.step()
    s3.step()
    meet(run, s4)
    s4.square()
    *g1, keep, send = run(attn_bwd, spans, source, segk, segq, strips, qkv1, attended_grad, lse1, turned, (), 4)
    meet(run, s2, s3, s4)
    s5 = Scatter(links, run, keep, send)
    offset_grads = jnp.concatenate([g0[3], g1[3]], axis=0).reshape(HEADS, 2 * SEQ)
    table_term = lax.dot_general(
        one_hot.astype(F32), offset_grads, (((0,), (1,)), ((), ())), precision=HIGHEST, preferred_element_type=F32
    )
    total = Total(links, run, table_term.reshape(-1, BLK))
    meet(run, s5, total)
    s5.square()
    s4.step()
    s3.step()
    total.step()
    input_gradient = run(
        last, source, layer_input, hidden_grad, gains, [*g0[:3], *g1[:3]], lead_blocks + next_blocks
    )
    meet(run, s3, s4, s5, total)
    s5.line()
    s4.step()
    total.step()
    meet(run, s4, s5)
    *grads, gain_grads = run(
        finish,
        [s.terms + s.got for s in (s4, s5, s1, s2, s3)],
        (query_weight, key_weight, value_weight, gate_weight, up_weight),
        gains_shard,
    )
    meet(run, total)
    table_gradient = total.x.reshape(BUCKETS, HEADS)
    return (block_output, input_gradient, *grads, gain_grads[:, 0], gain_grads[:, 1], table_gradient)


def solution(mesh):
    rows, flat, full = P(AXES, None), P(AXES), P()
    return jax.shard_map(
        functools.partial(on_device, Slice(mesh)),
        mesh=mesh,
        in_specs=(rows, flat, full, flat, rows, rows, rows, rows, full, flat, rows, rows, rows, rows),
        out_specs=(rows,) * 9 + (flat, flat, full),
        check_vma=False,
    )
```

```python
import functools

import jax
import jax.numpy as jnp
import numpy as np
from jax import lax
from jax.experimental import pallas as pl
from jax.experimental.pallas import tpu as pltpu
from jax.sharding import PartitionSpec as P

F32 = jnp.float32
BF = jnp.bfloat16
HEADS = 16
BUCKETS = 32
SEQ = 1024
D = 1024
FF = 2816
BLK = 128
NB = SEQ // BLK
STRIP = (2 * NB - 1) * BLK
EPS = 1e-06
NEG = -1e30
VLIM = 60 * 1024 * 1024
AXES = ("dp", "fsdp")
GROUP = 512
PIECES = (512, 1280, 1024)
TILE = 512
FT = 256
ANY = pl.BlockSpec(memory_space=pl.ANY)
SMEM = pl.BlockSpec(memory_space=pltpu.SMEM)
HIGHEST = lax.Precision.HIGHEST
RATE = 2e7
GELU_A = 0.7978845608028654
GELU_B = 0.044715


def params(grid=1):
    return pltpu.CompilerParams(vmem_limit_bytes=VLIM, dimension_semantics=("arbitrary",) * grid)


def cost(flops, moved, trans=0):
    return pl.CostEstimate(flops=int(flops), bytes_accessed=int(moved / 50), transcendentals=int(trans))


def after(kernel, used, deps):
    if not deps:
        return kernel
    return lambda *refs: kernel(*refs[:used], *refs[used + len(deps) :])


def nt(a,b): return lax.dot_general(a,b,(((1,),(1,)),((),())),preferred_element_type=F32)
def nn(a,b): return lax.dot_general(a,b,(((1,),(0,)),((),())),preferred_element_type=F32)

def build_strip(rev_ref, strip):
    for h in range(2):
        row=jnp.broadcast_to(rev_ref[h:h+1,:],(8,2*SEQ))
        base=pltpu.roll(row,0,1,stride=1,stride_axis=0)
        for m in range(BLK//8):
            turned=pltpu.roll(base,(8*m-(BLK-1))%(2*SEQ),1)
            for d in range(2*NB-1):
                e=2*NB-2-d
                strip[d*BLK+8*m:d*BLK+8*m+8,h*BLK:(h+1)*BLK]=turned[:,e*BLK:(e+1)*BLK]

def fold_strip(strip, out_ref):
    for h in range(2):
        total=jnp.zeros((8,2*SEQ),F32)
        for m in range(BLK//8):
            parts=[strip[(2*NB-2-e)*BLK+8*m:(2*NB-2-e)*BLK+8*m+8,h*BLK:(h+1)*BLK] for e in range(2*NB-1)]
            parts.append(jnp.zeros((8,BLK),F32))
            total=total+pltpu.roll(jnp.concatenate(parts,axis=1),(BLK-1-8*m)%(2*SEQ),1)
        row=total[0:1]
        for s in range(1,8):
            row=row+pltpu.roll(total[s:s+1],2*SEQ-s,1)
        out_ref[h:h+1,:]=row

def lanes_mask():
    lane=lax.broadcasted_iota(jnp.int32,(1,BLK),1)
    return lane<64

def stack_heads(x, first):
    zero=jnp.zeros_like(x)
    return jnp.concatenate([jnp.where(first,x,zero),jnp.where(first,zero,x)],axis=0)


def strip_kernel(rev_ref, strip):
    build_strip(rev_ref, strip)

def make_strips(rev, deps=()):
    return pl.pallas_call(after(strip_kernel, 1, deps),grid=(8,),
        in_specs=[pl.BlockSpec((None,2,2*SEQ),lambda p:(p,0,0))]+[ANY]*len(deps),
        out_specs=pl.BlockSpec((None,STRIP,2*BLK),lambda p:(p,0,0)),
        out_shape=jax.ShapeDtypeStruct((8,STRIP,2*BLK),F32),
        compiler_params=pltpu.CompilerParams(vmem_limit_bytes=VLIM),
        name="bias_strips")(rev, *deps)

def attn_fwd_kernel(UNIT, rng_ref, segk_ref, segq_ref, strip, qkv, o_ref, lse_ref, vt):
    first=lanes_mask()
    for u in range(UNIT):
        vt[u]=qkv[:,2*GROUP+u*BLK:2*GROUP+(u+1)*BLK].T
    mean=jnp.sum(qkv[:,2*GROUP:].astype(F32),axis=0,keepdims=True)*(1.0/SEQ)

    def block(qi, carry):
        q0=pl.multiple_of(qi*BLK,BLK)
        lo=rng_ref[qi]; width=rng_ref[NB+qi]
        k0=pl.multiple_of(lo*BLK,BLK)
        b0=pl.multiple_of((lo-qi+NB-1)*BLK,BLK)
        segq=segq_ref[pl.ds(qi,1),:]
        @pl.when(width==0)
        def _():
            o_ref[pl.ds(q0,BLK),:]=jnp.broadcast_to(mean,(BLK,UNIT*BLK)).astype(BF)
            for u in range(UNIT):
                lse_ref[u,pl.ds(qi,1),:]=jnp.zeros((1,2*BLK),F32)
        for w in range(1,NB+1):
            @pl.when(width==w)
            def _():
                rows=w*BLK
                allowed=segk_ref[pl.ds(k0,rows),:]==segq
                live_row=segq>0
                live_row=jnp.concatenate([live_row,live_row],axis=1)
                live_col=segk_ref[pl.ds(q0,BLK),:]>0
                units=[slice(u*BLK,(u+1)*BLK) for u in range(UNIT)]
                qcats=[stack_heads(qkv[pl.ds(q0,BLK),lanes],first) for lanes in units]
                scores=[nt(qkv[pl.ds(k0,rows),GROUP+lanes.start:GROUP+lanes.stop],qcat) for lanes,qcat in zip(units,qcats)]
                probs=[]; stats=[]; totals=[]
                for u in range(UNIT):
                    both=[]; stat=[]; tot=[]
                    s=scores[u]+strip[u,pl.ds(b0,rows),:]
                    for h in range(2):
                        sh=jnp.where(allowed,s[:,h*BLK:(h+1)*BLK],NEG)
                        peak=jnp.max(sh,axis=0,keepdims=True)
                        e=jnp.exp(sh-peak)
                        t=jnp.sum(e,axis=0,keepdims=True)
                        both.append(e.astype(BF)); stat.append(peak+jnp.log(t)); tot.append(t)
                    probs.append(jnp.concatenate(both,axis=1)); stats.append(jnp.concatenate(stat,axis=1)); totals.append(jnp.concatenate(tot,axis=1))
                ots=[nn(vt[u,:,pl.ds(k0,rows)],probs[u]) for u in range(UNIT)]
                for u,lanes in enumerate(units):
                    ot=ots[u]*(1.0/totals[u])
                    o=jnp.concatenate([ot[:64,:BLK],ot[64:,BLK:]],axis=0).T
                    o_ref[pl.ds(q0,BLK),lanes]=jnp.where(live_col,o,mean[:,lanes]).astype(BF)
                    lse_ref[u,pl.ds(qi,1),:]=jnp.where(live_row,stats[u],0.0)
        return carry
    lax.fori_loop(0,NB,block,0)

def attn_bwd_kernel(UNIT, rng_ref, segk_ref, segq_ref, strip, q_ref, k_ref, v_ref, g_ref, lse_ref,
                    dq_ref, dk_ref, dv_ref, off_ref, dstrip, kt, dk, dv):
    first=lanes_mask()
    dstrip[...]=jnp.zeros_like(dstrip)
    dk[...]=jnp.zeros_like(dk)
    for u in range(UNIT):
        lanes=slice(u*BLK,(u+1)*BLK)
        kt[u]=k_ref[:,lanes].T
        padded=jnp.where(segk_ref[...]>0,0.0,g_ref[:,lanes].astype(F32))
        dv[:,lanes]=jnp.broadcast_to(jnp.sum(padded,axis=0,keepdims=True)*(1.0/SEQ),(SEQ,BLK))

    def block(qi, carry):
        q0=pl.multiple_of(qi*BLK,BLK)
        lo=rng_ref[qi]; width=rng_ref[NB+qi]
        k0=pl.multiple_of(lo*BLK,BLK)
        b0=pl.multiple_of((lo-qi+NB-1)*BLK,BLK)
        segq=segq_ref[pl.ds(qi,1),:]
        @pl.when(width==0)
        def _():
            dq_ref[pl.ds(q0,BLK),:]=jnp.zeros((BLK,UNIT*BLK),BF)
        for w in range(1,NB+1):
            @pl.when(width==w)
            def _():
                rows=w*BLK
                allowed=segk_ref[pl.ds(k0,rows),:]==segq
                units=[slice(u*BLK,(u+1)*BLK) for u in range(UNIT)]
                qcats=[stack_heads(q_ref[pl.ds(q0,BLK),lanes],first) for lanes in units]
                gcats=[stack_heads(g_ref[pl.ds(q0,BLK),lanes],first) for lanes in units]
                scores=[nt(k_ref[pl.ds(k0,rows),lanes],qcat) for lanes,qcat in zip(units,qcats)]
                dps=[nt(v_ref[pl.ds(k0,rows),lanes],gcat) for lanes,gcat in zip(units,gcats)]
                probs=[]; grads=[]
                for u in range(UNIT):
                    lse=lse_ref[u,pl.ds(qi,1),:]
                    s=scores[u]+strip[u,pl.ds(b0,rows),:]
                    ps=[]; ds=[]
                    for h in range(2):
                        cols=slice(h*BLK,(h+1)*BLK)
                        prob=jnp.exp(jnp.where(allowed,s[:,cols],NEG)-lse[:,cols])
                        t=prob*dps[u][:,cols]
                        inner=jnp.sum(t,axis=0,keepdims=True)
                        d=t-prob*inner
                        dstrip[u,pl.ds(b0,rows),cols]+=d
                        ps.append(prob.astype(BF)); ds.append(d.astype(BF))
                    probs.append(jnp.concatenate(ps,axis=1)); grads.append(jnp.concatenate(ds,axis=1))
                for u,lanes in enumerate(units):
                    dv[pl.ds(k0,rows),lanes]+=nn(probs[u],gcats[u])
                dqts=[nn(kt[u,:,pl.ds(k0,rows)],grads[u]) for u in range(UNIT)]
                for u,lanes in enumerate(units):
                    dk[pl.ds(k0,rows),lanes]+=nn(grads[u],qcats[u])
                for u,lanes in enumerate(units):
                    dq_ref[pl.ds(q0,BLK),lanes]=jnp.concatenate([dqts[u][:64,:BLK],dqts[u][64:,BLK:]],axis=0).T.astype(BF)
        return carry
    lax.fori_loop(0,NB,block,0)
    dk_ref[...]=dk[...].astype(BF)
    dv_ref[...]=dv[...].astype(BF)
    for u in range(UNIT):
        fold_strip(dstrip.at[u], off_ref.at[u])

def backward_kernel(unit, lead, rng, source, segk, segq, strip, q, k, v, grad, lse, *refs):
    lefts, rights, refs = refs[: 1 + lead], refs[1 + lead : 1 + 3 * lead], refs[1 + 3 * lead :]
    dq, dk, dv, off, keep, send, dstrip, kt, dk_sum, dv_sum, held, sem = refs
    p = pl.program_id(0)

    @pl.when(p == 0)
    def _():
        for n, left in enumerate(lefts):
            order_rows(source, left, held.at[n], sem.at[n])

    attn_bwd_kernel(
        unit, rng, segk, segq, strip, q, k, v, grad, lse, dq, dk, dv, off, dstrip, kt, dk_sum, dv_sum
    )

    @pl.when(p == 0)
    def _():
        for n in range(1 + lead):
            wait_whole(held.at[n], sem.at[n])

    half, wide = D // 2, unit * BLK
    for j, right in enumerate((dq, dk, dv)):
        part = nn(held[0], right[...]).astype(BF)
        keep[:, j * wide : (j + 1) * wide] = part[:half]
        send[:, j * wide : (j + 1) * wide] = part[half:]
    for n, right in enumerate(rights):

        @pl.when(p == n)
        def _():
            for j in range(GROUP // wide):
                part = nn(held[1], right[:, j * wide : (j + 1) * wide]).astype(BF)
                cols = slice((3 + j) * wide, (4 + j) * wide)
                keep[:, cols] = part[:half]
                send[:, cols] = part[half:]


def attn_bwd(rng, source, segk, segq, strips, qkv, g, lse, turned, more, first_pair):
    unit, steps = 2, 2
    wide = unit * BLK
    lead = int(len(more) > 0)
    f = first_pair // unit
    c = lambda o: pl.BlockSpec((SEQ, wide), lambda p, r, s: (0, o + p))
    whole = lambda *s: pl.BlockSpec(s, lambda p, r, s: (0, 0))
    width = 3 * wide + lead * GROUP
    out = pl.BlockSpec((D // 2, width), lambda p, r, s: (0, p))
    gs = pltpu.PrefetchScalarGridSpec(
        num_scalar_prefetch=2,
        grid=(steps,),
        in_specs=[
            whole(SEQ, BLK), whole(NB, BLK),
            pl.BlockSpec((unit, STRIP, 2 * BLK), lambda p, r, s: (f + p, 0, 0)),
            c(0), c(steps), c(2 * steps), c(f),
            pl.BlockSpec((unit, NB, 2 * BLK), lambda p, r, s: (p, 0, 0)),
        ] + [ANY] * (1 + lead) + [whole(SEQ, GROUP)] * (2 * lead),
        out_specs=[c(0), c(0), c(0), pl.BlockSpec((unit, 2, 2 * SEQ), lambda p, r, s: (p, 0, 0)), out, out],
        scratch_shapes=[
            pltpu.VMEM((unit, STRIP, 2 * BLK), F32), pltpu.VMEM((unit, BLK, SEQ), BF),
            pltpu.VMEM((SEQ, wide), F32), pltpu.VMEM((SEQ, wide), F32),
            pltpu.VMEM((1 + lead, D, SEQ), BF), pltpu.SemaphoreType.DMA((1 + lead,)),
        ],
    )
    sh = jax.ShapeDtypeStruct((SEQ, steps * wide), BF)
    term = jax.ShapeDtypeStruct((D // 2, steps * width), BF)
    return pl.pallas_call(
        functools.partial(backward_kernel, unit, lead),
        grid_spec=gs,
        out_shape=[sh, sh, sh, jax.ShapeDtypeStruct((steps * unit, 2, 2 * SEQ), F32), term, term],
        compiler_params=params(),
        cost_estimate=cost(24 * RATE, 16 * SEQ * wide * 2),
        name="attention_backward",
    )(rng, source, segk, segq, strips, qkv, qkv, qkv, g, lse, turned, *more)


def ranges(seg):
    s=seg.reshape(NB,BLK)
    least=s[:,0]; most=jnp.max(s,axis=1)
    lo=jnp.sum((most[None,:]<least[:,None])&(least[None,:]>0),axis=1)
    hi=jnp.sum((least[None,:]<=most[:,None])&(least[None,:]>0),axis=1)
    w=jnp.where(least>0,hi-lo,0)
    return jnp.concatenate([jnp.where(least>0,lo,0),w]).astype(jnp.int32)


def prep_kernel(c_ref, seg_ref, out_ref, turned_ref):
    low = jnp.where(jnp.concatenate([seg_ref[...] > 0] * (D // BLK), axis=1), c_ref[...].astype(F32), 0.0).astype(BF)
    out_ref[...] = low
    turned_ref[...] = low.T


def prepare(c, segk):
    rows = 256
    blk = pl.BlockSpec((rows, D), lambda i: (i, 0))
    return pl.pallas_call(
        prep_kernel,
        grid=(SEQ // rows,),
        in_specs=[blk, pl.BlockSpec((rows, BLK), lambda i: (i, 0))],
        out_specs=[blk, pl.BlockSpec((D, rows), lambda i: (0, i))],
        out_shape=[jax.ShapeDtypeStruct((SEQ, D), BF), jax.ShapeDtypeStruct((D, SEQ), BF)],
        compiler_params=params(),
        cost_estimate=cost(4 * RATE, 6 * SEQ * D),
        name="prepare",
    )(c, segk)


def pack_kernel(spans, count, *refs):
    ins, outs = refs[:count], refs[count:]
    for out, cols in zip(outs, spans):
        at = 0
        for n, lo, hi in cols:
            out[:, at : at + hi - lo] = ins[n][:, lo:hi]
            at += hi - lo


def pack(shards, spans, deps=()):
    rows = shards[0].shape[0]
    widths = [sum(hi - lo for _, lo, hi in cols) for cols in spans]
    whole = pl.BlockSpec(memory_space=pltpu.VMEM)
    return pl.pallas_call(
        after(functools.partial(pack_kernel, spans, len(shards)), len(shards), deps),
        in_specs=[whole] * len(shards) + [ANY] * len(deps),
        out_specs=[whole] * len(widths),
        out_shape=[jax.ShapeDtypeStruct((rows, w), BF) for w in widths],
        name="pack_shards",
    )(*shards, *deps)


def join(*parts):
    return jnp.concatenate(parts, axis=0)


def add_terms(terms, rows):
    return sum(t[off : off + rows].astype(F32) for t, off in terms).astype(BF)


def finish_kernel(counts, *refs):
    weights, gains, refs = refs[:5], refs[5], refs[6:]
    sums, at = [], 0
    for n in counts:
        total = refs[at][...].astype(F32)
        for ref in refs[at + 1 : at + n]:
            total = total + ref[...].astype(F32)
        sums.append(total)
        at += n
    outs = refs[at:]
    wide = GROUP // 2
    for g, step in ((0, 3 * wide + GROUP), (1, 3 * wide)):
        for p in range(2):
            for j in range(3):
                col = g * GROUP + p * wide
                outs[j][:, col : col + wide] = sums[g][:, p * step + j * wide : p * step + (j + 1) * wide]
    for p in range(2):
        start = (p + 1) * (3 * wide + GROUP) - GROUP
        outs[3][:, p * GROUP : (p + 1) * GROUP] = sums[0][:, start : start + GROUP]
    at = 0
    for s, width in zip(sums[2:], PIECES):
        for j in range(3):
            outs[4 + j][:, at : at + width] = s[:, j * width : (j + 1) * width]
        at += width
    match = lambda w, out: jnp.sum(w[...].astype(F32) * out[...], axis=1, keepdims=True)
    one = match(weights[0], outs[0]) + match(weights[1], outs[1]) + match(weights[2], outs[2])
    two = match(weights[3], outs[4]) + match(weights[4], outs[5])
    lane = lax.broadcasted_iota(jnp.int32, gains.shape, 1)
    outs[7][...] = jnp.where(lane == 0, one, two) / jnp.where(lane < 2, gains[...].astype(F32), 1.0)


def finish(sets, weights, gains):
    rows = gains.shape[0]
    flat = [x for terms in sets for x in terms]
    widths = (D,) * 4 + (FF,) * 3 + (BLK,)
    top = lambda w: pl.BlockSpec((rows, w), lambda i: (0, 0))
    return pl.pallas_call(
        functools.partial(finish_kernel, tuple(len(t) for t in sets)),
        grid=(1,),
        in_specs=[top(x.shape[1]) for x in (*weights, gains, *flat)],
        out_specs=[top(w) for w in widths],
        out_shape=[jax.ShapeDtypeStruct((rows, w), F32) for w in widths],
        compiler_params=params(),
        name="weight_gradients",
    )(*weights, gains, *flat)


def place_blocks(source_ref, blocks, start, cols, dst, at, sem):
    rows = blocks[0].shape[0]
    size = D // source_ref.shape[0]
    per = rows // size
    for n, ref in enumerate(blocks):

        def one(i, carry):
            row = pl.multiple_of(source_ref[n * per + i] * size, size)
            pltpu.make_async_copy(
                ref.at[pl.ds(pl.multiple_of(i * size, size), size), pl.ds(start, cols)],
                dst.at[pl.ds(row, size), pl.ds(at, cols)],
                sem,
            ).start()
            return carry

        lax.fori_loop(0, per, one, 0)


def wait_whole(dst, sem):
    pltpu.make_async_copy(dst, dst, sem).wait()


def order_rows(source_ref, src, dst, sem):
    size = D // source_ref.shape[0]

    def one(p, carry):
        row = pl.multiple_of(source_ref[p] * size, size)
        pltpu.make_async_copy(
            src.at[pl.ds(row, size)], dst.at[pl.ds(pl.multiple_of(p * size, size), size)], sem
        ).start()
        return carry

    lax.fori_loop(0, D // size, one, 0)


def scaled_rows(x):
    return lax.rsqrt(jnp.mean(x * x, axis=-1, keepdims=True) + EPS)


def attend_kernel(lead, first_pair, *refs):
    rng, source, segk, segq, x, strips = refs[:6]
    blocks, refs = refs[6:14], refs[14:]
    if lead:
        qkv_out, o_ref, lse_ref, gains_ref, normed_out, turned_out = refs[:6]
        qkv, w, strip, normed, vt, sem, turned = refs[6:]
    else:
        qkv_out, o_ref, lse_ref = refs[:3]
        qkv, w, strip, normed, vt, sem = refs[3:]
    unit = vt.shape[0]
    bring = pltpu.make_async_copy(x, normed, sem.at[0])
    bring.start()
    place_blocks(source, blocks, 0, w.shape[1], w, 0, sem.at[1])
    pads = pltpu.make_async_copy(strips.at[pl.ds(first_pair, unit)], strip, sem.at[2])
    pads.start()
    outs = [pltpu.make_async_copy(qkv, qkv_out, sem.at[3])]
    bring.wait()
    wait_whole(w, sem.at[1])
    if lead:
        gains_ref[...] = w[:, 3 * GROUP :].astype(F32).T[:8]

        def rows_of(i, carry):
            at = pl.multiple_of(i * 256, 256)
            rows = normed[pl.ds(at, 256), :].astype(F32)
            low = (rows * scaled_rows(rows) * gains_ref[0:1, :]).astype(BF)
            normed[pl.ds(at, 256), :] = low
            turned[:, pl.ds(at, 256)] = low.T
            return carry

        lax.fori_loop(0, SEQ // 256, rows_of, 0)
        outs += [pltpu.make_async_copy(normed, normed_out, sem.at[4]), pltpu.make_async_copy(turned, turned_out, sem.at[5])]
        for c in outs[1:]:
            c.start()

    def columns(j, carry):
        cols = pl.ds(pl.multiple_of(j * FT, FT), FT)
        qkv[:, cols] = nn(normed[...], w[:, cols]).astype(BF)
        return carry

    lax.fori_loop(0, 3 * GROUP // FT, columns, 0)
    outs[0].start()
    pads.wait()
    attn_fwd_kernel(unit, rng, segk, segq, strip, qkv, o_ref, lse_ref, vt)
    for c in outs:
        c.wait()


def attend(rng, source, segk, segq, strips, x, blocks, lead):
    unit = 4
    width = 3 * GROUP + (BLK if lead else 0)
    vmem = pl.BlockSpec(memory_space=pltpu.VMEM)
    shape = lambda t, *s: jax.ShapeDtypeStruct(s, t)
    out_specs = [ANY, vmem, vmem] + ([vmem, ANY, ANY] if lead else [])
    out_shape = [shape(BF, SEQ, 3 * GROUP), shape(BF, SEQ, GROUP), shape(F32, unit, NB, 2 * BLK)]
    out_shape += [shape(F32, 8, D), shape(BF, SEQ, D), shape(BF, D, SEQ)] if lead else []
    return pl.pallas_call(
        functools.partial(attend_kernel, lead, 0 if lead else unit),
        in_specs=[SMEM, SMEM, vmem, vmem, ANY, ANY] + [ANY] * len(blocks),
        out_specs=out_specs,
        out_shape=out_shape,
        scratch_shapes=[
            pltpu.VMEM((SEQ, 3 * GROUP), BF), pltpu.VMEM((D, width), BF), pltpu.VMEM((unit, STRIP, 2 * BLK), F32),
            pltpu.VMEM((SEQ, D), BF), pltpu.VMEM((unit, BLK, SEQ), BF), pltpu.SemaphoreType.DMA((6,)),
        ] + ([pltpu.VMEM((D, SEQ), BF)] if lead else []),
        compiler_params=pltpu.CompilerParams(vmem_limit_bytes=VLIM),
        cost_estimate=cost(20 * RATE, 2 * D * width + 4 * SEQ * D),
        name="attention_forward",
    )(rng, source, segk, segq, x, strips, *blocks)


def hidden_kernel(*refs):
    source, a0, a1, x_ref, gains_ref = refs[:5]
    h_ref, n2_ref, n2t_ref, w, sem = refs[13:]

    @pl.when(pl.program_id(0) == 0)
    def _():
        place_blocks(source, refs[5:13], 3 * GROUP, D, w, 0, sem.at[0])
        wait_whole(w, sem.at[0])

    hidden = x_ref[...].astype(F32) + nt(jnp.concatenate([a0[...], a1[...]], axis=1), w[...])
    h_ref[...] = hidden
    normed = (hidden * scaled_rows(hidden) * gains_ref[1:2, :]).astype(BF)
    n2_ref[...] = normed
    n2t_ref[...] = normed.T


def hidden_units(source, a0, a1, x, gains, blocks):
    rows = TILE
    tok = lambda c: pl.BlockSpec((rows, c), lambda i: (i, 0))
    return pl.pallas_call(
        hidden_kernel,
        grid=(SEQ // rows,),
        in_specs=[SMEM, tok(GROUP), tok(GROUP), tok(D), pl.BlockSpec((8, D), lambda i: (0, 0))] + [ANY] * len(blocks),
        out_specs=[tok(D), tok(D), pl.BlockSpec((D, rows), lambda i: (0, i))],
        out_shape=[
            jax.ShapeDtypeStruct((SEQ, D), F32),
            jax.ShapeDtypeStruct((SEQ, D), BF),
            jax.ShapeDtypeStruct((D, SEQ), BF),
        ],
        scratch_shapes=[pltpu.VMEM((D, D), BF), pltpu.SemaphoreType.DMA((1,))],
        compiler_params=params(),
        cost_estimate=cost(6 * RATE, 16 * SEQ * D),
        name="hidden_units",
    )(source, a0, a1, x, gains, *blocks)


def feed_kernel(lead, final, width, base, *refs):
    source, n2, n2t, cot, cott, whole = refs[:6]
    refs = refs[6:]
    sums_from = () if lead else refs[:2]
    refs = refs[len(sums_from) :]
    if final:
        h_in, gains_ref, seg_in, blocks, refs = refs[0], refs[1], refs[2], refs[3:11], refs[11:]
    keep, send = refs[:2]
    outs, refs = (refs[2:6], refs[6:]) if final else (refs[2:4], refs[4:])
    n2_v, n2t_v, cot_v, cott_v, w, stage, bo, ng, mix_v, gu_v, sem_w, sem_o, sem_i = refs[:13]
    half = D // 2
    tiles = width // FT

    def weight_copies(f):
        out = []
        for j in range(3):
            col = pl.multiple_of(j * width + f * FT, FT)
            out.append(
                pltpu.make_async_copy(
                    whole.at[:, pl.ds(pl.multiple_of(base + col, BLK), FT)], w.at[:, pl.ds(col, FT)], sem_w.at[f, j]
                )
            )
        return out

    def term_copies(g):
        col = pl.multiple_of(g * FT, FT)
        return [
            pltpu.make_async_copy(
                stage.at[pl.ds(s * half, half), pl.ds(col, FT)], dst.at[:, pl.ds(col, FT)], sem_o.at[g, s]
            )
            for s, dst in enumerate((keep, send))
        ]

    first = [pltpu.make_async_copy(n2, n2_v, sem_i.at[0]), pltpu.make_async_copy(cot, cot_v, sem_i.at[1])]
    sums_in = [pltpu.make_async_copy(a, b, sem_i.at[4 + n]) for n, (a, b) in enumerate(zip(sums_from, (bo, ng)))]
    if final:
        h_v, wo, ag_v, bt_v, out_v, seg_v = refs[13:]
        sums_in += [pltpu.make_async_copy(h_in, h_v, sem_i.at[6]), pltpu.make_async_copy(seg_in, seg_v, sem_i.at[7])]
        sources = (out_v, ng, bt_v, ag_v)
    else:
        sources = (bo, ng)
    results = [pltpu.make_async_copy(a, b, sem_i.at[8 + n]) for n, (a, b) in enumerate(zip(sources, outs))]
    for c in weight_copies(0) + first:
        c.start()
    for c in first:
        c.wait()
    for f in range(1, tiles):
        for c in weight_copies(f):
            c.start()
    for c in sums_in:
        c.start()

    def units(f, carry):
        for c in weight_copies(f):
            c.wait()
        at = [pl.ds(pl.multiple_of(j * width + f * FT, FT), FT) for j in range(3)]

        gate = nn(n2_v[...], w[:, at[0]])
        upward = nn(n2_v[...], w[:, at[1]])
        mixed_grad = nn(cot_v[...], w[:, at[2]])
        square = gate * gate
        bend = jnp.tanh(gate * (GELU_A + (GELU_A * GELU_B) * square))
        curve = 0.5 * (1.0 + bend)
        active = gate * curve
        slope = curve + (0.5 * gate) * (1.0 - bend * bend) * (GELU_A + (3.0 * GELU_A * GELU_B) * square)
        mix_v[:, at[0]] = (active * upward).astype(BF)
        gu_v[:, at[0]] = (mixed_grad * upward * slope).astype(BF)
        gu_v[:, at[1]] = (mixed_grad * active).astype(BF)
        return carry

    lax.fori_loop(0, tiles, units, 0)
    order_rows(source, n2t, n2t_v, sem_i.at[2])
    order_rows(source, cott, cott_v, sem_i.at[3])
    if final:
        place_blocks(source, blocks, 3 * GROUP, D, wo, 0, sem_i.at[13])
    for c in sums_in:
        c.wait()

    for j in range(D // FT):
        cols = slice(j * FT, (j + 1) * FT)
        one = nt(mix_v[...], w[cols, 2 * width :])
        two = nt(gu_v[...], w[cols, : 2 * width])
        bo[:, cols] = one if lead else bo[:, cols] + one
        ng[:, cols] = two if lead else ng[:, cols] + two
    if final:
        wait_whole(wo, sem_i.at[13])

        def close(i, carry):
            rows = pl.ds(pl.multiple_of(i * 256, 256), 256)
            hidden = h_v[rows, :]
            live = jnp.concatenate([seg_v[rows, :] > 0] * (D // BLK), axis=1)
            out_v[rows, :] = jnp.where(live, hidden + bo[rows, :], 0.0).astype(BF)
            grad = ng[rows, :]
            scale = scaled_rows(hidden)
            grad = grad * gains_ref[1:2, :]
            mean = jnp.mean(grad * hidden, axis=-1, keepdims=True)
            out = cot_v[rows, :].astype(F32) + (scale * grad - hidden * (scale * scale * scale * mean))
            ng[rows, :] = out
            low = out.astype(BF)
            mix_low[rows, :] = low
            bt_v[:, rows] = low.T
            return carry

        mix_low = n2_v
        lax.fori_loop(0, SEQ // 256, close, 0)

        def attended(i, carry):
            cols = pl.ds(pl.multiple_of(i * FT, FT), FT)
            ag_v[:, cols] = nn(mix_low[...], wo[:, cols]).astype(BF)
            return carry

        lax.fori_loop(0, D // FT, attended, 0)
    for c in results:
        c.start()
    wait_whole(n2t_v, sem_i.at[2])
    wait_whole(cott_v, sem_i.at[3])

    def term(left, right, f, start):
        cols = pl.ds(pl.multiple_of(f * FT, FT), FT)
        out = pl.ds(pl.multiple_of((start + f) * FT, FT), FT)
        stage[:, out] = nn(left[...], right[:, cols]).astype(BF)
        for c in term_copies(start + f):
            c.start()

    def pair(f, carry):
        term(n2t_v, gu_v, 2 * f, 0)
        term(n2t_v, gu_v, 2 * f + 1, 0)
        return carry

    lax.fori_loop(0, tiles, pair, 0)
    for f in range(tiles):
        term(cott_v, mix_v, f, 2 * tiles)
    for c in results:
        c.wait()

    def drain(g, carry):
        for c in term_copies(g):
            c.wait()
        return carry

    lax.fori_loop(0, 3 * tiles, drain, 0)


def feed(source, acts, whole, base, width, sums, closing=None):
    lead, final = sums is None, closing is not None
    tiles = width // FT
    args = [source, *acts, whole] + ([] if lead else list(sums))
    specs = [SMEM] + [ANY] * (len(args) - 1)
    if final:
        hidden, gains, segk, blocks = closing
        args += [hidden, gains, segk, *blocks]
        specs += [ANY, pl.BlockSpec(memory_space=pltpu.VMEM), ANY] + [ANY] * len(blocks)
    half = jax.ShapeDtypeStruct((D // 2, 3 * width), BF)
    shape = lambda t, *s: jax.ShapeDtypeStruct(s, t)
    total = shape(F32, SEQ, D)
    outs = [shape(BF, SEQ, D), total, shape(BF, D, SEQ), shape(BF, SEQ, D)] if final else [total, total]
    bf = lambda *s: pltpu.VMEM(s, BF)
    scratch = [
        bf(SEQ, D), bf(D, SEQ), bf(SEQ, D), bf(D, SEQ), bf(D, 3 * width), bf(D, 3 * width),
        pltpu.VMEM((SEQ, D), F32), pltpu.VMEM((SEQ, D), F32),
        bf(SEQ, width), bf(SEQ, 2 * width),
        pltpu.SemaphoreType.DMA((tiles, 3)), pltpu.SemaphoreType.DMA((3 * tiles, 2)), pltpu.SemaphoreType.DMA((14,)),
    ]
    if final:
        scratch += [
            pltpu.VMEM((SEQ, D), F32), bf(D, D), bf(SEQ, D), bf(D, SEQ), bf(SEQ, D),
            pltpu.VMEM((SEQ, BLK), jnp.int32),
        ]
    return pl.pallas_call(
        functools.partial(feed_kernel, lead, final, width, base),
        in_specs=specs,
        out_specs=[ANY] * (2 + len(outs)),
        out_shape=[half, half] + outs,
        scratch_shapes=scratch,
        compiler_params=pltpu.CompilerParams(vmem_limit_bytes=VLIM),
        cost_estimate=cost((30 * width / 1024 + (6 if final else 0)) * RATE, 12 * D * width + 24 * SEQ * D, SEQ * width),
        name="feed_forward",
    )(*args)


def last_kernel(count, *refs):
    source, x_ref, hg_ref, gains_ref = refs[:4]
    grads = refs[4 : 4 + count]
    blocks = refs[4 + count : 20 + count]
    out_ref, w, sem = refs[-3:]
    half = 3 * GROUP

    @pl.when(pl.program_id(0) == 0)
    def _():
        for n in range(2):
            place_blocks(source, blocks[8 * n : 8 * n + 8], 0, half, w, n * half, sem.at[n])
        for n in range(2):
            wait_whole(w.at[:, pl.ds(n * half, half)], sem.at[n])

    grad = nt(jnp.concatenate([g[...] for g in grads], axis=1), w[...])
    x = x_ref[...].astype(F32)
    scale = scaled_rows(x)
    grad = grad * gains_ref[0:1, :]
    mean = jnp.mean(grad * x, axis=-1, keepdims=True)
    out_ref[...] = hg_ref[...] + (scale * grad - x * (scale * scale * scale * mean))


def last(source, x, hg, gains, grads, blocks):
    rows = 256
    tok = lambda c: pl.BlockSpec((rows, c), lambda i: (i, 0))
    whole = pl.BlockSpec((8, D), lambda i: (0, 0))
    return pl.pallas_call(
        functools.partial(last_kernel, len(grads)),
        grid=(SEQ // rows,),
        in_specs=[SMEM, tok(D), tok(D), whole] + [tok(g.shape[1]) for g in grads] + [ANY] * len(blocks),
        out_specs=tok(D),
        out_shape=jax.ShapeDtypeStruct((SEQ, D), F32),
        scratch_shapes=[pltpu.VMEM((D, 6 * GROUP), BF), pltpu.SemaphoreType.DMA((2,))],
        compiler_params=params(),
        cost_estimate=cost(14 * RATE, 14 * SEQ * D),
        name="input_gradient",
    )(source, x, hg, gains, *grads, *blocks)


class Slice:
    def __init__(self, mesh):
        self.count = mesh.shape["dp"] * mesh.shape["fsdp"]
        self.inner = mesh.shape["fsdp"]
        self.core = self.inner
        bits = [1 << b for b in range(self.count.bit_length() - 1)]
        self.rest = [b for b in reversed(bits) if b not in (1, 2, self.core)]
        self.order = [self.core, 2, 1] + self.rest[::-1]
        self.size = D // self.count

    def place(self, index):
        p = index * 0
        for b in self.order:
            p = 2 * p + (index // b) % 2
        return p

    def swap(self, x, bit):
        return lax.ppermute(x, AXES, [(i, i ^ bit) for i in range(self.count)])

    @staticmethod
    def masks(bits):
        return [sum(b for j, b in enumerate(bits) if n >> j & 1) for n in range(1, 1 << len(bits))]


class Order:
    def __init__(self):
        self.token = None

    def hold(self, args):
        leaves, tree = jax.tree.flatten(args)
        at = [i for i, x in enumerate(leaves) if hasattr(x, "aval")]
        if self.token is not None:
            held = lax.optimization_barrier([leaves[i] for i in at] + [self.token])
            for i, x in zip(at, held):
                leaves[i] = x
        return jax.tree.unflatten(tree, leaves)

    def __call__(self, f, *args):
        out = f(*self.hold(args))
        self.token = jax.tree.leaves(out)[0]
        return out


class Chain:
    def __init__(self, links, run):
        self.links, self.run, self.pending = links, run, []


def meet(run, *chains):
    arrays = run.hold([c.pending for c in chains] + [run.token])
    run.token = arrays.pop()
    for c, got in zip(chains, arrays):
        c.met(got)
        c.pending = []


class Gather(Chain):
    def __init__(self, links, run, shard):
        super().__init__(links, run)
        self.line = run.hold(shard)
        self.pending = [links.swap(self.line, m) for m in links.masks(links.rest)]

    def met(self, got):
        self.got = got

    def square(self):
        self.line = self.run(join, self.line, *self.got)
        self.others = [self.links.swap(self.line, self.links.core)]
        self.pending = [self.links.swap(self.line, m) for m in (1, 2, 3)]

    def end(self):
        self.others += [self.links.swap(b, self.links.core) for b in self.got]
        return (self.line, *self.got, *self.others)


class Total(Chain):
    def __init__(self, links, run, x):
        super().__init__(links, run)
        self.x = run.hold(x)
        self.groups = [links.masks(b) for b in (links.rest, [1, 2], [links.core])]
        self.step()

    def met(self, got):
        self.x = self.x + sum(got)

    def step(self):
        self.pending = [self.links.swap(self.x, m) for m in self.groups.pop(0)]


class Scatter(Chain):
    def __init__(self, links, run, keep, send):
        super().__init__(links, run)
        self.terms, self.rows, self.bits = [keep], D // 2, links.rest[::-1]
        self.pending = [links.swap(run.hold(send), links.core)]

    def met(self, got):
        self.got = got

    def spread(self, masks):
        self.terms += self.got
        rows = self.rows // (len(masks) + 1)
        self.pending = []
        for n in list(range(len(masks)))[::-1]:
            send = self.run(add_terms, [(t, (n + 1) * rows) for t in self.terms], rows)
            self.pending.insert(0, self.links.swap(send, masks[n]))
        self.rows = rows

    def square(self):
        self.spread((1, 2, 3))

    def line(self):
        self.spread(self.links.masks(self.links.rest))
        self.bits = []

    def step(self):
        self.spread((self.bits.pop(0),))


def on_device(
    links,
    layer_input,
    segment_ids,
    relative_buckets,
    first_gain,
    query_weight,
    key_weight,
    value_weight,
    output_projection,
    relative_table,
    second_gain,
    gate_weight,
    up_weight,
    down_projection,
    output_cotangent,
):
    size = links.size
    me = lax.axis_index("dp") * links.inner + lax.axis_index("fsdp")
    place = np.array([links.place(i) for i in range(links.count)], np.int32)
    source = jnp.asarray(np.argsort(place).astype(np.int32)) ^ me

    gains_shard = jnp.pad(jnp.stack([first_gain, second_gain], axis=1), ((0, 0), (0, BLK - 2)))
    w1, w2, w3 = PIECES
    feed_shards = (gate_weight, up_weight, down_projection)
    qkv_shards = (query_weight, key_weight, value_weight)
    triple = lambda lo, hi: tuple((n, lo, hi) for n in range(3))
    run = Order()
    segk = jnp.broadcast_to(segment_ids[:, None], (SEQ, BLK))
    segq = jnp.where(segment_ids > 0, segment_ids, -1).reshape(NB, BLK)
    spans = ranges(segment_ids)
    one_hot = (relative_buckets[::-1][:, None] == jnp.arange(BUCKETS)[None, :]).astype(BF)
    one_hot = jnp.pad(one_hot, ((0, 1), (0, 0)))
    offsets = lax.dot_general(relative_table, one_hot, (((0,), (1,)), ((), ())), preferred_element_type=F32)

    (first_shard,) = run(pack, qkv_shards + (gains_shard,), (triple(0, GROUP) + ((3, 0, BLK),),))
    first = Gather(links, run, first_shard)
    (second_shard,) = run(pack, qkv_shards + (output_projection,), (triple(GROUP, 2 * GROUP) + ((3, 0, D),),))
    cot, cott = run(prepare, output_cotangent, segk)
    meet(run, first)
    first.square()
    second = Gather(links, run, second_shard)
    early_shard, late_shard = run(
        pack,
        feed_shards,
        (tuple((n, lo, lo + w) for lo, w in ((0, w1), (w1, w2)) for n in range(3)), triple(w1 + w2, FF)),
    )
    early = lax.all_gather(early_shard, AXES, axis=0, tiled=True)
    strips = run(make_strips, offsets.reshape(HEADS // 2, 2, 2 * SEQ))
    meet(run, second)
    second.square()
    meet(run, first)
    lead_blocks = first.end()
    qkv0, att0, lse0, gains, normed, turned = run(attend, spans, source, segk, segq, strips, layer_input, lead_blocks, True)
    second.got = [run.hold(b) for b in second.pending]
    next_blocks = second.end()
    late = lax.all_gather(late_shard, AXES, axis=0, tiled=True)
    qkv1, att1, lse1 = run(attend, spans, source, segk, segq, strips, normed, next_blocks, False)
    hidden, n2, n2t = run(hidden_units, source, att0, att1, layer_input, gains, next_blocks)
    acts = (n2, n2t, cot, cott)
    keep, send, *sums = run(feed, source, acts, early, 0, w1, None)
    s1 = Scatter(links, run, keep, send)
    meet(run, s1)
    s1.square()
    keep, send, *sums = run(feed, source, acts, early, 3 * w1, w2, sums)
    meet(run, s1)
    s2 = Scatter(links, run, keep, send)
    s1.step()
    meet(run, s2)
    s2.square()
    keep, send, block_output, hidden_grad, branch_t, attended_grad = run(
        feed, source, acts, late, 0, w3, sums, (hidden, gains, segk, next_blocks)
    )
    meet(run, s1, s2)
    s3 = Scatter(links, run, keep, send)
    s2.step()
    s1.step()
    meet(run, s3)
    s3.square()
    *g0, keep, send = run(
        attn_bwd, spans, source, segk, segq, strips, qkv0, attended_grad, lse0, turned, (branch_t, att0, att1), 0
    )
    meet(run, s1, s2, s3)
    s4 = Scatter(links, run, keep, send)
    s2.step()
    s3.step()
    meet(run, s4)
    s4.square()
    *g1, keep, send = run(attn_bwd, spans, source, segk, segq, strips, qkv1, attended_grad, lse1, turned, (), 4)
    meet(run, s2, s3, s4)
    s5 = Scatter(links, run, keep, send)
    offset_grads = jnp.concatenate([g0[3], g1[3]], axis=0).reshape(HEADS, 2 * SEQ)
    table_term = lax.dot_general(
        one_hot.astype(F32), offset_grads, (((0,), (1,)), ((), ())), precision=HIGHEST, preferred_element_type=F32
    )
    total = Total(links, run, table_term.reshape(-1, BLK))
    meet(run, s5, total)
    s5.square()
    s4.step()
    s3.step()
    total.step()
    input_gradient = run(
        last, source, layer_input, hidden_grad, gains, [*g0[:3], *g1[:3]], lead_blocks + next_blocks
    )
    meet(run, s3, s4, s5, total)
    s5.line()
    s4.step()
    total.step()
    meet(run, s4, s5)
    *grads, gain_grads = run(
        finish,
        [s.terms + s.got for s in (s4, s5, s1, s2, s3)],
        (query_weight, key_weight, value_weight, gate_weight, up_weight),
        gains_shard,
    )
    meet(run, total)
    table_gradient = total.x.reshape(BUCKETS, HEADS)
    return (block_output, input_gradient, *grads, gain_grads[:, 0], gain_grads[:, 1], table_gradient)


def solution(mesh):
    rows, flat, full = P(AXES, None), P(AXES), P()
    return jax.shard_map(
        functools.partial(on_device, Slice(mesh)),
        mesh=mesh,
        in_specs=(rows, flat, full, flat, rows, rows, rows, rows, full, flat, rows, rows, rows, rows),
        out_specs=(rows,) * 9 + (flat, flat, full),
        check_vma=False,
    )
```
